256 devices in a mesh: member: 16 (over z, x_hi), band: 16 (over x_lo, y, core).
Axes of the slice: x: 4 (x_hi: 2, x_lo: 2; x = x_hi * 2 + x_lo), y: 4, z: 8, core: 2. Of those that a mesh axis runs over, the one named last changes fastest.
Arguments:
- copy_fields: bfloat16 [16, 240, 384, 480], P('member', 'band'), may hold values from -6 to 6
- norm_gain: float32 [384], replicated, may hold values from 0.25 to 1.75
- mix_real: bfloat16 [384, 384], replicated, may hold values from -0.21875 to 0.21875
- mix_imag: bfloat16 [384, 384], replicated, may hold values from -0.21875 to 0.21875
- filter_bank: float32 [32, 240], replicated, may hold values from 0.5 to 1.5
- perturbation_draw_numbers: int32 [16], P('member'), may hold values from 0 to 31
- amplitudes: float32 [8], replicated, may hold values from 0.2 to 1
- desired_magnitude_slot: int32 [16], P('member'), may hold values from 0 to 7
Outputs:
- bred: bfloat16 [16, 240, 384, 480], P('member', 'band')
The draws below stay inside these ranges and needn't reach their ends.
All inputs are finite; a program needn't handle non-finite values.
Results may differ from the reference program's by a relative error of at most 0.007.
Values may be sent and summed in bfloat16 or wider, within the bound.
No kernel may reach another device: no remote copies, remote signals or barrier semaphores. Data moves between devices by JAX's collectives and lax.ppermute only.
A program may use at most 128 MiB of HBM per device.

```python
import math
import jax
import jax.numpy as jnp
import numpy as np
from jax import lax

E = 384
H = 240
W = 480
M = 240
L = 240
BANK = 32
LEVELS = 8
MEMBERS = 16


def draw_copy_fields(key, part):
    key = jax.random.fold_in(key, 11)
    position = jnp.arange(H, dtype=jnp.float32) / (H - 1)
    noise = jax.random.truncated_normal(key, -3.0, 3.0, (MEMBERS, H, E, W), jnp.float32)
    profile = 0.5 * jnp.exp(math.log(4.0) * position)
    return (noise * profile[None, :, None, None]).astype(jnp.bfloat16)


def set_ends(values, rng, smallest, high):
    shape = values.shape
    index_at = [jax.random.randint(jax.random.fold_in(rng, axis), (), 0, shape[axis]) for axis in range(len(shape))]
    values = values.at[tuple(index_at)].set(smallest)
    longest = shape.index(max(shape))
    index_at[longest] = (index_at[longest] + 1) % shape[longest]
    return values.at[tuple(index_at)].set(high)


def normal_values(stream_key, shape, scale, reach, held_as=jnp.bfloat16):
    entries = jax.random.normal(stream_key, shape, jnp.float32) * scale
    return jnp.minimum(jnp.maximum(entries, -reach), reach).astype(held_as)


def setup_inputs(seed: int = 0) -> dict:
    streams_of = jax.random.split(jax.random.key(seed), 9)
    return {
        "copy_fields": draw_copy_fields(jax.random.fold_in(streams_of[8], 71), 0),
        "norm_gain": jnp.clip(1.0 + 0.15 * jax.random.normal(streams_of[1], (E,), jnp.float32), 0.25, 1.75),
        "mix_real": normal_values(streams_of[2], (E, E), (2 * E) ** -0.5, 0.21875),
        "mix_imag": normal_values(streams_of[3], (E, E), (2 * E) ** -0.5, 0.21875),
        "filter_bank": jnp.clip(jax.random.uniform(streams_of[4], (BANK, L), jnp.float32, 0.5, 1.5), 0.5, 1.5),
        "perturbation_draw_numbers": set_ends(jax.random.randint(streams_of[5], (MEMBERS,), 0, BANK), jax.random.fold_in(streams_of[5], 1), 0, BANK - 1).astype(jnp.int32),
        "amplitudes": jnp.clip(jnp.exp(jax.random.uniform(streams_of[6], (LEVELS,), jnp.float32, math.log(0.2), math.log(1.0))), 0.2, 1.0),
        "desired_magnitude_slot": set_ends(jax.random.randint(streams_of[7], (MEMBERS,), 0, LEVELS), jax.random.fold_in(streams_of[7], 1), 0, LEVELS - 1).astype(jnp.int32),
    }


def legendre_table(degree_count, order_count, lat_count):
    colatitude = (np.arange(lat_count) + 0.5) * np.pi / lat_count
    cosines = np.cos(colatitude)
    sines = np.sin(colatitude)
    orders = np.arange(order_count)[:, None] * 1.0
    steps_up = np.arange(1, order_count) * 1.0
    log_factor = np.concatenate([[0.0], np.cumsum(np.log((2.0 * steps_up - 1.0) / (2.0 * steps_up)))])
    diagonal_start = np.exp(0.5 * np.log((2.0 * orders + 1.0) / 2.0) + 0.5 * log_factor[:, None] + orders * np.log(sines)[None, :])
    result = np.zeros((order_count, degree_count, lat_count))
    previous = np.zeros(diagonal_start.shape)
    before_previous = np.zeros(diagonal_start.shape)
    for degree in range(degree_count):
        lower = degree - 1.0
        rising = np.sqrt(np.maximum(4.0 * degree * degree - 1.0, 1.0) / np.maximum(degree * degree - orders * orders, 1.0))
        falling = np.sqrt(np.maximum(lower * lower - orders * orders, 0.0) / max(4.0 * lower * lower - 1.0, 1.0))
        current = np.where(orders == degree, diagonal_start, np.where(degree > orders, rising * (cosines[None, :] * previous - falling * before_previous), 0.0))
        result[:, degree] = current
        before_previous = previous
        previous = current
    return result

def fourier_tables(lon_count, mode_order):
    longitude = 2.0 * np.pi * np.arange(lon_count)[:, None] / lon_count
    angles = longitude * (mode_order[None, :] * 1.0)
    forward_factor = math.sqrt(2.0 * math.pi) / lon_count
    forward_table = np.stack([forward_factor * np.cos(angles), -forward_factor * np.sin(angles)], axis=1)
    inverse_factor = np.where(mode_order == 0, 1.0, 2.0) / math.sqrt(2.0 * math.pi)
    inverse_table = np.stack([(inverse_factor[None, :] * np.cos(angles)).T, (-inverse_factor[None, :] * np.sin(angles)).T], axis=0)
    return (forward_table, inverse_table)

def latitude_weights(lat_count):
    colatitude = (jnp.arange(lat_count, dtype=jnp.float32) + 0.5) * (math.pi / lat_count)
    return jnp.sin(colatitude) * (math.pi / lat_count)

def rounded(values):
    return lax.optimization_barrier(values.astype(jnp.bfloat16)).astype(jnp.float32)

def reference(copy_fields, norm_gain, mix_real, mix_imag, filter_bank, perturbation_draw_numbers, amplitudes, desired_magnitude_slot):
    legendre = rounded(jnp.asarray(legendre_table(L, M, H), jnp.float32))
    forward_np, inverse_np = fourier_tables(W, np.arange(M))
    forward_table = rounded(jnp.asarray(forward_np, jnp.float32))
    inverse_table = rounded(jnp.asarray(inverse_np, jnp.float32))
    weights = latitude_weights(H)
    mixing_matrix = jnp.concatenate([jnp.concatenate([mix_real, mix_imag], 1), jnp.concatenate([-mix_imag, mix_real], 1)], 0)

    def propagate_network(element):
        member_field, member_seed = element
        broadened_fields = member_field.astype(jnp.float32)
        average = lax.optimization_barrier(jnp.mean(broadened_fields, axis=1, keepdims=True))
        variance = lax.optimization_barrier(jnp.mean(jnp.square(broadened_fields - average), axis=1, keepdims=True))
        normed = rounded((broadened_fields - average) * lax.rsqrt(variance + 1e-05) * norm_gain[None, :, None])
        fourier = jnp.einsum('jew,wrm->mjre', normed, forward_table)
        fourier = rounded(fourier * weights[None, :, None, None]).reshape(M, H, 2 * E)
        coeffs = jnp.einsum('mlj,mjc->mlc', legendre, fourier).astype(jnp.bfloat16)
        degree_gain = filter_bank[member_seed]
        mixed_values = jnp.dot(coeffs.reshape(M * L, 2 * E), mixing_matrix, preferred_element_type=jnp.float32).reshape(M, L, 2 * E)
        mixed_values = rounded(mixed_values * degree_gain[None, :, None])
        spatial = rounded(jnp.einsum('mlj,mlc->mjc', legendre, mixed_values)).reshape(M, H, 2, E)
        split_ensemble_copy = jax.nn.gelu(jnp.einsum('mjre,rmw->jew', spatial, inverse_table))
        return (broadened_fields + split_ensemble_copy).astype(jnp.bfloat16)
    ensemble_predictions = lax.map(propagate_network, (copy_fields, perturbation_draw_numbers))
    unperturbed_field = lax.optimization_barrier(ensemble_predictions[0]).astype(jnp.float32)
    total_weight = jnp.sum(weights) * (E * W)

    def grow_perturbation_fields(element):
        member_field, level_index = element
        copy_minus_unperturbed = lax.optimization_barrier(member_field).astype(jnp.float32) - unperturbed_field
        spread = jnp.sum(weights[:, None, None] * copy_minus_unperturbed * copy_minus_unperturbed) / total_weight
        rescale = amplitudes[level_index] / jnp.sqrt(spread + 1e-06)
        return (unperturbed_field + rescale * copy_minus_unperturbed).astype(jnp.bfloat16)
    return lax.map(grow_perturbation_fields, (ensemble_predictions, desired_magnitude_slot))
```

```python
import functools
import math

import jax
import jax.numpy as jnp
import numpy as np
from jax import lax
from jax.experimental import pallas as pl
from jax.experimental.pallas import tpu as pltpu
from jax.sharding import PartitionSpec as P

H = 240
W = 480
M = 240
L = 240
E = 384
BANDS = 16
ROWS = H // BANDS
OWN = M // BANDS
SLOTS = 32
DEPTH = 8
VMEM_LIMIT = 58 * 1024 * 1024


def legendre_table(degree_count, order_count, lat_count):
    colatitude = (np.arange(lat_count) + 0.5) * np.pi / lat_count
    cosines = np.cos(colatitude)
    sines = np.sin(colatitude)
    orders = np.arange(order_count)[:, None] * 1.0
    steps_up = np.arange(1, order_count) * 1.0
    log_factor = np.concatenate(
        [[0.0], np.cumsum(np.log((2.0 * steps_up - 1.0) / (2.0 * steps_up)))]
    )
    diagonal_start = np.exp(
        0.5 * np.log((2.0 * orders + 1.0) / 2.0)
        + 0.5 * log_factor[:, None]
        + orders * np.log(sines)[None, :]
    )
    result = np.zeros((order_count, degree_count, lat_count))
    previous = np.zeros(diagonal_start.shape)
    before_previous = np.zeros(diagonal_start.shape)
    for degree in range(degree_count):
        lower = degree - 1.0
        rising = np.sqrt(
            np.maximum(4.0 * degree * degree - 1.0, 1.0)
            / np.maximum(degree * degree - orders * orders, 1.0)
        )
        falling = np.sqrt(
            np.maximum(lower * lower - orders * orders, 0.0) / max(4.0 * lower * lower - 1.0, 1.0)
        )
        current = np.where(
            orders == degree,
            diagonal_start,
            np.where(
                degree > orders,
                rising * (cosines[None, :] * previous - falling * before_previous),
                0.0,
            ),
        )
        result[:, degree] = current
        before_previous = previous
        previous = current
    return result


def fourier_tables(lon_count, mode_order):
    longitude = 2.0 * np.pi * np.arange(lon_count)[:, None] / lon_count
    angles = longitude * (mode_order[None, :] * 1.0)
    forward_factor = math.sqrt(2.0 * math.pi) / lon_count
    forward_table = np.stack(
        [forward_factor * np.cos(angles), -forward_factor * np.sin(angles)], axis=1
    )
    inverse_factor = np.where(mode_order == 0, 1.0, 2.0) / math.sqrt(2.0 * math.pi)
    inverse_table = np.stack(
        [
            (inverse_factor[None, :] * np.cos(angles)).T,
            (-inverse_factor[None, :] * np.sin(angles)).T,
        ],
        axis=0,
    )
    return (forward_table, inverse_table)


def latitude_weights(lat_count):
    colatitude = (jnp.arange(lat_count, dtype=jnp.float32) + 0.5) * (math.pi / lat_count)
    return jnp.sin(colatitude) * (math.pi / lat_count)


def slot_tables():
    forward, inverse = fourier_tables(W, np.arange(M))
    ahead = np.zeros((BANDS, 2, 16, W))
    back = np.zeros((BANDS, 2, 16, W))
    ahead[:, :, :OWN] = forward.reshape(W, 2, OWN, BANDS).transpose(3, 1, 2, 0)
    back[:, :, :OWN] = inverse.reshape(2, OWN, BANDS, W).transpose(2, 0, 1, 3)
    return ahead.reshape(BANDS * SLOTS, W), back.reshape(BANDS * SLOTS, W).T


def rounded(table):
    return jnp.asarray(table, jnp.float32).astype(jnp.bfloat16)


def exchange_matrix():
    matrix = np.zeros((256, 256))
    for a in range(16):
        for b in range(16):
            matrix[b * 16 + a, a * 16 + b] = 1.0
    return matrix


def forward_kernel(weights_ref, x_ref, gain_ref, table_ref, out_ref):
    x = x_ref[0].astype(jnp.float32)
    centred = x - jnp.mean(x, axis=1, keepdims=True)
    variance = jnp.mean(jnp.square(centred), axis=1, keepdims=True)
    normed = (centred * lax.rsqrt(variance + 1e-05) * gain_ref[...]).astype(jnp.bfloat16)
    sums = jnp.dot(table_ref[...], normed, preferred_element_type=jnp.float32)
    sums = (sums * weights_ref[pl.program_id(0)]).astype(jnp.bfloat16)
    out_ref[...] = sums.reshape(BANDS, 1, SLOTS, E)


def forward_transform(x, gain, weights, table):
    return pl.pallas_call(
        forward_kernel,
        grid=(ROWS,),
        in_specs=[
            pl.BlockSpec(memory_space=pltpu.SMEM),
            pl.BlockSpec((1, W, E), lambda j: (j, 0, 0)),
            pl.BlockSpec((1, E), lambda j: (0, 0)),
            pl.BlockSpec((BANDS * SLOTS, W), lambda j: (0, 0)),
        ],
        out_specs=pl.BlockSpec((BANDS, 1, SLOTS, E), lambda j: (0, j, 0, 0)),
        out_shape=jax.ShapeDtypeStruct((BANDS, ROWS, SLOTS, E), jnp.bfloat16),
        compiler_params=pltpu.CompilerParams(vmem_limit_bytes=VMEM_LIMIT),
        cost_estimate=pl.CostEstimate(
            flops=2 * ROWS * BANDS * SLOTS * W * E, bytes_accessed=12 << 20, transcendentals=0
        ),
        name="forward_transform",
    )(weights, x, gain, table)


def spectral_kernel(
    band_ref, moved_ref, legendre_ref, gain_ref, real_ref, imag_ref, swap_ref, out_ref, by_mode, mixed
):
    swap = swap_ref[...]

    def to_modes(step, carry):
        rows = pl.ds(pl.multiple_of(step * 16, 16), 16)
        for part in range(2):
            block = moved_ref[rows, part * 16 : part * 16 + 16, :].reshape(256, E)
            turned = jnp.dot(swap, block, preferred_element_type=jnp.float32)
            by_mode[part, :, rows, :] = turned.astype(jnp.bfloat16).reshape(16, 16, E)
        return carry

    lax.fori_loop(0, H // 16, to_modes, 0)
    mix_real = real_ref[...]
    mix_imag = imag_ref[...]
    for i in range(OWN):
        low = 16 * i
        table = legendre_ref[0, i]
        ahead = table[low:]
        re = jnp.dot(ahead, by_mode[0, i], preferred_element_type=jnp.float32).astype(jnp.bfloat16)
        im = jnp.dot(ahead, by_mode[1, i], preferred_element_type=jnp.float32).astype(jnp.bfloat16)
        gain = gain_ref[low:]
        new_re = jnp.dot(re, mix_real, preferred_element_type=jnp.float32) - jnp.dot(
            im, mix_imag, preferred_element_type=jnp.float32
        )
        new_im = jnp.dot(re, mix_imag, preferred_element_type=jnp.float32) + jnp.dot(
            im, mix_real, preferred_element_type=jnp.float32
        )
        mixed[0, low:, :] = (new_re * gain).astype(jnp.bfloat16)
        mixed[1, low:, :] = (new_im * gain).astype(jnp.bfloat16)
        for part in range(2):
            spatial = lax.dot_general(
                table, mixed[part], (((0,), (0,)), ((), ())), preferred_element_type=jnp.float32
            )
            by_mode[part, i] = spatial.astype(jnp.bfloat16)

    def to_rows(step, carry):
        rows = pl.ds(pl.multiple_of(step * 16, 16), 16)
        for part in range(2):
            block = by_mode[part, :, rows, :].reshape(256, E)
            turned = jnp.dot(swap, block, preferred_element_type=jnp.float32)
            out_ref[rows, part * 16 : part * 16 + 16, :] = turned.astype(jnp.bfloat16).reshape(16, 16, E)
        return carry

    lax.fori_loop(0, H // 16, to_rows, 0)


def spectral_pass(band, moved, legendre, gain, mix_real, mix_imag, swap):
    whole = lambda *shape: pl.BlockSpec(shape, lambda step, band: (0,) * len(shape))
    return pl.pallas_call(
        spectral_kernel,
        grid_spec=pltpu.PrefetchScalarGridSpec(
            num_scalar_prefetch=1,
            grid=(1,),
            in_specs=[
                whole(H, SLOTS, E),
                pl.BlockSpec((1, OWN, L, H), lambda step, band: (band[0], 0, 0, 0)),
                whole(L, 1),
                whole(E, E),
                whole(E, E),
                whole(256, 256),
            ],
            out_specs=whole(H, SLOTS, E),
            scratch_shapes=[
                pltpu.VMEM((2, 16, H, E), jnp.bfloat16),
                pltpu.VMEM((2, L, E), jnp.bfloat16),
            ],
        ),
        out_shape=jax.ShapeDtypeStruct((H, SLOTS, E), jnp.bfloat16),
        compiler_params=pltpu.CompilerParams(vmem_limit_bytes=VMEM_LIMIT),
        cost_estimate=pl.CostEstimate(flops=8 << 30, bytes_accessed=14 << 20, transcendentals=0),
        name="spectral_pass",
    )(band, moved, legendre, gain, mix_real, mix_imag, swap)


def inverse_kernel(spatial_ref, x_ref, table_ref, out_ref):
    sums = jnp.dot(
        table_ref[...], spatial_ref[...].reshape(BANDS * SLOTS, E), preferred_element_type=jnp.float32
    )
    out_ref[0] = (x_ref[0].astype(jnp.float32) + jax.nn.gelu(sums)).astype(jnp.bfloat16)


def inverse_transform(spatial, x, table):
    return pl.pallas_call(
        inverse_kernel,
        grid=(ROWS,),
        in_specs=[
            pl.BlockSpec((BANDS, 1, SLOTS, E), lambda j: (0, j, 0, 0)),
            pl.BlockSpec((1, W, E), lambda j: (j, 0, 0)),
            pl.BlockSpec((W, BANDS * SLOTS), lambda j: (0, 0)),
        ],
        out_specs=pl.BlockSpec((1, W, E), lambda j: (j, 0, 0)),
        out_shape=jax.ShapeDtypeStruct((16, W, E), jnp.bfloat16),
        compiler_params=pltpu.CompilerParams(vmem_limit_bytes=VMEM_LIMIT),
        cost_estimate=pl.CostEstimate(
            flops=2 * ROWS * BANDS * SLOTS * W * E, bytes_accessed=18 << 20, transcendentals=ROWS * W * E
        ),
        name="inverse_transform",
    )(spatial, x, table)


def spread_kernel(weights_ref, own_ref, control_ref, out_ref):
    step = pl.program_id(0)
    difference = own_ref[0].astype(jnp.float32) - control_ref[0].astype(jnp.float32)
    partial = jnp.sum((difference * difference).reshape(W // 8, 8, E), axis=0) * weights_ref[step]

    @pl.when(step == 0)
    def _():
        out_ref[...] = partial

    @pl.when(step > 0)
    def _():
        out_ref[...] += partial


def spread_sums(weights, own, control):
    row = pl.BlockSpec((1, W, E), lambda j: (j, 0, 0))
    return pl.pallas_call(
        spread_kernel,
        grid=(ROWS,),
        in_specs=[pl.BlockSpec(memory_space=pltpu.SMEM), row, row],
        out_specs=pl.BlockSpec((8, E), lambda j: (0, 0)),
        out_shape=jax.ShapeDtypeStruct((8, E), jnp.float32),
        compiler_params=pltpu.CompilerParams(vmem_limit_bytes=VMEM_LIMIT),
        cost_estimate=pl.CostEstimate(flops=9 << 20, bytes_accessed=11 << 20, transcendentals=0),
        name="spread_sums",
    )(weights, own, control)


def rescale_kernel(scale_ref, own_ref, control_ref, out_ref):
    control = control_ref[...].astype(jnp.float32)
    difference = own_ref[...].astype(jnp.float32) - control
    out_ref[...] = (control + scale_ref[0] * difference).astype(jnp.bfloat16)


def rescaled(scale, own, control):
    row = pl.BlockSpec((1, W, E), lambda j: (j, 0, 0))
    return pl.pallas_call(
        rescale_kernel,
        grid=(ROWS,),
        in_specs=[pl.BlockSpec(memory_space=pltpu.SMEM), row, row],
        out_specs=row,
        out_shape=jax.ShapeDtypeStruct((ROWS, W, E), jnp.bfloat16),
        compiler_params=pltpu.CompilerParams(vmem_limit_bytes=VMEM_LIMIT),
        cost_estimate=pl.CostEstimate(flops=9 << 20, bytes_accessed=17 << 20, transcendentals=0),
        name="rescaled",
    )(scale, own, control)


def from_control(field):
    eighths = field.reshape(DEPTH, 2, W, E)
    piece = eighths[0]
    for z in range(1, DEPTH):
        arrived = lax.ppermute(eighths[z], "member", [(0, 2 * z)])
        piece = jnp.where(lax.axis_index("member") == 2 * z, arrived, piece)
    across = lax.ppermute(piece, "member", [(2 * z, 2 * z + 1) for z in range(DEPTH)])
    piece = jnp.where(lax.axis_index("member") % 2 == 1, across, piece)
    rings = [[2 * z + h for z in range(DEPTH)] for h in range(2)]
    return lax.all_gather(piece, "member", tiled=True, axis_index_groups=rings)


def summed_over_band(partial):
    copies = jnp.broadcast_to(partial[None], (BANDS,) + partial.shape)
    return jnp.sum(lax.all_to_all(copies, "band", split_axis=0, concat_axis=0, tiled=True))


def shards(
    copy_fields,
    norm_gain,
    mix_real,
    mix_imag,
    filter_bank,
    perturbation_draw_numbers,
    amplitudes,
    desired_magnitude_slot,
):
    band_index = lax.axis_index("band")
    ahead_np, back_np = slot_tables()
    legendre_np = legendre_table(L, M, H).reshape(OWN, BANDS, L, H).transpose(1, 0, 2, 3)
    x = jnp.transpose(copy_fields[0], (0, 2, 1))

    global_rows = band_index * ROWS + jnp.arange(ROWS, dtype=jnp.int32)
    weights = jnp.sin((global_rows.astype(jnp.float32) + 0.5) * (math.pi / H)) * (math.pi / H)
    total_weight = jnp.sum(latitude_weights(H)) * (E * W)
    bank_rows = filter_bank.shape[0]
    draw_onehot = (jnp.arange(bank_rows, dtype=jnp.int32) == perturbation_draw_numbers[0]).astype(
        jnp.float32
    )
    degree_gain = jnp.sum(draw_onehot[:, None] * filter_bank, axis=0)

    fourier = forward_transform(x, norm_gain[None, :], weights, rounded(ahead_np))
    moved = lax.all_to_all(fourier, "band", split_axis=0, concat_axis=0, tiled=True)
    returned = spectral_pass(
        band_index[None],
        moved.reshape(H, SLOTS, E),
        rounded(legendre_np),
        degree_gain[:, None],
        mix_real,
        mix_imag,
        rounded(exchange_matrix()),
    )
    spatial = lax.all_to_all(
        returned.reshape(BANDS, ROWS, SLOTS, E), "band", split_axis=0, concat_axis=0, tiled=True
    )
    forecast = inverse_transform(spatial, x, rounded(back_np))
    control = from_control(forecast)
    spread_sum = summed_over_band(spread_sums(weights, forecast, control))
    spread = spread_sum / total_weight
    target = jnp.sum(
        jnp.where(
            jnp.arange(amplitudes.shape[0], dtype=jnp.int32) == desired_magnitude_slot[0],
            amplitudes,
            0.0,
        )
    )
    scale = target / jnp.sqrt(spread + 1e-06)
    bred = rescaled(scale[None], forecast, control)
    return jnp.transpose(bred, (0, 2, 1))[None]


def solution(mesh):
    in_specs = (P("member", "band", None, None), P(), P(), P(), P(), P("member"), P(), P("member"))
    out_specs = P("member", "band", None, None)
    return jax.shard_map(shards, mesh=mesh, in_specs=in_specs, out_specs=out_specs, check_vma=False)
```

```python
import functools
import math

import jax
import jax.numpy as jnp
import numpy as np
from jax import lax
from jax.experimental import pallas as pl
from jax.experimental.pallas import tpu as pltpu
from jax.sharding import PartitionSpec as P

H = 240
W = 480
M = 240
L = 240
E = 384
BANDS = 16
ROWS = H // BANDS
OWN = M // BANDS
SLOTS = 32
DEPTH = 8
RINGS = [[2 * z + h for z in range(DEPTH)] for h in range(2)]
STEP = 3
VMEM_LIMIT = 58 * 1024 * 1024


def legendre_table(degree_count, order_count, lat_count):
    colatitude = (np.arange(lat_count) + 0.5) * np.pi / lat_count
    cosines = np.cos(colatitude)
    sines = np.sin(colatitude)
    orders = np.arange(order_count)[:, None] * 1.0
    steps_up = np.arange(1, order_count) * 1.0
    log_factor = np.concatenate(
        [[0.0], np.cumsum(np.log((2.0 * steps_up - 1.0) / (2.0 * steps_up)))]
    )
    diagonal_start = np.exp(
        0.5 * np.log((2.0 * orders + 1.0) / 2.0)
        + 0.5 * log_factor[:, None]
        + orders * np.log(sines)[None, :]
    )
    result = np.zeros((order_count, degree_count, lat_count))
    previous = np.zeros(diagonal_start.shape)
    before_previous = np.zeros(diagonal_start.shape)
    for degree in range(degree_count):
        lower = degree - 1.0
        rising = np.sqrt(
            np.maximum(4.0 * degree * degree - 1.0, 1.0)
            / np.maximum(degree * degree - orders * orders, 1.0)
        )
        falling = np.sqrt(
            np.maximum(lower * lower - orders * orders, 0.0) / max(4.0 * lower * lower - 1.0, 1.0)
        )
        current = np.where(
            orders == degree,
            diagonal_start,
            np.where(
                degree > orders,
                rising * (cosines[None, :] * previous - falling * before_previous),
                0.0,
            ),
        )
        result[:, degree] = current
        before_previous = previous
        previous = current
    return result


def fourier_tables(lon_count, mode_order):
    longitude = 2.0 * np.pi * np.arange(lon_count)[:, None] / lon_count
    angles = longitude * (mode_order[None, :] * 1.0)
    forward_factor = math.sqrt(2.0 * math.pi) / lon_count
    forward_table = np.stack(
        [forward_factor * np.cos(angles), -forward_factor * np.sin(angles)], axis=1
    )
    inverse_factor = np.where(mode_order == 0, 1.0, 2.0) / math.sqrt(2.0 * math.pi)
    inverse_table = np.stack(
        [
            (inverse_factor[None, :] * np.cos(angles)).T,
            (-inverse_factor[None, :] * np.sin(angles)).T,
        ],
        axis=0,
    )
    return (forward_table, inverse_table)


def latitude_weights(lat_count):
    colatitude = (jnp.arange(lat_count, dtype=jnp.float32) + 0.5) * (math.pi / lat_count)
    return jnp.sin(colatitude) * (math.pi / lat_count)


def slot_tables():
    forward, inverse = fourier_tables(W, np.arange(M))
    ahead = np.zeros((W, 2, 16, BANDS))
    back = np.zeros((2, 16, BANDS, W))
    ahead[:, :, :OWN] = forward.reshape(W, 2, OWN, BANDS)
    back[:, :OWN] = inverse.reshape(2, OWN, BANDS, W)
    ahead = ahead.reshape(W, 2, DEPTH, 2, BANDS)
    back = back.reshape(2, DEPTH, 2, BANDS, W)
    rows = BANDS * SLOTS
    return (
        ahead.transpose(4, 2, 1, 3, 0).reshape(rows, W),
        back.transpose(3, 1, 0, 2, 4).reshape(rows, W).T,
        ahead.transpose(2, 4, 1, 3, 0).reshape(rows, W),
        back.transpose(1, 3, 0, 2, 4).reshape(rows, W).T,
    )


def rounded(table):
    return jnp.asarray(table, jnp.float32).astype(jnp.bfloat16)


def exchange_matrix():
    matrix = np.zeros((256, 256))
    for a in range(16):
        for b in range(16):
            matrix[b * 16 + a, a * 16 + b] = 1.0
    return matrix


def forward_kernel(weights_ref, x_ref, gain_ref, table_ref, out_ref):
    rows = x_ref.shape[0]
    for j in range(rows):
        x = x_ref[j].astype(jnp.float32)
        centred = x - jnp.mean(x, axis=1, keepdims=True)
        variance = jnp.mean(jnp.square(centred), axis=1, keepdims=True)
        normed = (centred * lax.rsqrt(variance + 1e-05) * gain_ref[...]).astype(jnp.bfloat16)
        sums = jnp.dot(table_ref[...], normed, preferred_element_type=jnp.float32)
        sums = (sums * weights_ref[pl.program_id(0) * rows + j]).astype(jnp.bfloat16)
        out_ref[:, j] = sums.reshape(out_ref.shape[0], out_ref.shape[2], E)


def forward_transform(x, gain, weights, table, groups, step):
    rows = x.shape[0]
    size = BANDS * SLOTS // groups
    return pl.pallas_call(
        forward_kernel,
        grid=(rows // step,),
        in_specs=[
            pl.BlockSpec(memory_space=pltpu.SMEM),
            pl.BlockSpec((step, W, E), lambda j: (j, 0, 0)),
            pl.BlockSpec((1, E), lambda j: (0, 0)),
            pl.BlockSpec((BANDS * SLOTS, W), lambda j: (0, 0)),
        ],
        out_specs=pl.BlockSpec((groups, step, size, E), lambda j: (0, j, 0, 0)),
        out_shape=jax.ShapeDtypeStruct((groups, rows, size, E), jnp.bfloat16),
        compiler_params=pltpu.CompilerParams(vmem_limit_bytes=VMEM_LIMIT),
        cost_estimate=pl.CostEstimate(
            flops=2 * rows * BANDS * SLOTS * W * E, bytes_accessed=rows << 20, transcendentals=0
        ),
        name="forward_transform",
    )(weights, x, gain, table)


def mix_degrees(table, values, gain, mixing):
    coeffs = jnp.dot(table, values, preferred_element_type=jnp.float32).astype(jnp.bfloat16)
    return (jnp.dot(coeffs, mixing, preferred_element_type=jnp.float32) * gain).astype(jnp.bfloat16)


def to_latitudes(table, mixed):
    return lax.dot_general(
        table, mixed, (((0,), (0,)), ((), ())), preferred_element_type=jnp.float32
    ).astype(jnp.bfloat16)


def shared_spectral_kernel(
    place_ref, re_ref, im_ref, legendre_ref, gain_ref, mixing_ref, out_re_ref, out_im_ref
):
    table = legendre_ref[0, 0]
    values = jnp.concatenate([re_ref[0], im_ref[0]], axis=1)
    spatial = to_latitudes(table, mix_degrees(table, values, gain_ref[...], mixing_ref[...]))
    out_re_ref[0] = spatial[:, :E]
    out_im_ref[0] = spatial[:, E:]


def shared_spectral_pass(place, moved, legendre, gain, mixing):
    row = lambda first: pl.BlockSpec((1, H, E), lambda o, place: (first + o, 0, 0))
    whole = lambda *shape: pl.BlockSpec(shape, lambda o, place: (0,) * len(shape))
    pair = jax.ShapeDtypeStruct((2, H, E), jnp.bfloat16)
    out_re, out_im = pl.pallas_call(
        shared_spectral_kernel,
        grid_spec=pltpu.PrefetchScalarGridSpec(
            num_scalar_prefetch=1,
            grid=(2,),
            in_specs=[
                row(0),
                row(2),
                pl.BlockSpec(
                    (1, 1, L, H),
                    lambda o, place: (place[0], jnp.minimum(2 * place[1] + o, OWN - 1), 0, 0),
                ),
                whole(L, 1),
                whole(2 * E, 2 * E),
            ],
            out_specs=[row(0), row(0)],
        ),
        out_shape=[pair, pair],
        compiler_params=pltpu.CompilerParams(vmem_limit_bytes=VMEM_LIMIT),
        cost_estimate=pl.CostEstimate(flops=1 << 30, bytes_accessed=4 << 20, transcendentals=0),
        name="shared_spectral_pass",
    )(place, moved, moved, legendre, gain, mixing)
    return jnp.concatenate([out_re, out_im], axis=0)


def spectral_kernel(
    band_ref, moved_ref, legendre_ref, gain_ref, mixing_ref, swap_ref, out_ref, by_mode, mixed
):
    swap = swap_ref[...]
    halves = [(half, lanes) for half, lanes in ((0, slice(0, E)), (16, slice(E, 2 * E)))]
    unroll = 3

    def place_of(slot):
        z, part, o = slot // 4, (slot // 2) % 2, slot % 2
        return 2 * z + o, slice(part * E, part * E + E)

    def to_modes(step, carry):
        for piece in range(unroll):
            rows = pl.ds(pl.multiple_of((step * unroll + piece) * 16, 16), 16)
            block = jnp.concatenate(
                [moved_ref[rows, half : half + 16, :].reshape(256, E) for half, _ in halves], axis=1
            )
            turned = jnp.dot(swap, block, preferred_element_type=jnp.float32).astype(jnp.bfloat16)
            turned = turned.reshape(16, 16, 2 * E)
            for half, lanes in halves:
                for k in range(16):
                    i, part = place_of(half + k)
                    by_mode[i, rows, part] = turned[k, :, lanes]
        return carry

    lax.fori_loop(0, H // 16 // unroll, to_modes, 0)
    mixing = mixing_ref[...]
    for i in range(OWN):
        low = 16 * i
        table = legendre_ref[0, i]
        mixed[low:, :] = mix_degrees(table[low:], by_mode[i], gain_ref[low:], mixing)
        by_mode[i] = to_latitudes(table, mixed[...])

    def to_rows(step, carry):
        for piece in range(unroll):
            rows = pl.ds(pl.multiple_of((step * unroll + piece) * 16, 16), 16)
            blocks = []
            for half, _ in halves:
                slots = []
                for k in range(16):
                    i, part = place_of(half + k)
                    slots.append(by_mode[i, rows, part])
                blocks.append(jnp.concatenate(slots, axis=0))
            block = jnp.concatenate(blocks, axis=1)
            turned = jnp.dot(swap, block, preferred_element_type=jnp.float32).astype(jnp.bfloat16)
            turned = turned.reshape(16, 16, 2 * E)
            for half, lanes in halves:
                out_ref[rows, half : half + 16, :] = turned[:, :, lanes]
        return carry

    lax.fori_loop(0, H // 16 // unroll, to_rows, 0)


def spectral_pass(band, moved, legendre, gain, mixing, swap):
    whole = lambda *shape: pl.BlockSpec(shape, lambda step, band: (0,) * len(shape))
    return pl.pallas_call(
        spectral_kernel,
        grid_spec=pltpu.PrefetchScalarGridSpec(
            num_scalar_prefetch=1,
            grid=(1,),
            in_specs=[
                whole(H, SLOTS, E),
                pl.BlockSpec((1, OWN, L, H), lambda step, band: (band[0], 0, 0, 0)),
                whole(L, 1),
                whole(2 * E, 2 * E),
                whole(256, 256),
            ],
            out_specs=whole(H, SLOTS, E),
            scratch_shapes=[
                pltpu.VMEM((16, H, 2 * E), jnp.bfloat16),
                pltpu.VMEM((L, 2 * E), jnp.bfloat16),
            ],
        ),
        out_shape=jax.ShapeDtypeStruct((H, SLOTS, E), jnp.bfloat16),
        compiler_params=pltpu.CompilerParams(vmem_limit_bytes=VMEM_LIMIT),
        cost_estimate=pl.CostEstimate(flops=8 << 30, bytes_accessed=14 << 20, transcendentals=0),
        name="spectral_pass",
    )(band, moved, legendre, gain, mixing, swap)


def inverse_kernel(spatial_ref, x_ref, table_ref, out_ref):
    for j in range(x_ref.shape[0]):
        spatial = spatial_ref[:, j].reshape(BANDS * SLOTS, E)
        sums = jnp.dot(table_ref[...], spatial, preferred_element_type=jnp.float32)
        out_ref[j] = (x_ref[j].astype(jnp.float32) + jax.nn.gelu(sums)).astype(jnp.bfloat16)


def inverse_transform(spatial, x, table, step, flops):
    rows = x.shape[0]
    groups, _, size, _ = spatial.shape
    return pl.pallas_call(
        inverse_kernel,
        grid=(rows // step,),
        in_specs=[
            pl.BlockSpec((groups, step, size, E), lambda j: (0, j, 0, 0)),
            pl.BlockSpec((step, W, E), lambda j: (j, 0, 0)),
            pl.BlockSpec((W, BANDS * SLOTS), lambda j: (0, 0)),
        ],
        out_specs=pl.BlockSpec((step, W, E), lambda j: (j, 0, 0)),
        out_shape=jax.ShapeDtypeStruct((rows, W, E), jnp.bfloat16),
        compiler_params=pltpu.CompilerParams(vmem_limit_bytes=VMEM_LIMIT),
        cost_estimate=pl.CostEstimate(
            flops=flops, bytes_accessed=rows << 20, transcendentals=rows * W * E
        ),
        name="inverse_transform",
    )(spatial, x, table)


def difference_of(share, own, control):
    return jnp.where(share > 0.0, own.astype(jnp.float32) - control, 0.0)


def spread_kernel(weights_ref, share_ref, own_ref, control_ref, out_ref):
    step = pl.program_id(0)
    partial = 0.0
    for j in range(STEP):
        difference = difference_of(share_ref[0], own_ref[j], control_ref[j].astype(jnp.float32))
        squares = jnp.sum((difference * difference).reshape(W // 8, 8, E), axis=0)
        partial = partial + squares * weights_ref[step * STEP + j]

    @pl.when(step == 0)
    def _():
        out_ref[...] = partial

    @pl.when(step > 0)
    def _():
        out_ref[...] += partial


def spread_sums(weights, share, own, control):
    row = pl.BlockSpec((STEP, W, E), lambda j: (j, 0, 0))
    return pl.pallas_call(
        spread_kernel,
        grid=(ROWS // STEP,),
        in_specs=[pl.BlockSpec(memory_space=pltpu.SMEM), pl.BlockSpec(memory_space=pltpu.SMEM), row, row],
        out_specs=pl.BlockSpec((8, E), lambda j: (0, 0)),
        out_shape=jax.ShapeDtypeStruct((8, E), jnp.float32),
        compiler_params=pltpu.CompilerParams(vmem_limit_bytes=VMEM_LIMIT),
        cost_estimate=pl.CostEstimate(flops=9 << 20, bytes_accessed=11 << 20, transcendentals=0),
        name="spread_sums",
    )(weights, share, own, control)


def rescale_kernel(scale_ref, share_ref, own_ref, control_ref, out_ref):
    control = control_ref[...].astype(jnp.float32)
    difference = difference_of(share_ref[0], own_ref[...], control)
    out_ref[...] = (control + scale_ref[0] * difference).astype(jnp.bfloat16)


def rescaled(scale, share, own, control):
    row = pl.BlockSpec((STEP, W, E), lambda j: (j, 0, 0))
    return pl.pallas_call(
        rescale_kernel,
        grid=(ROWS // STEP,),
        in_specs=[pl.BlockSpec(memory_space=pltpu.SMEM), pl.BlockSpec(memory_space=pltpu.SMEM), row, row],
        out_specs=row,
        out_shape=jax.ShapeDtypeStruct((ROWS, W, E), jnp.bfloat16),
        compiler_params=pltpu.CompilerParams(vmem_limit_bytes=VMEM_LIMIT),
        cost_estimate=pl.CostEstimate(flops=9 << 20, bytes_accessed=17 << 20, transcendentals=0),
        name="rescaled",
    )(scale, share, own, control)


def scattered(pieces):
    member = lax.axis_index("member")
    kept = pieces[0]
    for z in range(1, DEPTH):
        arrived = lax.ppermute(pieces[z], "member", [(0, 2 * z)])
        kept = jnp.where(member == 2 * z, arrived, kept)
    return kept


def exchanged_along_z(pieces, z):
    result = pieces
    for shift in range(1, DEPTH):
        block = lax.dynamic_index_in_dim(pieces, (z + shift) % DEPTH, 0, keepdims=False)
        pairs = [(ring[a], ring[(a + shift) % DEPTH]) for ring in RINGS for a in range(DEPTH)]
        arrived = lax.ppermute(block, "member", pairs)
        result = lax.dynamic_update_index_in_dim(result, arrived, (z - shift) % DEPTH, 0)
    return result


def to_everyone(piece):
    across = lax.ppermute(piece, "member", [(2 * z, 2 * z + 1) for z in range(DEPTH)])
    piece = jnp.where(lax.axis_index("member") % 2 == 1, across, piece)
    return lax.all_gather(piece, "member", tiled=True, axis_index_groups=RINGS)


def doubled_along_z(value):
    z = lax.axis_index("member") // 2
    for stride in (4, 2, 1):
        pairs = [(2 * a, 2 * (a + stride)) for a in range(0, DEPTH, 2 * stride)]
        arrived = lax.ppermute(value, "member", pairs)
        value = jnp.where(z % (2 * stride) == stride, arrived, value)
    return value


def summed_over_band(partial):
    copies = jnp.broadcast_to(partial[None], (BANDS,) + partial.shape)
    return jnp.sum(lax.all_to_all(copies, "band", split_axis=0, concat_axis=0, tiled=True))


def shards(
    copy_fields,
    norm_gain,
    mix_real,
    mix_imag,
    filter_bank,
    perturbation_draw_numbers,
    amplitudes,
    desired_magnitude_slot,
):
    band_index = lax.axis_index("band")
    ahead_np, back_np, shared_ahead_np, shared_back_np = slot_tables()
    legendre_np = legendre_table(L, M, H).reshape(OWN, BANDS, L, H).transpose(1, 0, 2, 3)
    x = jnp.transpose(copy_fields[0], (0, 2, 1))

    global_rows = band_index * ROWS + jnp.arange(ROWS, dtype=jnp.int32)
    weights = jnp.sin((global_rows.astype(jnp.float32) + 0.5) * (math.pi / H)) * (math.pi / H)
    total_weight = jnp.sum(latitude_weights(H)) * (E * W)
    bank_rows = filter_bank.shape[0]
    draw_onehot = (jnp.arange(bank_rows, dtype=jnp.int32) == perturbation_draw_numbers[0]).astype(
        jnp.float32
    )
    degree_gain = jnp.sum(draw_onehot[:, None] * filter_bank, axis=0)

    legendre = rounded(legendre_np)
    gain = degree_gain[:, None]
    member = lax.axis_index("member")
    place = jnp.stack([band_index, member // 2])
    share = jnp.where(member > 0, 1.0, 0.0)[None]

    mixing = jnp.concatenate(
        [jnp.concatenate([mix_real, mix_imag], 1), jnp.concatenate([-mix_imag, mix_real], 1)], 0
    )
    z = member // 2

    fourier = forward_transform(x, norm_gain[None, :], weights, rounded(ahead_np), BANDS, STEP)
    moved = lax.all_to_all(fourier, "band", split_axis=0, concat_axis=0, tiled=True)

    control_x = scattered(
        [x[2 * a : 2 * a + 2] for a in range(DEPTH - 1)] + [jnp.concatenate([x[ROWS - 1 :]] * 2)]
    )
    control_gain = doubled_along_z(degree_gain[None, :])
    control_weights = lax.dynamic_slice(jnp.pad(weights, (0, 1)), (2 * z,), (2,))
    control_fourier = forward_transform(
        control_x, norm_gain[None, :], control_weights, rounded(shared_ahead_np), DEPTH, 2
    )
    control_fourier = exchanged_along_z(control_fourier, z).reshape(DEPTH, 2, BANDS, 4, E)
    control_fourier = control_fourier.transpose(2, 0, 1, 3, 4).reshape(BANDS, 16, 4, E)[:, :ROWS]
    moved, control_fourier = lax.optimization_barrier((moved, control_fourier))
    control_moved = lax.all_to_all(control_fourier, "band", split_axis=0, concat_axis=0, tiled=True)
    returned = spectral_pass(
        band_index[None],
        moved.reshape(H, SLOTS, E),
        legendre,
        gain,
        mixing,
        rounded(exchange_matrix()),
    )
    control_spatial = shared_spectral_pass(
        place,
        control_moved.reshape(H, 4, E).transpose(1, 0, 2),
        legendre,
        control_gain.reshape(L, 1),
        mixing,
    )
    control_spatial = lax.all_to_all(
        control_spatial.transpose(1, 0, 2).reshape(BANDS, ROWS, 4, E),
        "band",
        split_axis=0,
        concat_axis=0,
        tiled=True,
    )
    control_spatial, returned = lax.optimization_barrier((control_spatial, returned))
    spatial = lax.all_to_all(
        returned.reshape(BANDS, ROWS, SLOTS, E), "band", split_axis=0, concat_axis=0, tiled=True
    )
    control_spatial = jnp.pad(control_spatial, ((0, 0), (0, 1), (0, 0), (0, 0)))
    control_spatial = control_spatial.reshape(BANDS, DEPTH, 2, 4, E).transpose(1, 2, 0, 3, 4)
    control_spatial = exchanged_along_z(control_spatial.reshape(DEPTH, 2, BANDS * 4, E), z)
    control = to_everyone(
        inverse_transform(control_spatial, control_x, rounded(shared_back_np), 2, 1 << 29)
    )

    forecast = inverse_transform(spatial, x, rounded(back_np), STEP, 1 << 38)
    spread_sum = summed_over_band(spread_sums(weights, share, forecast, control))
    spread = spread_sum / total_weight
    target = jnp.sum(
        jnp.where(
            jnp.arange(amplitudes.shape[0], dtype=jnp.int32) == desired_magnitude_slot[0],
            amplitudes,
            0.0,
        )
    )
    scale = target / jnp.sqrt(spread + 1e-06)
    bred = rescaled(scale[None], share, forecast, control)
    return jnp.transpose(bred, (0, 2, 1))[None]


def solution(mesh):
    in_specs = (P("member", "band", None, None), P(), P(), P(), P(), P("member"), P(), P("member"))
    out_specs = P("member", "band", None, None)
    return jax.shard_map(shards, mesh=mesh, in_specs=in_specs, out_specs=out_specs, check_vma=False)
```

```python
import functools
import math

import jax
import jax.numpy as jnp
import numpy as np
from jax import lax
from jax.experimental import pallas as pl
from jax.experimental.pallas import tpu as pltpu
from jax.sharding import PartitionSpec as P

H = 240
W = 480
M = 240
L = 240
E = 384
BANDS = 16
ROWS = H // BANDS
OWN = M // BANDS
SLOTS = 32
DEPTH = 8
RINGS = [[2 * z + h for z in range(DEPTH)] for h in range(2)]
STEP = 3
TOTAL_WEIGHT = float(np.sum(np.sin((np.arange(H) + 0.5) * np.pi / H)) * np.pi / H * E * W)
VMEM_LIMIT = 58 * 1024 * 1024


def legendre_table(degree_count, order_count, lat_count):
    colatitude = (np.arange(lat_count) + 0.5) * np.pi / lat_count
    cosines = np.cos(colatitude)
    sines = np.sin(colatitude)
    orders = np.arange(order_count)[:, None] * 1.0
    steps_up = np.arange(1, order_count) * 1.0
    log_factor = np.concatenate(
        [[0.0], np.cumsum(np.log((2.0 * steps_up - 1.0) / (2.0 * steps_up)))]
    )
    diagonal_start = np.exp(
        0.5 * np.log((2.0 * orders + 1.0) / 2.0)
        + 0.5 * log_factor[:, None]
        + orders * np.log(sines)[None, :]
    )
    result = np.zeros((order_count, degree_count, lat_count))
    previous = np.zeros(diagonal_start.shape)
    before_previous = np.zeros(diagonal_start.shape)
    for degree in range(degree_count):
        lower = degree - 1.0
        rising = np.sqrt(
            np.maximum(4.0 * degree * degree - 1.0, 1.0)
            / np.maximum(degree * degree - orders * orders, 1.0)
        )
        falling = np.sqrt(
            np.maximum(lower * lower - orders * orders, 0.0) / max(4.0 * lower * lower - 1.0, 1.0)
        )
        current = np.where(
            orders == degree,
            diagonal_start,
            np.where(
                degree > orders,
                rising * (cosines[None, :] * previous - falling * before_previous),
                0.0,
            ),
        )
        result[:, degree] = current
        before_previous = previous
        previous = current
    return result


def fourier_tables(lon_count, mode_order):
    longitude = 2.0 * np.pi * np.arange(lon_count)[:, None] / lon_count
    angles = longitude * (mode_order[None, :] * 1.0)
    forward_factor = math.sqrt(2.0 * math.pi) / lon_count
    forward_table = np.stack(
        [forward_factor * np.cos(angles), -forward_factor * np.sin(angles)], axis=1
    )
    inverse_factor = np.where(mode_order == 0, 1.0, 2.0) / math.sqrt(2.0 * math.pi)
    inverse_table = np.stack(
        [
            (inverse_factor[None, :] * np.cos(angles)).T,
            (-inverse_factor[None, :] * np.sin(angles)).T,
        ],
        axis=0,
    )
    return (forward_table, inverse_table)


def slot_tables():
    forward, inverse = fourier_tables(W, np.arange(M))
    ahead = np.zeros((W, 2, 16, BANDS))
    back = np.zeros((2, 16, BANDS, W))
    ahead[:, :, :OWN] = forward.reshape(W, 2, OWN, BANDS)
    back[:, :OWN] = inverse.reshape(2, OWN, BANDS, W)
    ahead = ahead.reshape(W, 2, DEPTH, 2, BANDS)
    back = back.reshape(2, DEPTH, 2, BANDS, W)
    rows = BANDS * SLOTS
    return (
        ahead.transpose(4, 2, 1, 3, 0).reshape(rows, W),
        back.transpose(3, 1, 0, 2, 4).reshape(rows, W).T,
        ahead.transpose(2, 4, 1, 3, 0).reshape(rows, W),
        back.transpose(1, 3, 0, 2, 4).reshape(rows, W).T,
    )


def rounded(table):
    return jnp.asarray(table, jnp.float32).astype(jnp.bfloat16)


def exchange_matrix():
    matrix = np.zeros((256, 256))
    for a in range(16):
        for b in range(16):
            matrix[b * 16 + a, a * 16 + b] = 1.0
    return matrix


def forward_kernel(weights_ref, x_ref, gain_ref, table_ref, out_ref):
    rows = x_ref.shape[0]
    for j in range(rows):
        x = x_ref[j].astype(jnp.float32)
        centred = x - jnp.mean(x, axis=1, keepdims=True)
        variance = jnp.mean(jnp.square(centred), axis=1, keepdims=True)
        normed = (centred * lax.rsqrt(variance + 1e-05) * gain_ref[...]).astype(jnp.bfloat16)
        sums = jnp.dot(table_ref[...], normed, preferred_element_type=jnp.float32)
        sums = (sums * weights_ref[pl.program_id(0) * rows + j]).astype(jnp.bfloat16)
        out_ref[:, j] = sums.reshape(out_ref.shape[0], out_ref.shape[2], E)


def forward_transform(x, gain, weights, table, groups, step, flops):
    rows = x.shape[0]
    size = BANDS * SLOTS // groups
    return pl.pallas_call(
        forward_kernel,
        grid=(rows // step,),
        in_specs=[
            pl.BlockSpec(memory_space=pltpu.SMEM),
            pl.BlockSpec((step, W, E), lambda j: (j, 0, 0)),
            pl.BlockSpec((1, E), lambda j: (0, 0)),
            pl.BlockSpec((BANDS * SLOTS, W), lambda j: (0, 0)),
        ],
        out_specs=pl.BlockSpec((groups, step, size, E), lambda j: (0, j, 0, 0)),
        out_shape=jax.ShapeDtypeStruct((groups, rows, size, E), jnp.bfloat16),
        compiler_params=pltpu.CompilerParams(vmem_limit_bytes=VMEM_LIMIT),
        cost_estimate=pl.CostEstimate(flops=flops, bytes_accessed=rows << 20, transcendentals=0),
        name="forward_transform",
    )(weights, x, gain, table)


def mix_degrees(table, values, gain, mixing):
    coeffs = jnp.dot(table, values, preferred_element_type=jnp.float32).astype(jnp.bfloat16)
    return (jnp.dot(coeffs, mixing, preferred_element_type=jnp.float32) * gain).astype(jnp.bfloat16)


def to_latitudes(table, mixed):
    return lax.dot_general(
        table, mixed, (((0,), (0,)), ((), ())), preferred_element_type=jnp.float32
    ).astype(jnp.bfloat16)


def shared_spectral_kernel(
    place_ref, re_ref, im_ref, legendre_ref, gain_ref, mixing_ref, out_re_ref, out_im_ref
):
    table = legendre_ref[0, 0]
    values = jnp.concatenate([re_ref[0], im_ref[0]], axis=1)
    spatial = to_latitudes(table, mix_degrees(table, values, gain_ref[...], mixing_ref[...]))
    out_re_ref[0] = spatial[:, :E]
    out_im_ref[0] = spatial[:, E:]


def shared_spectral_pass(place, moved, legendre, gain, mixing):
    row = lambda first: pl.BlockSpec((1, H, E), lambda o, place: (first + o, 0, 0))
    whole = lambda *shape: pl.BlockSpec(shape, lambda o, place: (0,) * len(shape))
    pair = jax.ShapeDtypeStruct((2, H, E), jnp.bfloat16)
    out_re, out_im = pl.pallas_call(
        shared_spectral_kernel,
        grid_spec=pltpu.PrefetchScalarGridSpec(
            num_scalar_prefetch=1,
            grid=(2,),
            in_specs=[
                row(0),
                row(2),
                pl.BlockSpec(
                    (1, 1, L, H),
                    lambda o, place: (place[0], jnp.minimum(2 * place[1] + o, OWN - 1), 0, 0),
                ),
                whole(L, 1),
                whole(2 * E, 2 * E),
            ],
            out_specs=[row(0), row(0)],
        ),
        out_shape=[pair, pair],
        compiler_params=pltpu.CompilerParams(vmem_limit_bytes=VMEM_LIMIT),
        cost_estimate=pl.CostEstimate(flops=1 << 30, bytes_accessed=4 << 20, transcendentals=0),
        name="shared_spectral_pass",
    )(place, moved, moved, legendre, gain, mixing)
    return jnp.concatenate([out_re, out_im], axis=0)


def spectral_kernel(
    band_ref, moved_ref, legendre_ref, gain_ref, mixing_ref, swap_ref, out_ref, by_mode, mixed
):
    swap = swap_ref[...]
    halves = [(half, lanes) for half, lanes in ((0, slice(0, E)), (16, slice(E, 2 * E)))]
    unroll = 3

    def place_of(slot):
        z, part, o = slot // 4, (slot // 2) % 2, slot % 2
        return 2 * z + o, slice(part * E, part * E + E)

    def to_modes(step, carry):
        for piece in range(unroll):
            rows = pl.ds(pl.multiple_of((step * unroll + piece) * 16, 16), 16)
            block = jnp.concatenate(
                [moved_ref[rows, half : half + 16, :].reshape(256, E) for half, _ in halves], axis=1
            )
            turned = jnp.dot(swap, block, preferred_element_type=jnp.float32).astype(jnp.bfloat16)
            turned = turned.reshape(16, 16, 2 * E)
            for half, lanes in halves:
                for k in range(16):
                    i, part = place_of(half + k)
                    by_mode[i, rows, part] = turned[k, :, lanes]
        return carry

    lax.fori_loop(0, H // 16 // unroll, to_modes, 0)
    mixing = mixing_ref[...]
    for i in range(OWN):
        low = 16 * i
        table = legendre_ref[0, i]
        mixed[low:, :] = mix_degrees(table[low:], by_mode[i], gain_ref[low:], mixing)
        by_mode[i] = to_latitudes(table, mixed[...])

    def to_rows(step, carry):
        for piece in range(unroll):
            rows = pl.ds(pl.multiple_of((step * unroll + piece) * 16, 16), 16)
            blocks = []
            for half, _ in halves:
                slots = []
                for k in range(16):
                    i, part = place_of(half + k)
                    slots.append(by_mode[i, rows, part])
                blocks.append(jnp.concatenate(slots, axis=0))
            block = jnp.concatenate(blocks, axis=1)
            turned = jnp.dot(swap, block, preferred_element_type=jnp.float32).astype(jnp.bfloat16)
            turned = turned.reshape(16, 16, 2 * E)
            for half, lanes in halves:
                out_ref[rows, half : half + 16, :] = turned[:, :, lanes]
        return carry

    lax.fori_loop(0, H // 16 // unroll, to_rows, 0)


def spectral_pass(band, moved, legendre, gain, mixing, swap):
    whole = lambda *shape: pl.BlockSpec(shape, lambda step, band: (0,) * len(shape))
    return pl.pallas_call(
        spectral_kernel,
        grid_spec=pltpu.PrefetchScalarGridSpec(
            num_scalar_prefetch=1,
            grid=(1,),
            in_specs=[
                whole(H, SLOTS, E),
                pl.BlockSpec((1, OWN, L, H), lambda step, band: (band[0], 0, 0, 0)),
                whole(L, 1),
                whole(2 * E, 2 * E),
                whole(256, 256),
            ],
            out_specs=whole(H, SLOTS, E),
            scratch_shapes=[
                pltpu.VMEM((16, H, 2 * E), jnp.bfloat16),
                pltpu.VMEM((L, 2 * E), jnp.bfloat16),
            ],
        ),
        out_shape=jax.ShapeDtypeStruct((H, SLOTS, E), jnp.bfloat16),
        compiler_params=pltpu.CompilerParams(vmem_limit_bytes=VMEM_LIMIT),
        cost_estimate=pl.CostEstimate(flops=8 << 30, bytes_accessed=14 << 20, transcendentals=0),
        name="spectral_pass",
    )(band, moved, legendre, gain, mixing, swap)


def inverse_kernel(spatial_ref, x_ref, table_ref, out_ref):
    for j in range(x_ref.shape[0]):
        spatial = spatial_ref[:, j].reshape(BANDS * SLOTS, E)
        sums = jnp.dot(table_ref[...], spatial, preferred_element_type=jnp.float32)
        out_ref[j] = (x_ref[j].astype(jnp.float32) + jax.nn.gelu(sums)).astype(jnp.bfloat16)


def inverse_transform(spatial, x, table, step, flops):
    rows = x.shape[0]
    groups, _, size, _ = spatial.shape
    return pl.pallas_call(
        inverse_kernel,
        grid=(rows // step,),
        in_specs=[
            pl.BlockSpec((groups, step, size, E), lambda j: (0, j, 0, 0)),
            pl.BlockSpec((step, W, E), lambda j: (j, 0, 0)),
            pl.BlockSpec((W, BANDS * SLOTS), lambda j: (0, 0)),
        ],
        out_specs=pl.BlockSpec((step, W, E), lambda j: (j, 0, 0)),
        out_shape=jax.ShapeDtypeStruct((rows, W, E), jnp.bfloat16),
        compiler_params=pltpu.CompilerParams(vmem_limit_bytes=VMEM_LIMIT),
        cost_estimate=pl.CostEstimate(
            flops=flops, bytes_accessed=rows << 20, transcendentals=rows * W * E
        ),
        name="inverse_transform",
    )(spatial, x, table)


def difference_of(share, own, control):
    return jnp.where(share > 0.0, own.astype(jnp.float32) - control, 0.0)


def spread_kernel(weights_ref, share_ref, own_ref, control_ref, out_ref, total):
    step = pl.program_id(0)
    partial = 0.0
    for j in range(STEP):
        difference = difference_of(share_ref[0], own_ref[j], control_ref[j].astype(jnp.float32))
        squares = jnp.sum((difference * difference).reshape(W // 8, 8, E), axis=0)
        partial = partial + squares * weights_ref[step * STEP + j]

    @pl.when(step == 0)
    def _():
        total[...] = partial

    @pl.when(step > 0)
    def _():
        total[...] += partial

    @pl.when(step == ROWS // STEP - 1)
    def _():
        lanes = total[:, :128] + total[:, 128:256] + total[:, 256:]
        out_ref[...] = jnp.broadcast_to(lanes[None], out_ref.shape)


def spread_sums(weights, share, own, control):
    row = pl.BlockSpec((STEP, W, E), lambda j: (j, 0, 0))
    scalars = pl.BlockSpec(memory_space=pltpu.SMEM)
    return pl.pallas_call(
        spread_kernel,
        grid=(ROWS // STEP,),
        in_specs=[scalars, scalars, row, row],
        out_specs=pl.BlockSpec((BANDS, 8, 128), lambda j: (0, 0, 0)),
        out_shape=jax.ShapeDtypeStruct((BANDS, 8, 128), jnp.float32),
        scratch_shapes=[pltpu.VMEM((8, E), jnp.float32)],
        compiler_params=pltpu.CompilerParams(vmem_limit_bytes=VMEM_LIMIT),
        cost_estimate=pl.CostEstimate(flops=9 << 20, bytes_accessed=11 << 20, transcendentals=0),
        name="spread_sums",
    )(weights, share, own, control)


def rescale_kernel(share_ref, target_ref, sums_ref, own_ref, control_ref, out_ref):
    total = jnp.sum(jnp.sum(sums_ref[...], axis=0), axis=(0, 1), keepdims=True)
    scale = target_ref[0] / jnp.sqrt(total * (1.0 / TOTAL_WEIGHT) + 1e-06)
    for j in range(STEP):
        control = control_ref[j].astype(jnp.float32)
        difference = difference_of(share_ref[0], own_ref[j], control)
        out_ref[j] = (control + scale * difference).astype(jnp.bfloat16)


def rescaled(share, target, sums, own, control):
    row = pl.BlockSpec((STEP, W, E), lambda j: (j, 0, 0))
    scalars = pl.BlockSpec(memory_space=pltpu.SMEM)
    return pl.pallas_call(
        rescale_kernel,
        grid=(ROWS // STEP,),
        in_specs=[
            scalars,
            scalars,
            pl.BlockSpec((BANDS, 8, 128), lambda j: (0, 0, 0)),
            row,
            row,
        ],
        out_specs=row,
        out_shape=jax.ShapeDtypeStruct((ROWS, W, E), jnp.bfloat16),
        compiler_params=pltpu.CompilerParams(vmem_limit_bytes=VMEM_LIMIT),
        cost_estimate=pl.CostEstimate(flops=9 << 20, bytes_accessed=17 << 20, transcendentals=0),
        name="rescaled",
    )(share, target, sums, own, control)


def scattered(pieces):
    member = lax.axis_index("member")
    kept = pieces[0]
    for z in range(1, DEPTH):
        arrived = lax.ppermute(pieces[z], "member", [(0, 2 * z)])
        kept = jnp.where(member == 2 * z, arrived, kept)
    return kept


def doubled_along_z(value):
    z = lax.axis_index("member") // 2
    for stride in (4, 2, 1):
        pairs = [(2 * a, 2 * (a + stride)) for a in range(0, DEPTH, 2 * stride)]
        arrived = lax.ppermute(value, "member", pairs)
        value = jnp.where(z % (2 * stride) == stride, arrived, value)
    return value


def exchanged_along_z(pieces):
    return lax.all_to_all(
        pieces, "member", split_axis=0, concat_axis=0, axis_index_groups=RINGS, tiled=True
    )


def across(value):
    arrived = lax.ppermute(value, "member", [(2 * z, 2 * z + 1) for z in range(DEPTH)])
    return jnp.where(lax.axis_index("member") % 2 == 1, arrived, value)


def shards(
    copy_fields,
    norm_gain,
    mix_real,
    mix_imag,
    filter_bank,
    perturbation_draw_numbers,
    amplitudes,
    desired_magnitude_slot,
):
    band_index = lax.axis_index("band")
    ahead_np, back_np, shared_ahead_np, shared_back_np = slot_tables()
    legendre_np = legendre_table(L, M, H).reshape(OWN, BANDS, L, H).transpose(1, 0, 2, 3)
    x = jnp.transpose(copy_fields[0], (0, 2, 1))

    global_rows = band_index * ROWS + jnp.arange(ROWS, dtype=jnp.int32)
    weights = jnp.sin((global_rows.astype(jnp.float32) + 0.5) * (math.pi / H)) * (math.pi / H)
    bank_rows = filter_bank.shape[0]
    draw_onehot = (jnp.arange(bank_rows, dtype=jnp.int32) == perturbation_draw_numbers[0]).astype(
        jnp.float32
    )
    degree_gain = jnp.sum(draw_onehot[:, None] * filter_bank, axis=0)

    legendre = rounded(legendre_np)
    gain = degree_gain[:, None]
    member = lax.axis_index("member")
    place = jnp.stack([band_index, member // 2])
    share = jnp.where(member > 0, 1.0, 0.0)[None]

    mixing = jnp.concatenate(
        [jnp.concatenate([mix_real, mix_imag], 1), jnp.concatenate([-mix_imag, mix_real], 1)], 0
    )
    z = member // 2

    fourier = forward_transform(x, norm_gain[None, :], weights, rounded(ahead_np), BANDS, STEP, 1 << 37)
    moved = lax.all_to_all(fourier, "band", split_axis=0, concat_axis=0, tiled=True)

    control_x = across(
        scattered(
            [x[2 * a : 2 * a + 2] for a in range(DEPTH - 1)]
            + [jnp.concatenate([x[ROWS - 1 :]] * 2)]
        )
    )
    control_gain = across(doubled_along_z(degree_gain[None, :]))
    control_weights = lax.dynamic_slice(jnp.pad(weights, (0, 1)), (2 * z,), (2,))
    control_fourier = forward_transform(
        control_x, norm_gain[None, :], control_weights, rounded(shared_ahead_np), DEPTH, 2, 1 << 29
    )
    moved, control_fourier = lax.optimization_barrier((moved, control_fourier))
    control_fourier = exchanged_along_z(control_fourier).reshape(DEPTH, 2, BANDS, 4, E)
    control_fourier = control_fourier.transpose(2, 0, 1, 3, 4).reshape(BANDS, 16, 4, E)[:, :ROWS]
    control_moved = lax.all_to_all(control_fourier, "band", split_axis=0, concat_axis=0, tiled=True)
    returned = spectral_pass(
        band_index[None],
        moved.reshape(H, SLOTS, E),
        legendre,
        gain,
        mixing,
        rounded(exchange_matrix()),
    )
    control_spatial = shared_spectral_pass(
        place,
        control_moved.reshape(H, 4, E).transpose(1, 0, 2),
        legendre,
        control_gain.reshape(L, 1),
        mixing,
    )
    control_spatial = lax.all_to_all(
        control_spatial.transpose(1, 0, 2).reshape(BANDS, ROWS, 4, E),
        "band",
        split_axis=0,
        concat_axis=0,
        tiled=True,
    )
    control_spatial = jnp.pad(control_spatial, ((0, 0), (0, 1), (0, 0), (0, 0)))
    control_spatial = control_spatial.reshape(BANDS, DEPTH, 2, 4, E).transpose(1, 2, 0, 3, 4)
    control_spatial = exchanged_along_z(control_spatial.reshape(DEPTH, 2, BANDS * 4, E))
    control_spatial, returned = lax.optimization_barrier((control_spatial, returned))
    spatial = lax.all_to_all(
        returned.reshape(BANDS, ROWS, SLOTS, E), "band", split_axis=0, concat_axis=0, tiled=True
    )
    control = inverse_transform(control_spatial, control_x, rounded(shared_back_np), 2, 1 << 29)
    control = lax.all_gather(control, "member", tiled=True, axis_index_groups=RINGS)

    forecast = inverse_transform(spatial, x, rounded(back_np), STEP, 1 << 38)
    sums = lax.all_to_all(
        spread_sums(weights, share, forecast, control),
        "band",
        split_axis=0,
        concat_axis=0,
        tiled=True,
    )
    target = jnp.sum(
        jnp.where(
            jnp.arange(amplitudes.shape[0], dtype=jnp.int32) == desired_magnitude_slot[0],
            amplitudes,
            0.0,
        )
    )
    bred = rescaled(share, target[None], sums, forecast, control)
    return jnp.transpose(bred, (0, 2, 1))[None]


def solution(mesh):
    in_specs = (P("member", "band", None, None), P(), P(), P(), P(), P("member"), P(), P("member"))
    out_specs = P("member", "band", None, None)
    return jax.shard_map(shards, mesh=mesh, in_specs=in_specs, out_specs=out_specs, check_vma=False)
```

```python
import functools
import math

import jax
import jax.numpy as jnp
import numpy as np
from jax import lax
from jax.experimental import pallas as pl
from jax.experimental.pallas import tpu as pltpu
from jax.sharding import PartitionSpec as P

H = 240
W = 480
M = 240
L = 240
E = 384
BANDS = 16
ROWS = H // BANDS
OWN = M // BANDS
SLOTS = 32
DEPTH = 8
RINGS = [[2 * z + h for z in range(DEPTH)] for h in range(2)]
STEP = 3
TOTAL_WEIGHT = float(np.sum(np.sin((np.arange(H) + 0.5) * np.pi / H)) * np.pi / H * E * W)
VMEM_LIMIT = 58 * 1024 * 1024


def legendre_table(degree_count, order_count, lat_count):
    colatitude = (np.arange(lat_count) + 0.5) * np.pi / lat_count
    cosines = np.cos(colatitude)
    sines = np.sin(colatitude)
    orders = np.arange(order_count)[:, None] * 1.0
    steps_up = np.arange(1, order_count) * 1.0
    log_factor = np.concatenate(
        [[0.0], np.cumsum(np.log((2.0 * steps_up - 1.0) / (2.0 * steps_up)))]
    )
    diagonal_start = np.exp(
        0.5 * np.log((2.0 * orders + 1.0) / 2.0)
        + 0.5 * log_factor[:, None]
        + orders * np.log(sines)[None, :]
    )
    result = np.zeros((order_count, degree_count, lat_count))
    previous = np.zeros(diagonal_start.shape)
    before_previous = np.zeros(diagonal_start.shape)
    for degree in range(degree_count):
        lower = degree - 1.0
        rising = np.sqrt(
            np.maximum(4.0 * degree * degree - 1.0, 1.0)
            / np.maximum(degree * degree - orders * orders, 1.0)
        )
        falling = np.sqrt(
            np.maximum(lower * lower - orders * orders, 0.0) / max(4.0 * lower * lower - 1.0, 1.0)
        )
        current = np.where(
            orders == degree,
            diagonal_start,
            np.where(
                degree > orders,
                rising * (cosines[None, :] * previous - falling * before_previous),
                0.0,
            ),
        )
        result[:, degree] = current
        before_previous = previous
        previous = current
    return result


def fourier_tables(lon_count, mode_order):
    longitude = 2.0 * np.pi * np.arange(lon_count)[:, None] / lon_count
    angles = longitude * (mode_order[None, :] * 1.0)
    forward_factor = math.sqrt(2.0 * math.pi) / lon_count
    forward_table = np.stack(
        [forward_factor * np.cos(angles), -forward_factor * np.sin(angles)], axis=1
    )
    inverse_factor = np.where(mode_order == 0, 1.0, 2.0) / math.sqrt(2.0 * math.pi)
    inverse_table = np.stack(
        [
            (inverse_factor[None, :] * np.cos(angles)).T,
            (-inverse_factor[None, :] * np.sin(angles)).T,
        ],
        axis=0,
    )
    return (forward_table, inverse_table)


def slot_tables():
    forward, inverse = fourier_tables(W, np.arange(M))
    ahead = np.zeros((W, 2, 16, BANDS))
    back = np.zeros((2, 16, BANDS, W))
    ahead[:, :, :OWN] = forward.reshape(W, 2, OWN, BANDS)
    back[:, :OWN] = inverse.reshape(2, OWN, BANDS, W)
    ahead = ahead.reshape(W, 2, DEPTH, 2, BANDS)
    back = back.reshape(2, DEPTH, 2, BANDS, W)
    rows = BANDS * SLOTS
    return (
        ahead.transpose(4, 2, 1, 3, 0).reshape(rows, W),
        back.transpose(3, 1, 0, 2, 4).reshape(rows, W).T,
        ahead.transpose(2, 4, 1, 3, 0).reshape(rows, W),
        back.transpose(1, 3, 0, 2, 4).reshape(rows, W).T,
    )


def rounded(table):
    return jnp.asarray(table, jnp.float32).astype(jnp.bfloat16)


def exchange_matrix():
    matrix = np.zeros((256, 256))
    for a in range(16):
        for b in range(16):
            matrix[b * 16 + a, a * 16 + b] = 1.0
    return matrix


def forward_kernel(weights_ref, x_ref, gain_ref, table_ref, out_ref):
    rows = x_ref.shape[0]
    for j in range(rows):
        x = x_ref[j].astype(jnp.float32)
        centred = x - jnp.mean(x, axis=1, keepdims=True)
        variance = jnp.mean(jnp.square(centred), axis=1, keepdims=True)
        normed = (centred * lax.rsqrt(variance + 1e-05) * gain_ref[...]).astype(jnp.bfloat16)
        sums = jnp.dot(table_ref[...], normed, preferred_element_type=jnp.float32)
        sums = (sums * weights_ref[pl.program_id(0) * rows + j]).astype(jnp.bfloat16)
        out_ref[:, j] = sums.reshape(out_ref.shape[0], out_ref.shape[2], E)


def forward_transform(x, gain, weights, table, groups, step, flops):
    rows = x.shape[0]
    size = BANDS * SLOTS // groups
    return pl.pallas_call(
        forward_kernel,
        grid=(rows // step,),
        in_specs=[
            pl.BlockSpec(memory_space=pltpu.SMEM),
            pl.BlockSpec((step, W, E), lambda j: (j, 0, 0)),
            pl.BlockSpec((1, E), lambda j: (0, 0)),
            pl.BlockSpec((BANDS * SLOTS, W), lambda j: (0, 0)),
        ],
        out_specs=pl.BlockSpec((groups, step, size, E), lambda j: (0, j, 0, 0)),
        out_shape=jax.ShapeDtypeStruct((groups, rows, size, E), jnp.bfloat16),
        compiler_params=pltpu.CompilerParams(vmem_limit_bytes=VMEM_LIMIT),
        cost_estimate=pl.CostEstimate(flops=flops, bytes_accessed=rows << 20, transcendentals=0),
        name="forward_transform",
    )(weights, x, gain, table)


def mix_degrees(table, values, gain, mixing):
    coeffs = jnp.dot(table, values, preferred_element_type=jnp.float32).astype(jnp.bfloat16)
    return (jnp.dot(coeffs, mixing, preferred_element_type=jnp.float32) * gain).astype(jnp.bfloat16)


def to_latitudes(table, mixed):
    return lax.dot_general(
        table, mixed, (((0,), (0,)), ((), ())), preferred_element_type=jnp.float32
    ).astype(jnp.bfloat16)


def shared_spectral_kernel(
    place_ref, re_ref, im_ref, legendre_ref, gain_ref, mixing_ref, out_re_ref, out_im_ref
):
    table = legendre_ref[0, 0]
    values = jnp.concatenate([re_ref[0], im_ref[0]], axis=1)
    spatial = to_latitudes(table, mix_degrees(table, values, gain_ref[...], mixing_ref[...]))
    out_re_ref[0] = spatial[:, :E]
    out_im_ref[0] = spatial[:, E:]


def shared_spectral_pass(place, moved, legendre, gain, mixing):
    row = lambda first: pl.BlockSpec((1, H, E), lambda o, place: (first + o, 0, 0))
    whole = lambda *shape: pl.BlockSpec(shape, lambda o, place: (0,) * len(shape))
    pair = jax.ShapeDtypeStruct((2, H, E), jnp.bfloat16)
    out_re, out_im = pl.pallas_call(
        shared_spectral_kernel,
        grid_spec=pltpu.PrefetchScalarGridSpec(
            num_scalar_prefetch=1,
            grid=(2,),
            in_specs=[
                row(0),
                row(2),
                pl.BlockSpec(
                    (1, 1, L, H),
                    lambda o, place: (place[0], jnp.minimum(2 * place[1] + o, OWN - 1), 0, 0),
                ),
                whole(L, 1),
                whole(2 * E, 2 * E),
            ],
            out_specs=[row(0), row(0)],
        ),
        out_shape=[pair, pair],
        compiler_params=pltpu.CompilerParams(vmem_limit_bytes=VMEM_LIMIT),
        cost_estimate=pl.CostEstimate(flops=1 << 30, bytes_accessed=4 << 20, transcendentals=0),
        name="shared_spectral_pass",
    )(place, moved, moved, legendre, gain, mixing)
    return jnp.concatenate([out_re, out_im], axis=0)


def spectral_kernel(
    band_ref, moved_ref, legendre_ref, gain_ref, mixing_ref, swap_ref, out_ref, by_mode, mixed
):
    swap = swap_ref[...]
    halves = [(half, lanes) for half, lanes in ((0, slice(0, E)), (16, slice(E, 2 * E)))]
    unroll = 3

    def place_of(slot):
        z, part, o = slot // 4, (slot // 2) % 2, slot % 2
        return 2 * z + o, slice(part * E, part * E + E)

    def to_modes(step, carry):
        for piece in range(unroll):
            rows = pl.ds(pl.multiple_of((step * unroll + piece) * 16, 16), 16)
            block = jnp.concatenate(
                [moved_ref[rows, half : half + 16, :].reshape(256, E) for half, _ in halves], axis=1
            )
            turned = jnp.dot(swap, block, preferred_element_type=jnp.float32).astype(jnp.bfloat16)
            turned = turned.reshape(16, 16, 2 * E)
            for half, lanes in halves:
                for k in range(16):
                    i, part = place_of(half + k)
                    by_mode[i, rows, part] = turned[k, :, lanes]
        return carry

    lax.fori_loop(0, H // 16 // unroll, to_modes, 0)
    mixing = mixing_ref[...]
    for i in range(OWN):
        low = 16 * i
        table = legendre_ref[0, i]
        mixed[low:, :] = mix_degrees(table[low:], by_mode[i], gain_ref[low:], mixing)
        by_mode[i] = to_latitudes(table, mixed[...])

    def to_rows(step, carry):
        for piece in range(unroll):
            rows = pl.ds(pl.multiple_of((step * unroll + piece) * 16, 16), 16)
            blocks = []
            for half, _ in halves:
                slots = []
                for k in range(16):
                    i, part = place_of(half + k)
                    slots.append(by_mode[i, rows, part])
                blocks.append(jnp.concatenate(slots, axis=0))
            block = jnp.concatenate(blocks, axis=1)
            turned = jnp.dot(swap, block, preferred_element_type=jnp.float32).astype(jnp.bfloat16)
            turned = turned.reshape(16, 16, 2 * E)
            for half, lanes in halves:
                out_ref[rows, half : half + 16, :] = turned[:, :, lanes]
        return carry

    lax.fori_loop(0, H // 16 // unroll, to_rows, 0)


def spectral_pass(band, moved, legendre, gain, mixing, swap):
    whole = lambda *shape: pl.BlockSpec(shape, lambda step, band: (0,) * len(shape))
    return pl.pallas_call(
        spectral_kernel,
        grid_spec=pltpu.PrefetchScalarGridSpec(
            num_scalar_prefetch=1,
            grid=(1,),
            in_specs=[
                whole(H, SLOTS, E),
                pl.BlockSpec((1, OWN, L, H), lambda step, band: (band[0], 0, 0, 0)),
                whole(L, 1),
                whole(2 * E, 2 * E),
                whole(256, 256),
            ],
            out_specs=whole(H, SLOTS, E),
            scratch_shapes=[
                pltpu.VMEM((16, H, 2 * E), jnp.bfloat16),
                pltpu.VMEM((L, 2 * E), jnp.bfloat16),
            ],
        ),
        out_shape=jax.ShapeDtypeStruct((H, SLOTS, E), jnp.bfloat16),
        compiler_params=pltpu.CompilerParams(vmem_limit_bytes=VMEM_LIMIT),
        cost_estimate=pl.CostEstimate(flops=8 << 30, bytes_accessed=14 << 20, transcendentals=0),
        name="spectral_pass",
    )(band, moved, legendre, gain, mixing, swap)


def inverse_kernel(spatial_ref, x_ref, table_ref, out_ref):
    for j in range(x_ref.shape[0]):
        spatial = spatial_ref[:, j].reshape(BANDS * SLOTS, E)
        sums = jnp.dot(table_ref[...], spatial, preferred_element_type=jnp.float32)
        out_ref[j] = (x_ref[j].astype(jnp.float32) + jax.nn.gelu(sums)).astype(jnp.bfloat16)


def inverse_transform(spatial, x, table, step, flops):
    rows = x.shape[0]
    groups, _, size, _ = spatial.shape
    return pl.pallas_call(
        inverse_kernel,
        grid=(rows // step,),
        in_specs=[
            pl.BlockSpec((groups, step, size, E), lambda j: (0, j, 0, 0)),
            pl.BlockSpec((step, W, E), lambda j: (j, 0, 0)),
            pl.BlockSpec((W, BANDS * SLOTS), lambda j: (0, 0)),
        ],
        out_specs=pl.BlockSpec((step, W, E), lambda j: (j, 0, 0)),
        out_shape=jax.ShapeDtypeStruct((rows, W, E), jnp.bfloat16),
        compiler_params=pltpu.CompilerParams(vmem_limit_bytes=VMEM_LIMIT),
        cost_estimate=pl.CostEstimate(
            flops=flops, bytes_accessed=rows << 20, transcendentals=rows * W * E
        ),
        name="inverse_transform",
    )(spatial, x, table)


def spread_kernel(weights_ref, own_ref, control_ref, out_ref, total):
    step = pl.program_id(0)
    partial = 0.0
    for j in range(STEP):
        difference = own_ref[j].astype(jnp.float32) - control_ref[j].astype(jnp.float32)
        squares = jnp.sum((difference * difference).reshape(W // 8, 8, E), axis=0)
        partial = partial + squares * weights_ref[step * STEP + j]

    @pl.when(step == 0)
    def _():
        total[...] = partial

    @pl.when(step > 0)
    def _():
        total[...] += partial

    @pl.when(step == ROWS // STEP - 1)
    def _():
        lanes = total[:, :128] + total[:, 128:256] + total[:, 256:]
        out_ref[...] = jnp.broadcast_to(lanes[None], out_ref.shape)


def spread_sums(weights, own, control):
    row = pl.BlockSpec((STEP, W, E), lambda j: (j, 0, 0))
    scalars = pl.BlockSpec(memory_space=pltpu.SMEM)
    return pl.pallas_call(
        spread_kernel,
        grid=(ROWS // STEP,),
        in_specs=[scalars, row, row],
        out_specs=pl.BlockSpec((BANDS, 8, 128), lambda j: (0, 0, 0)),
        out_shape=jax.ShapeDtypeStruct((BANDS, 8, 128), jnp.float32),
        scratch_shapes=[pltpu.VMEM((8, E), jnp.float32)],
        compiler_params=pltpu.CompilerParams(vmem_limit_bytes=VMEM_LIMIT),
        cost_estimate=pl.CostEstimate(flops=9 << 20, bytes_accessed=11 << 20, transcendentals=0),
        name="spread_sums",
    )(weights, own, control)


def rescale_kernel(target_ref, sums_ref, own_ref, control_ref, out_ref):
    total = jnp.sum(jnp.sum(sums_ref[...], axis=0), axis=(0, 1), keepdims=True)
    scale = target_ref[0] / jnp.sqrt(total * (1.0 / TOTAL_WEIGHT) + 1e-06)
    for j in range(STEP):
        control = control_ref[j].astype(jnp.float32)
        difference = own_ref[j].astype(jnp.float32) - control
        out_ref[j] = (control + scale * difference).astype(jnp.bfloat16)


def rescaled(target, sums, own, control):
    row = pl.BlockSpec((STEP, W, E), lambda j: (j, 0, 0))
    scalars = pl.BlockSpec(memory_space=pltpu.SMEM)
    return pl.pallas_call(
        rescale_kernel,
        grid=(ROWS // STEP,),
        in_specs=[
            scalars,
            pl.BlockSpec((BANDS, 8, 128), lambda j: (0, 0, 0)),
            row,
            row,
        ],
        out_specs=row,
        out_shape=jax.ShapeDtypeStruct((ROWS, W, E), jnp.bfloat16),
        compiler_params=pltpu.CompilerParams(vmem_limit_bytes=VMEM_LIMIT),
        cost_estimate=pl.CostEstimate(flops=9 << 20, bytes_accessed=17 << 20, transcendentals=0),
        name="rescaled",
    )(target, sums, own, control)


def in_three(value):
    parts = []
    for _ in range(3):
        parts.append(lax.reduce_precision(value, exponent_bits=8, mantissa_bits=7))
        value = value - parts[-1]
    return jnp.stack(parts).astype(jnp.bfloat16)


def scattered(field, extra):
    member = lax.axis_index("member")
    kept = jnp.concatenate([field[:2].reshape(2 * W, E), extra])
    for z in range(1, DEPTH):
        piece = field[2 * z : min(2 * z + 2, ROWS)].reshape(-1, E)
        arrived = lax.ppermute(jnp.concatenate([piece, extra]), "member", [(0, 2 * z)])
        if 2 * z + 1 == ROWS:
            arrived = jnp.concatenate([arrived[:W], arrived])
        kept = jnp.where(member == 2 * z, arrived, kept)
    return kept


def exchanged_along_z(pieces):
    return lax.all_to_all(
        pieces, "member", split_axis=0, concat_axis=0, axis_index_groups=RINGS, tiled=True
    )


def across(value):
    arrived = lax.ppermute(value, "member", [(2 * z, 2 * z + 1) for z in range(DEPTH)])
    return jnp.where(lax.axis_index("member") % 2 == 1, arrived, value)


def shards(
    copy_fields,
    norm_gain,
    mix_real,
    mix_imag,
    filter_bank,
    perturbation_draw_numbers,
    amplitudes,
    desired_magnitude_slot,
):
    band_index = lax.axis_index("band")
    ahead_np, back_np, shared_ahead_np, shared_back_np = slot_tables()
    legendre_np = legendre_table(L, M, H).reshape(OWN, BANDS, L, H).transpose(1, 0, 2, 3)
    x = jnp.transpose(copy_fields[0], (0, 2, 1))

    global_rows = band_index * ROWS + jnp.arange(ROWS, dtype=jnp.int32)
    weights = jnp.sin((global_rows.astype(jnp.float32) + 0.5) * (math.pi / H)) * (math.pi / H)
    bank_rows = filter_bank.shape[0]
    draw_onehot = (jnp.arange(bank_rows, dtype=jnp.int32) == perturbation_draw_numbers[0]).astype(
        jnp.float32
    )
    degree_gain = jnp.sum(draw_onehot[:, None] * filter_bank, axis=0)

    legendre = rounded(legendre_np)
    gain = degree_gain[:, None]
    member = lax.axis_index("member")
    place = jnp.stack([band_index, member // 2])

    mixing = jnp.concatenate(
        [jnp.concatenate([mix_real, mix_imag], 1), jnp.concatenate([-mix_imag, mix_real], 1)], 0
    )
    z = member // 2

    fourier = forward_transform(x, norm_gain[None, :], weights, rounded(ahead_np), BANDS, STEP, 1 << 37)
    moved = lax.all_to_all(fourier, "band", split_axis=0, concat_axis=0, tiled=True)

    control_parts = across(
        scattered(x, jnp.pad(in_three(degree_gain), ((0, 16 - 3), (0, E - L))))
    )
    control_x = control_parts[: 2 * W].reshape(2, W, E)
    control_gain = jnp.sum(control_parts[2 * W : 2 * W + 3, :L].astype(jnp.float32), axis=0)
    control_weights = lax.dynamic_slice(jnp.pad(weights, (0, 1)), (2 * z,), (2,))
    control_fourier = forward_transform(
        control_x, norm_gain[None, :], control_weights, rounded(shared_ahead_np), DEPTH, 2, 32 << 30
    )
    moved, control_fourier = lax.optimization_barrier((moved, control_fourier))
    control_fourier = exchanged_along_z(control_fourier).reshape(DEPTH, 2, BANDS, 4, E)
    control_fourier = control_fourier.transpose(2, 0, 1, 3, 4).reshape(BANDS, 16, 4, E)[:, :ROWS]
    returned = spectral_pass(
        band_index[None],
        moved.reshape(H, SLOTS, E),
        legendre,
        gain,
        mixing,
        rounded(exchange_matrix()),
    )
    returned, control_fourier = lax.optimization_barrier((returned, control_fourier))
    control_moved = lax.all_to_all(control_fourier, "band", split_axis=0, concat_axis=0, tiled=True)
    control_spatial = shared_spectral_pass(
        place,
        control_moved.reshape(H, 4, E).transpose(1, 0, 2),
        legendre,
        control_gain.reshape(L, 1),
        mixing,
    )
    control_spatial = lax.all_to_all(
        control_spatial.transpose(1, 0, 2).reshape(BANDS, ROWS, 4, E),
        "band",
        split_axis=0,
        concat_axis=0,
        tiled=True,
    )
    control_spatial = jnp.pad(control_spatial, ((0, 0), (0, 1), (0, 0), (0, 0)))
    control_spatial = control_spatial.reshape(BANDS, DEPTH, 2, 4, E).transpose(1, 2, 0, 3, 4)
    control_spatial = exchanged_along_z(control_spatial.reshape(DEPTH, 2, BANDS * 4, E))
    control_spatial, returned = lax.optimization_barrier((control_spatial, returned))
    spatial = lax.all_to_all(
        returned.reshape(BANDS, ROWS, SLOTS, E), "band", split_axis=0, concat_axis=0, tiled=True
    )
    control = inverse_transform(control_spatial, control_x, rounded(shared_back_np), 2, 1 << 29)
    control = lax.all_gather(control, "member", tiled=True, axis_index_groups=RINGS)

    forecast = inverse_transform(spatial, x, rounded(back_np), STEP, 1 << 38)
    sums = lax.all_to_all(
        spread_sums(weights, forecast, control),
        "band",
        split_axis=0,
        concat_axis=0,
        tiled=True,
    )
    target = jnp.sum(
        jnp.where(
            jnp.arange(amplitudes.shape[0], dtype=jnp.int32) == desired_magnitude_slot[0],
            amplitudes,
            0.0,
        )
    )
    bred = rescaled(jnp.where(member > 0, target, 0.0)[None], sums, forecast, control)
    return jnp.transpose(bred, (0, 2, 1))[None]


def solution(mesh):
    in_specs = (P("member", "band", None, None), P(), P(), P(), P(), P("member"), P(), P("member"))
    out_specs = P("member", "band", None, None)
    return jax.shard_map(shards, mesh=mesh, in_specs=in_specs, out_specs=out_specs, check_vma=False)
```

```python
import functools
import math

import jax
import jax.numpy as jnp
import numpy as np
from jax import lax
from jax.experimental import pallas as pl
from jax.experimental.pallas import tpu as pltpu
from jax.sharding import PartitionSpec as P

H = 240
W = 480
M = 240
L = 240
E = 384
BANDS = 16
ROWS = H // BANDS
OWN = M // BANDS
SLOTS = 32
DEPTH = 8
RINGS = [[2 * z + h for z in range(DEPTH)] for h in range(2)]
STEP = 3
TOTAL_WEIGHT = float(np.sum(np.sin((np.arange(H) + 0.5) * np.pi / H)) * np.pi / H * E * W)
MIB = 1 << 20


def legendre_table(degree_count, order_count, lat_count):
    colatitude = (np.arange(lat_count) + 0.5) * np.pi / lat_count
    cosines = np.cos(colatitude)
    sines = np.sin(colatitude)
    orders = np.arange(order_count)[:, None] * 1.0
    steps_up = np.arange(1, order_count) * 1.0
    log_factor = np.concatenate(
        [[0.0], np.cumsum(np.log((2.0 * steps_up - 1.0) / (2.0 * steps_up)))]
    )
    diagonal_start = np.exp(
        0.5 * np.log((2.0 * orders + 1.0) / 2.0)
        + 0.5 * log_factor[:, None]
        + orders * np.log(sines)[None, :]
    )
    result = np.zeros((order_count, degree_count, lat_count))
    previous = np.zeros(diagonal_start.shape)
    before_previous = np.zeros(diagonal_start.shape)
    for degree in range(degree_count):
        lower = degree - 1.0
        rising = np.sqrt(
            np.maximum(4.0 * degree * degree - 1.0, 1.0)
            / np.maximum(degree * degree - orders * orders, 1.0)
        )
        falling = np.sqrt(
            np.maximum(lower * lower - orders * orders, 0.0) / max(4.0 * lower * lower - 1.0, 1.0)
        )
        current = np.where(
            orders == degree,
            diagonal_start,
            np.where(
                degree > orders,
                rising * (cosines[None, :] * previous - falling * before_previous),
                0.0,
            ),
        )
        result[:, degree] = current
        before_previous = previous
        previous = current
    return result


def fourier_tables(lon_count, mode_order):
    longitude = 2.0 * np.pi * np.arange(lon_count)[:, None] / lon_count
    angles = longitude * (mode_order[None, :] * 1.0)
    forward_factor = math.sqrt(2.0 * math.pi) / lon_count
    forward_table = np.stack(
        [forward_factor * np.cos(angles), -forward_factor * np.sin(angles)], axis=1
    )
    inverse_factor = np.where(mode_order == 0, 1.0, 2.0) / math.sqrt(2.0 * math.pi)
    inverse_table = np.stack(
        [
            (inverse_factor[None, :] * np.cos(angles)).T,
            (-inverse_factor[None, :] * np.sin(angles)).T,
        ],
        axis=0,
    )
    return (forward_table, inverse_table)


def slot_tables():
    forward, inverse = fourier_tables(W, np.arange(M))
    ahead = np.zeros((W, 2, 16, BANDS))
    back = np.zeros((2, 16, BANDS, W))
    ahead[:, :, :OWN] = forward.reshape(W, 2, OWN, BANDS)
    back[:, :OWN] = inverse.reshape(2, OWN, BANDS, W)
    ahead = ahead.reshape(W, 2, DEPTH, 2, BANDS)
    back = back.reshape(2, DEPTH, 2, BANDS, W)
    rows = BANDS * SLOTS
    return (
        ahead.transpose(4, 2, 1, 3, 0).reshape(rows, W),
        back.transpose(3, 1, 0, 2, 4).reshape(rows, W).T,
        ahead.transpose(2, 4, 1, 3, 0).reshape(rows, W),
        back.transpose(1, 3, 0, 2, 4).reshape(rows, W).T,
    )


def rounded(table):
    return jnp.asarray(table, jnp.float32).astype(jnp.bfloat16)


def exchange_matrix():
    matrix = np.zeros((256, 256))
    for a in range(16):
        for b in range(16):
            matrix[b * 16 + a, a * 16 + b] = 1.0
    return matrix


def forward_kernel(weights_ref, x_ref, gain_ref, table_ref, out_ref):
    rows = x_ref.shape[0]
    for j in range(rows):
        x = x_ref[j].astype(jnp.float32)
        centred = x - jnp.mean(x, axis=1, keepdims=True)
        variance = jnp.mean(jnp.square(centred), axis=1, keepdims=True)
        normed = (centred * lax.rsqrt(variance + 1e-05) * gain_ref[...]).astype(jnp.bfloat16)
        sums = jnp.dot(table_ref[...], normed, preferred_element_type=jnp.float32)
        sums = (sums * weights_ref[pl.program_id(0) * rows + j]).astype(jnp.bfloat16)
        out_ref[:, j] = sums.reshape(out_ref.shape[0], out_ref.shape[2], E)


def forward_transform(x, gain, weights, table, groups, step, flops):
    rows = x.shape[0]
    size = BANDS * SLOTS // groups
    return pl.pallas_call(
        forward_kernel,
        grid=(rows // step,),
        in_specs=[
            pl.BlockSpec(memory_space=pltpu.SMEM),
            pl.BlockSpec((step, W, E), lambda j: (j, 0, 0)),
            pl.BlockSpec((1, E), lambda j: (0, 0)),
            pl.BlockSpec((BANDS * SLOTS, W), lambda j: (0, 0)),
        ],
        out_specs=pl.BlockSpec((groups, step, size, E), lambda j: (0, j, 0, 0)),
        out_shape=jax.ShapeDtypeStruct((groups, rows, size, E), jnp.bfloat16),
        compiler_params=pltpu.CompilerParams(vmem_limit_bytes=58 * MIB),
        cost_estimate=pl.CostEstimate(flops=flops, bytes_accessed=rows << 20, transcendentals=0),
        name="forward_transform",
    )(weights, x, gain, table)


def mix_degrees(table, values, gain, mixing):
    coeffs = jnp.dot(table, values, preferred_element_type=jnp.float32).astype(jnp.bfloat16)
    return (jnp.dot(coeffs, mixing, preferred_element_type=jnp.float32) * gain).astype(jnp.bfloat16)


def to_latitudes(table, mixed):
    return lax.dot_general(
        table, mixed, (((0,), (0,)), ((), ())), preferred_element_type=jnp.float32
    ).astype(jnp.bfloat16)


def shared_spectral_kernel(
    place_ref, re_ref, im_ref, legendre_ref, gain_ref, mixing_ref, out_re_ref, out_im_ref
):
    table = legendre_ref[0, 0]
    values = jnp.concatenate([re_ref[0], im_ref[0]], axis=1)
    spatial = to_latitudes(table, mix_degrees(table, values, gain_ref[...], mixing_ref[...]))
    out_re_ref[0] = spatial[:, :E]
    out_im_ref[0] = spatial[:, E:]


def shared_spectral_pass(place, moved, legendre, gain, mixing):
    row = lambda first: pl.BlockSpec((1, H, E), lambda o, place: (first + o, 0, 0))
    whole = lambda *shape: pl.BlockSpec(shape, lambda o, place: (0,) * len(shape))
    pair = jax.ShapeDtypeStruct((2, H, E), jnp.bfloat16)
    out_re, out_im = pl.pallas_call(
        shared_spectral_kernel,
        grid_spec=pltpu.PrefetchScalarGridSpec(
            num_scalar_prefetch=1,
            grid=(2,),
            in_specs=[
                row(0),
                row(2),
                pl.BlockSpec(
                    (1, 1, L, H),
                    lambda o, place: (place[0], jnp.minimum(2 * place[1] + o, OWN - 1), 0, 0),
                ),
                whole(L, 1),
                whole(2 * E, 2 * E),
            ],
            out_specs=[row(0), row(0)],
        ),
        out_shape=[pair, pair],
        compiler_params=pltpu.CompilerParams(vmem_limit_bytes=16 * MIB),
        cost_estimate=pl.CostEstimate(flops=1 << 30, bytes_accessed=4 << 20, transcendentals=0),
        name="shared_spectral_pass",
    )(place, moved, moved, legendre, gain, mixing)
    return jnp.concatenate([out_re, out_im], axis=0)


def spectral_kernel(
    band_ref, moved_ref, legendre_ref, gain_ref, mixing_ref, swap_ref, out_ref, by_mode, mixed
):
    swap = swap_ref[...]
    halves = [(half, lanes) for half, lanes in ((0, slice(0, E)), (16, slice(E, 2 * E)))]
    unroll = 3

    def place_of(slot):
        z, part, o = slot // 4, (slot // 2) % 2, slot % 2
        return 2 * z + o, slice(part * E, part * E + E)

    def to_modes(step, carry):
        for piece in range(unroll):
            rows = pl.ds(pl.multiple_of((step * unroll + piece) * 16, 16), 16)
            block = jnp.concatenate(
                [moved_ref[rows, half : half + 16, :].reshape(256, E) for half, _ in halves], axis=1
            )
            turned = jnp.dot(swap, block, preferred_element_type=jnp.float32).astype(jnp.bfloat16)
            turned = turned.reshape(16, 16, 2 * E)
            for half, lanes in halves:
                for k in range(16):
                    i, part = place_of(half + k)
                    by_mode[i, rows, part] = turned[k, :, lanes]
        return carry

    lax.fori_loop(0, H // 16 // unroll, to_modes, 0)
    mixing = mixing_ref[...]
    for i in range(OWN):
        low = 16 * i
        table = legendre_ref[0, i]
        mixed[low:, :] = mix_degrees(table[low:], by_mode[i], gain_ref[low:], mixing)
        by_mode[i] = to_latitudes(table, mixed[...])

    def to_rows(step, carry):
        for piece in range(unroll):
            rows = pl.ds(pl.multiple_of((step * unroll + piece) * 16, 16), 16)
            blocks = []
            for half, _ in halves:
                slots = []
                for k in range(16):
                    i, part = place_of(half + k)
                    slots.append(by_mode[i, rows, part])
                blocks.append(jnp.concatenate(slots, axis=0))
            block = jnp.concatenate(blocks, axis=1)
            turned = jnp.dot(swap, block, preferred_element_type=jnp.float32).astype(jnp.bfloat16)
            turned = turned.reshape(16, 16, 2 * E)
            for half, lanes in halves:
                out_ref[rows, half : half + 16, :] = turned[:, :, lanes]
        return carry

    lax.fori_loop(0, H // 16 // unroll, to_rows, 0)


def spectral_pass(band, moved, legendre, gain, mixing, swap):
    whole = lambda *shape: pl.BlockSpec(shape, lambda step, band: (0,) * len(shape))
    return pl.pallas_call(
        spectral_kernel,
        grid_spec=pltpu.PrefetchScalarGridSpec(
            num_scalar_prefetch=1,
            grid=(1,),
            in_specs=[
                whole(H, SLOTS, E),
                pl.BlockSpec((1, OWN, L, H), lambda step, band: (band[0], 0, 0, 0)),
                whole(L, 1),
                whole(2 * E, 2 * E),
                whole(256, 256),
            ],
            out_specs=whole(H, SLOTS, E),
            scratch_shapes=[
                pltpu.VMEM((16, H, 2 * E), jnp.bfloat16),
                pltpu.VMEM((L, 2 * E), jnp.bfloat16),
            ],
        ),
        out_shape=jax.ShapeDtypeStruct((H, SLOTS, E), jnp.bfloat16),
        compiler_params=pltpu.CompilerParams(vmem_limit_bytes=58 * MIB),
        cost_estimate=pl.CostEstimate(flops=8 << 30, bytes_accessed=14 << 20, transcendentals=0),
        name="spectral_pass",
    )(band, moved, legendre, gain, mixing, swap)


def inverse_kernel(spatial_ref, x_ref, table_ref, out_ref):
    for j in range(x_ref.shape[0]):
        spatial = spatial_ref[:, j].reshape(BANDS * SLOTS, E)
        sums = jnp.dot(table_ref[...], spatial, preferred_element_type=jnp.float32)
        out_ref[j] = (x_ref[j].astype(jnp.float32) + jax.nn.gelu(sums)).astype(jnp.bfloat16)


def inverse_transform(spatial, x, table, step, flops):
    rows = x.shape[0]
    groups, _, size, _ = spatial.shape
    return pl.pallas_call(
        inverse_kernel,
        grid=(rows // step,),
        in_specs=[
            pl.BlockSpec((groups, step, size, E), lambda j: (0, j, 0, 0)),
            pl.BlockSpec((step, W, E), lambda j: (j, 0, 0)),
            pl.BlockSpec((W, BANDS * SLOTS), lambda j: (0, 0)),
        ],
        out_specs=pl.BlockSpec((step, W, E), lambda j: (j, 0, 0)),
        out_shape=jax.ShapeDtypeStruct((rows, W, E), jnp.bfloat16),
        compiler_params=pltpu.CompilerParams(vmem_limit_bytes=18 * MIB),
        cost_estimate=pl.CostEstimate(
            flops=flops, bytes_accessed=rows << 20, transcendentals=rows * W * E
        ),
        name="inverse_transform",
    )(spatial, x, table)


def spread_kernel(weights_ref, own_ref, control_ref, out_ref, total):
    step = pl.program_id(0)
    partial = 0.0
    for j in range(STEP):
        difference = own_ref[j].astype(jnp.float32) - control_ref[j].astype(jnp.float32)
        squares = jnp.sum((difference * difference).reshape(W // 8, 8, E), axis=0)
        partial = partial + squares * weights_ref[step * STEP + j]

    @pl.when(step == 0)
    def _():
        total[...] = partial

    @pl.when(step > 0)
    def _():
        total[...] += partial

    @pl.when(step == ROWS // STEP - 1)
    def _():
        lanes = total[:, :128] + total[:, 128:256] + total[:, 256:]
        out_ref[...] = jnp.broadcast_to(lanes[None], out_ref.shape)


def spread_sums(weights, own, control):
    row = pl.BlockSpec((STEP, W, E), lambda j: (j, 0, 0))
    scalars = pl.BlockSpec(memory_space=pltpu.SMEM)
    return pl.pallas_call(
        spread_kernel,
        grid=(ROWS // STEP,),
        in_specs=[scalars, row, row],
        out_specs=pl.BlockSpec((BANDS, 8, 128), lambda j: (0, 0, 0)),
        out_shape=jax.ShapeDtypeStruct((BANDS, 8, 128), jnp.float32),
        scratch_shapes=[pltpu.VMEM((8, E), jnp.float32)],
        compiler_params=pltpu.CompilerParams(vmem_limit_bytes=12 * MIB),
        cost_estimate=pl.CostEstimate(flops=9 << 20, bytes_accessed=11 << 20, transcendentals=0),
        name="spread_sums",
    )(weights, own, control)


def rescale_kernel(target_ref, sums_ref, own_ref, control_ref, out_ref):
    total = jnp.sum(jnp.sum(sums_ref[...], axis=0), axis=(0, 1), keepdims=True)
    scale = target_ref[0] / jnp.sqrt(total * (1.0 / TOTAL_WEIGHT) + 1e-06)
    for j in range(STEP):
        control = control_ref[j].astype(jnp.float32)
        difference = own_ref[j].astype(jnp.float32) - control
        out_ref[j] = (control + scale * difference).astype(jnp.bfloat16)


def rescaled(target, sums, own, control):
    row = pl.BlockSpec((STEP, W, E), lambda j: (j, 0, 0))
    scalars = pl.BlockSpec(memory_space=pltpu.SMEM)
    return pl.pallas_call(
        rescale_kernel,
        grid=(ROWS // STEP,),
        in_specs=[
            scalars,
            pl.BlockSpec((BANDS, 8, 128), lambda j: (0, 0, 0)),
            row,
            row,
        ],
        out_specs=row,
        out_shape=jax.ShapeDtypeStruct((ROWS, W, E), jnp.bfloat16),
        compiler_params=pltpu.CompilerParams(vmem_limit_bytes=14 * MIB),
        cost_estimate=pl.CostEstimate(flops=9 << 20, bytes_accessed=17 << 20, transcendentals=0),
        name="rescaled",
    )(target, sums, own, control)


def in_three(value):
    parts = []
    for _ in range(3):
        parts.append(lax.reduce_precision(value, exponent_bits=8, mantissa_bits=7))
        value = value - parts[-1]
    return jnp.stack(parts).astype(jnp.bfloat16)


def scattered(field, extra):
    member = lax.axis_index("member")
    kept = jnp.concatenate([field[:2].reshape(2 * W, E), extra])
    for z in (1, 7, 2, 6, 3, 5, 4):
        piece = field[2 * z : min(2 * z + 2, ROWS)].reshape(-1, E)
        arrived = lax.ppermute(jnp.concatenate([piece, extra]), "member", [(0, 2 * z)])
        if 2 * z + 1 == ROWS:
            arrived = jnp.concatenate([arrived[:W], arrived])
        kept = jnp.where(member == 2 * z, arrived, kept)
    return kept


def exchanged_along_z(pieces):
    return lax.all_to_all(
        pieces, "member", split_axis=0, concat_axis=0, axis_index_groups=RINGS, tiled=True
    )


def permuted_along_z(pieces):
    z = lax.axis_index("member") // 2
    result = pieces
    for shift in (1, 7, 2, 6, 3, 5, 4):
        block = lax.dynamic_index_in_dim(pieces, (z + shift) % DEPTH, 0, keepdims=False)
        pairs = [(ring[a], ring[(a + shift) % DEPTH]) for ring in RINGS for a in range(DEPTH)]
        arrived = lax.ppermute(block, "member", pairs)
        result = lax.dynamic_update_index_in_dim(result, arrived, (z - shift) % DEPTH, 0)
    return result


def across(value):
    arrived = lax.ppermute(value, "member", [(2 * z, 2 * z + 1) for z in range(DEPTH)])
    return jnp.where(lax.axis_index("member") % 2 == 1, arrived, value)


def shards(
    copy_fields,
    norm_gain,
    mix_real,
    mix_imag,
    filter_bank,
    perturbation_draw_numbers,
    amplitudes,
    desired_magnitude_slot,
):
    band_index = lax.axis_index("band")
    ahead_np, back_np, shared_ahead_np, shared_back_np = slot_tables()
    legendre_np = legendre_table(L, M, H).reshape(OWN, BANDS, L, H).transpose(1, 0, 2, 3)
    x = jnp.transpose(copy_fields[0], (0, 2, 1))

    global_rows = band_index * ROWS + jnp.arange(ROWS, dtype=jnp.int32)
    weights = jnp.sin((global_rows.astype(jnp.float32) + 0.5) * (math.pi / H)) * (math.pi / H)
    bank_rows = filter_bank.shape[0]
    draw_onehot = (jnp.arange(bank_rows, dtype=jnp.int32) == perturbation_draw_numbers[0]).astype(
        jnp.float32
    )
    degree_gain = jnp.sum(draw_onehot[:, None] * filter_bank, axis=0)

    legendre = rounded(legendre_np)
    gain = degree_gain[:, None]
    member = lax.axis_index("member")
    place = jnp.stack([band_index, member // 2])

    mixing = jnp.concatenate(
        [jnp.concatenate([mix_real, mix_imag], 1), jnp.concatenate([-mix_imag, mix_real], 1)], 0
    )
    z = member // 2

    fourier = forward_transform(x, norm_gain[None, :], weights, rounded(ahead_np), BANDS, STEP, 1 << 37)
    moved = lax.all_to_all(fourier, "band", split_axis=0, concat_axis=0, tiled=True)

    control_parts = across(
        scattered(x, jnp.pad(in_three(degree_gain), ((0, 16 - 3), (0, E - L))))
    )
    control_x = control_parts[: 2 * W].reshape(2, W, E)
    control_gain = jnp.sum(control_parts[2 * W : 2 * W + 3, :L].astype(jnp.float32), axis=0)
    control_weights = lax.dynamic_slice(jnp.pad(weights, (0, 1)), (2 * z,), (2,))
    control_fourier = forward_transform(
        control_x, norm_gain[None, :], control_weights, rounded(shared_ahead_np), DEPTH, 2, 1 << 29
    )
    moved, control_fourier = lax.optimization_barrier((moved, control_fourier))
    control_fourier = exchanged_along_z(control_fourier).reshape(DEPTH, 2, BANDS, 4, E)
    control_fourier = control_fourier.transpose(2, 0, 1, 3, 4).reshape(BANDS, 16, 4, E)[:, :ROWS]
    returned = spectral_pass(
        band_index[None],
        moved.reshape(H, SLOTS, E),
        legendre,
        gain,
        mixing,
        rounded(exchange_matrix()),
    )
    returned, control_fourier = lax.optimization_barrier((returned, control_fourier))
    control_moved = lax.all_to_all(control_fourier, "band", split_axis=0, concat_axis=0, tiled=True)
    control_spatial = shared_spectral_pass(
        place,
        control_moved.reshape(H, 4, E).transpose(1, 0, 2),
        legendre,
        control_gain.reshape(L, 1),
        mixing,
    )
    control_spatial = lax.all_to_all(
        control_spatial.transpose(1, 0, 2).reshape(BANDS, ROWS, 4, E),
        "band",
        split_axis=0,
        concat_axis=0,
        tiled=True,
    )
    control_spatial, returned = lax.optimization_barrier((control_spatial, returned))
    spatial = lax.all_to_all(
        returned.reshape(BANDS, ROWS, SLOTS, E), "band", split_axis=0, concat_axis=0, tiled=True
    )
    control_spatial = jnp.pad(control_spatial, ((0, 0), (0, 1), (0, 0), (0, 0)))
    control_spatial = control_spatial.reshape(BANDS, DEPTH, 2, 4, E).transpose(1, 2, 0, 3, 4)
    control_spatial = permuted_along_z(control_spatial.reshape(DEPTH, 2, BANDS * 4, E))
    control = inverse_transform(control_spatial, control_x, rounded(shared_back_np), 2, 1 << 29)
    control = lax.all_gather(control, "member", tiled=True, axis_index_groups=RINGS)

    forecast = inverse_transform(spatial, x, rounded(back_np), STEP, 1 << 38)
    sums = lax.all_to_all(
        spread_sums(weights, forecast, control),
        "band",
        split_axis=0,
        concat_axis=0,
        tiled=True,
    )
    target = jnp.sum(
        jnp.where(
            jnp.arange(amplitudes.shape[0], dtype=jnp.int32) == desired_magnitude_slot[0],
            amplitudes,
            0.0,
        )
    )
    bred = rescaled(jnp.where(member > 0, target, 0.0)[None], sums, forecast, control)
    return jnp.transpose(bred, (0, 2, 1))[None]


def solution(mesh):
    in_specs = (P("member", "band", None, None), P(), P(), P(), P(), P("member"), P(), P("member"))
    out_specs = P("member", "band", None, None)
    return jax.shard_map(shards, mesh=mesh, in_specs=in_specs, out_specs=out_specs, check_vma=False)
```

```python
import functools
import math

import jax
import jax.numpy as jnp
import numpy as np
from jax import lax
from jax.experimental import pallas as pl
from jax.experimental.pallas import tpu as pltpu
from jax.sharding import PartitionSpec as P

H = 240
W = 480
M = 240
L = 240
E = 384
BANDS = 16
ROWS = H // BANDS
OWN = M // BANDS
SLOTS = 32
DEPTH = 8
RINGS = [[2 * z + h for z in range(DEPTH)] for h in range(2)]
STEP = 3
TOTAL_WEIGHT = float(np.sum(np.sin((np.arange(H) + 0.5) * np.pi / H)) * np.pi / H * E * W)
MIB = 1 << 20


def legendre_table(degree_count, order_count, lat_count):
    colatitude = (np.arange(lat_count) + 0.5) * np.pi / lat_count
    cosines = np.cos(colatitude)
    sines = np.sin(colatitude)
    orders = np.arange(order_count)[:, None] * 1.0
    steps_up = np.arange(1, order_count) * 1.0
    log_factor = np.concatenate(
        [[0.0], np.cumsum(np.log((2.0 * steps_up - 1.0) / (2.0 * steps_up)))]
    )
    diagonal_start = np.exp(
        0.5 * np.log((2.0 * orders + 1.0) / 2.0)
        + 0.5 * log_factor[:, None]
        + orders * np.log(sines)[None, :]
    )
    result = np.zeros((order_count, degree_count, lat_count))
    previous = np.zeros(diagonal_start.shape)
    before_previous = np.zeros(diagonal_start.shape)
    for degree in range(degree_count):
        lower = degree - 1.0
        rising = np.sqrt(
            np.maximum(4.0 * degree * degree - 1.0, 1.0)
            / np.maximum(degree * degree - orders * orders, 1.0)
        )
        falling = np.sqrt(
            np.maximum(lower * lower - orders * orders, 0.0) / max(4.0 * lower * lower - 1.0, 1.0)
        )
        current = np.where(
            orders == degree,
            diagonal_start,
            np.where(
                degree > orders,
                rising * (cosines[None, :] * previous - falling * before_previous),
                0.0,
            ),
        )
        result[:, degree] = current
        before_previous = previous
        previous = current
    return result


def fourier_tables(lon_count, mode_order):
    longitude = 2.0 * np.pi * np.arange(lon_count)[:, None] / lon_count
    angles = longitude * (mode_order[None, :] * 1.0)
    forward_factor = math.sqrt(2.0 * math.pi) / lon_count
    forward_table = np.stack(
        [forward_factor * np.cos(angles), -forward_factor * np.sin(angles)], axis=1
    )
    inverse_factor = np.where(mode_order == 0, 1.0, 2.0) / math.sqrt(2.0 * math.pi)
    inverse_table = np.stack(
        [
            (inverse_factor[None, :] * np.cos(angles)).T,
            (-inverse_factor[None, :] * np.sin(angles)).T,
        ],
        axis=0,
    )
    return (forward_table, inverse_table)


def slot_tables():
    forward, inverse = fourier_tables(W, np.arange(M))
    ahead = np.zeros((W, 2, 16, BANDS))
    back = np.zeros((2, 16, BANDS, W))
    ahead[:, :, :OWN] = forward.reshape(W, 2, OWN, BANDS)
    back[:, :OWN] = inverse.reshape(2, OWN, BANDS, W)
    ahead = ahead.reshape(W, 2, DEPTH, 2, BANDS)
    back = back.reshape(2, DEPTH, 2, BANDS, W)
    rows = BANDS * SLOTS
    return (
        ahead.transpose(4, 2, 1, 3, 0).reshape(rows, W),
        back.transpose(3, 1, 0, 2, 4).reshape(rows, W).T,
        ahead.transpose(2, 4, 1, 3, 0).reshape(rows, W),
        back.transpose(1, 3, 0, 2, 4).reshape(rows, W).T,
    )


def rounded(table):
    return jnp.asarray(table, jnp.float32).astype(jnp.bfloat16)


def exchange_matrix():
    matrix = np.zeros((256, 256))
    for a in range(16):
        for b in range(16):
            matrix[b * 16 + a, a * 16 + b] = 1.0
    return matrix


def forward_kernel(weights_ref, x_ref, gain_ref, table_ref, out_ref):
    rows = x_ref.shape[0]
    for j in range(rows):
        x = x_ref[j].astype(jnp.float32)
        centred = x - jnp.mean(x, axis=1, keepdims=True)
        variance = jnp.mean(jnp.square(centred), axis=1, keepdims=True)
        normed = (centred * lax.rsqrt(variance + 1e-05) * gain_ref[...]).astype(jnp.bfloat16)
        sums = jnp.dot(table_ref[...], normed, preferred_element_type=jnp.float32)
        sums = (sums * weights_ref[pl.program_id(0) * rows + j]).astype(jnp.bfloat16)
        out_ref[:, j] = sums.reshape(out_ref.shape[0], out_ref.shape[2], E)


def forward_transform(x, gain, weights, table, groups, step, flops):
    rows = x.shape[0]
    size = BANDS * SLOTS // groups
    return pl.pallas_call(
        forward_kernel,
        grid=(rows // step,),
        in_specs=[
            pl.BlockSpec(memory_space=pltpu.SMEM),
            pl.BlockSpec((step, W, E), lambda j: (j, 0, 0)),
            pl.BlockSpec((1, E), lambda j: (0, 0)),
            pl.BlockSpec((BANDS * SLOTS, W), lambda j: (0, 0)),
        ],
        out_specs=pl.BlockSpec((groups, step, size, E), lambda j: (0, j, 0, 0)),
        out_shape=jax.ShapeDtypeStruct((groups, rows, size, E), jnp.bfloat16),
        compiler_params=pltpu.CompilerParams(vmem_limit_bytes=58 * MIB),
        cost_estimate=pl.CostEstimate(flops=flops, bytes_accessed=rows << 20, transcendentals=0),
        name="forward_transform",
    )(weights, x, gain, table)


def mix_degrees(table, values, gain, mixing):
    coeffs = jnp.dot(table, values, preferred_element_type=jnp.float32).astype(jnp.bfloat16)
    return (jnp.dot(coeffs, mixing, preferred_element_type=jnp.float32) * gain).astype(jnp.bfloat16)


def to_latitudes(table, mixed):
    return lax.dot_general(
        table, mixed, (((0,), (0,)), ((), ())), preferred_element_type=jnp.float32
    ).astype(jnp.bfloat16)


def shared_spectral_kernel(
    place_ref, re_ref, im_ref, legendre_ref, gain_ref, mixing_ref, out_re_ref, out_im_ref
):
    table = legendre_ref[0, 0]
    values = jnp.concatenate([re_ref[0], im_ref[0]], axis=1)
    spatial = to_latitudes(table, mix_degrees(table, values, gain_ref[...], mixing_ref[...]))
    out_re_ref[0] = spatial[:, :E]
    out_im_ref[0] = spatial[:, E:]


def shared_spectral_pass(place, moved, legendre, gain, mixing):
    row = lambda first: pl.BlockSpec((1, H, E), lambda o, place: (first + o, 0, 0))
    whole = lambda *shape: pl.BlockSpec(shape, lambda o, place: (0,) * len(shape))
    pair = jax.ShapeDtypeStruct((2, H, E), jnp.bfloat16)
    out_re, out_im = pl.pallas_call(
        shared_spectral_kernel,
        grid_spec=pltpu.PrefetchScalarGridSpec(
            num_scalar_prefetch=1,
            grid=(2,),
            in_specs=[
                row(0),
                row(2),
                pl.BlockSpec(
                    (1, 1, L, H),
                    lambda o, place: (place[0], jnp.minimum(2 * place[1] + o, OWN - 1), 0, 0),
                ),
                whole(L, 1),
                whole(2 * E, 2 * E),
            ],
            out_specs=[row(0), row(0)],
        ),
        out_shape=[pair, pair],
        compiler_params=pltpu.CompilerParams(vmem_limit_bytes=58 * MIB),
        cost_estimate=pl.CostEstimate(flops=1 << 30, bytes_accessed=4 << 20, transcendentals=0),
        name="shared_spectral_pass",
    )(place, moved, moved, legendre, gain, mixing)
    return jnp.concatenate([out_re, out_im], axis=0)


def spectral_kernel(
    band_ref, moved_ref, legendre_ref, gain_ref, mixing_ref, swap_ref, out_ref, by_mode, mixed
):
    swap = swap_ref[...]
    halves = [(half, lanes) for half, lanes in ((0, slice(0, E)), (16, slice(E, 2 * E)))]
    unroll = 3

    def place_of(slot):
        z, part, o = slot // 4, (slot // 2) % 2, slot % 2
        return 2 * z + o, slice(part * E, part * E + E)

    def to_modes(step, carry):
        for piece in range(unroll):
            rows = pl.ds(pl.multiple_of((step * unroll + piece) * 16, 16), 16)
            block = jnp.concatenate(
                [moved_ref[rows, half : half + 16, :].reshape(256, E) for half, _ in halves], axis=1
            )
            turned = jnp.dot(swap, block, preferred_element_type=jnp.float32).astype(jnp.bfloat16)
            turned = turned.reshape(16, 16, 2 * E)
            for half, lanes in halves:
                for k in range(16):
                    i, part = place_of(half + k)
                    by_mode[i, rows, part] = turned[k, :, lanes]
        return carry

    lax.fori_loop(0, H // 16 // unroll, to_modes, 0)
    mixing = mixing_ref[...]
    for i in range(OWN):
        low = 16 * i
        table = legendre_ref[0, i]
        mixed[low:, :] = mix_degrees(table[low:], by_mode[i], gain_ref[low:], mixing)
        by_mode[i] = to_latitudes(table, mixed[...])

    def to_rows(step, carry):
        for piece in range(unroll):
            rows = pl.ds(pl.multiple_of((step * unroll + piece) * 16, 16), 16)
            blocks = []
            for half, _ in halves:
                slots = []
                for k in range(16):
                    i, part = place_of(half + k)
                    slots.append(by_mode[i, rows, part])
                blocks.append(jnp.concatenate(slots, axis=0))
            block = jnp.concatenate(blocks, axis=1)
            turned = jnp.dot(swap, block, preferred_element_type=jnp.float32).astype(jnp.bfloat16)
            turned = turned.reshape(16, 16, 2 * E)
            for half, lanes in halves:
                out_ref[rows, half : half + 16, :] = turned[:, :, lanes]
        return carry

    lax.fori_loop(0, H // 16 // unroll, to_rows, 0)


def spectral_pass(band, moved, legendre, gain, mixing, swap):
    whole = lambda *shape: pl.BlockSpec(shape, lambda step, band: (0,) * len(shape))
    return pl.pallas_call(
        spectral_kernel,
        grid_spec=pltpu.PrefetchScalarGridSpec(
            num_scalar_prefetch=1,
            grid=(1,),
            in_specs=[
                whole(H, SLOTS, E),
                pl.BlockSpec((1, OWN, L, H), lambda step, band: (band[0], 0, 0, 0)),
                whole(L, 1),
                whole(2 * E, 2 * E),
                whole(256, 256),
            ],
            out_specs=whole(H, SLOTS, E),
            scratch_shapes=[
                pltpu.VMEM((16, H, 2 * E), jnp.bfloat16),
                pltpu.VMEM((L, 2 * E), jnp.bfloat16),
            ],
        ),
        out_shape=jax.ShapeDtypeStruct((H, SLOTS, E), jnp.bfloat16),
        compiler_params=pltpu.CompilerParams(vmem_limit_bytes=58 * MIB),
        cost_estimate=pl.CostEstimate(flops=8 << 30, bytes_accessed=14 << 20, transcendentals=0),
        name="spectral_pass",
    )(band, moved, legendre, gain, mixing, swap)


def inverse_kernel(spatial_ref, x_ref, table_ref, out_ref):
    for j in range(x_ref.shape[0]):
        spatial = spatial_ref[:, j].reshape(BANDS * SLOTS, E)
        sums = jnp.dot(table_ref[...], spatial, preferred_element_type=jnp.float32)
        out_ref[j] = (x_ref[j].astype(jnp.float32) + jax.nn.gelu(sums)).astype(jnp.bfloat16)


def inverse_transform(spatial, x, table, step, flops):
    rows = x.shape[0]
    groups, _, size, _ = spatial.shape
    return pl.pallas_call(
        inverse_kernel,
        grid=(rows // step,),
        in_specs=[
            pl.BlockSpec((groups, step, size, E), lambda j: (0, j, 0, 0)),
            pl.BlockSpec((step, W, E), lambda j: (j, 0, 0)),
            pl.BlockSpec((W, BANDS * SLOTS), lambda j: (0, 0)),
        ],
        out_specs=pl.BlockSpec((step, W, E), lambda j: (j, 0, 0)),
        out_shape=jax.ShapeDtypeStruct((rows, W, E), jnp.bfloat16),
        compiler_params=pltpu.CompilerParams(vmem_limit_bytes=58 * MIB),
        cost_estimate=pl.CostEstimate(
            flops=flops, bytes_accessed=rows << 20, transcendentals=rows * W * E
        ),
        name="inverse_transform",
    )(spatial, x, table)


def spread_kernel(weights_ref, own_ref, control_ref, out_ref, total):
    step = pl.program_id(0)
    partial = 0.0
    for j in range(STEP):
        difference = own_ref[j].astype(jnp.float32) - control_ref[j].astype(jnp.float32)
        squares = jnp.sum((difference * difference).reshape(W // 8, 8, E), axis=0)
        partial = partial + squares * weights_ref[step * STEP + j]

    @pl.when(step == 0)
    def _():
        total[...] = partial

    @pl.when(step > 0)
    def _():
        total[...] += partial

    @pl.when(step == ROWS // STEP - 1)
    def _():
        lanes = total[:, :128] + total[:, 128:256] + total[:, 256:]
        out_ref[...] = jnp.broadcast_to(lanes[None], out_ref.shape)


def spread_sums(weights, own, control):
    row = pl.BlockSpec((STEP, W, E), lambda j: (j, 0, 0))
    scalars = pl.BlockSpec(memory_space=pltpu.SMEM)
    return pl.pallas_call(
        spread_kernel,
        grid=(ROWS // STEP,),
        in_specs=[scalars, row, row],
        out_specs=pl.BlockSpec((BANDS, 8, 128), lambda j: (0, 0, 0)),
        out_shape=jax.ShapeDtypeStruct((BANDS, 8, 128), jnp.float32),
        scratch_shapes=[pltpu.VMEM((8, E), jnp.float32)],
        compiler_params=pltpu.CompilerParams(vmem_limit_bytes=58 * MIB),
        cost_estimate=pl.CostEstimate(flops=9 << 20, bytes_accessed=11 << 20, transcendentals=0),
        name="spread_sums",
    )(weights, own, control)


def rescale_kernel(target_ref, sums_ref, own_ref, control_ref, out_ref):
    total = jnp.sum(jnp.sum(sums_ref[...], axis=0), axis=(0, 1), keepdims=True)
    scale = target_ref[0] / jnp.sqrt(total * (1.0 / TOTAL_WEIGHT) + 1e-06)
    for j in range(STEP):
        control = control_ref[j].astype(jnp.float32)
        difference = own_ref[j].astype(jnp.float32) - control
        out_ref[j] = (control + scale * difference).astype(jnp.bfloat16)


def rescaled(target, sums, own, control):
    row = pl.BlockSpec((STEP, W, E), lambda j: (j, 0, 0))
    scalars = pl.BlockSpec(memory_space=pltpu.SMEM)
    return pl.pallas_call(
        rescale_kernel,
        grid=(ROWS // STEP,),
        in_specs=[
            scalars,
            pl.BlockSpec((BANDS, 8, 128), lambda j: (0, 0, 0)),
            row,
            row,
        ],
        out_specs=row,
        out_shape=jax.ShapeDtypeStruct((ROWS, W, E), jnp.bfloat16),
        compiler_params=pltpu.CompilerParams(vmem_limit_bytes=58 * MIB),
        cost_estimate=pl.CostEstimate(flops=9 << 20, bytes_accessed=17 << 20, transcendentals=0),
        name="rescaled",
    )(target, sums, own, control)


def in_three(value):
    parts = []
    for _ in range(3):
        parts.append(lax.reduce_precision(value, exponent_bits=8, mantissa_bits=7))
        value = value - parts[-1]
    return jnp.stack(parts).astype(jnp.bfloat16)


def scattered(field, extra):
    member = lax.axis_index("member")
    kept = jnp.concatenate([field[:2].reshape(2 * W, E), extra])
    for z in (1, 7, 2, 6, 3, 5, 4):
        piece = field[2 * z : min(2 * z + 2, ROWS)].reshape(-1, E)
        arrived = lax.ppermute(jnp.concatenate([piece, extra]), "member", [(0, 2 * z)])
        if 2 * z + 1 == ROWS:
            arrived = jnp.concatenate([arrived[:W], arrived])
        kept = jnp.where(member == 2 * z, arrived, kept)
    return kept


def exchanged_along_z(pieces):
    return lax.all_to_all(
        pieces, "member", split_axis=0, concat_axis=0, axis_index_groups=RINGS, tiled=True
    )


def permuted_along_z(pieces):
    z = lax.axis_index("member") // 2
    result = pieces
    for shift in (1, 7, 2, 6, 3, 5, 4):
        block = lax.dynamic_index_in_dim(pieces, (z + shift) % DEPTH, 0, keepdims=False)
        pairs = [(ring[a], ring[(a + shift) % DEPTH]) for ring in RINGS for a in range(DEPTH)]
        arrived = lax.ppermute(block, "member", pairs)
        result = lax.dynamic_update_index_in_dim(result, arrived, (z - shift) % DEPTH, 0)
    return result


def across(value):
    arrived = lax.ppermute(value, "member", [(2 * z, 2 * z + 1) for z in range(DEPTH)])
    return jnp.where(lax.axis_index("member") % 2 == 1, arrived, value)


def shards(
    copy_fields,
    norm_gain,
    mix_real,
    mix_imag,
    filter_bank,
    perturbation_draw_numbers,
    amplitudes,
    desired_magnitude_slot,
):
    band_index = lax.axis_index("band")
    ahead_np, back_np, shared_ahead_np, shared_back_np = slot_tables()
    legendre_np = legendre_table(L, M, H).reshape(OWN, BANDS, L, H).transpose(1, 0, 2, 3)
    x = jnp.transpose(copy_fields[0], (0, 2, 1))

    global_rows = band_index * ROWS + jnp.arange(ROWS, dtype=jnp.int32)
    weights = jnp.sin((global_rows.astype(jnp.float32) + 0.5) * (math.pi / H)) * (math.pi / H)
    bank_rows = filter_bank.shape[0]
    draw_onehot = (jnp.arange(bank_rows, dtype=jnp.int32) == perturbation_draw_numbers[0]).astype(
        jnp.float32
    )
    degree_gain = jnp.sum(draw_onehot[:, None] * filter_bank, axis=0)

    legendre = rounded(legendre_np)
    gain = degree_gain[:, None]
    member = lax.axis_index("member")
    place = jnp.stack([band_index, member // 2])

    mixing = jnp.concatenate(
        [jnp.concatenate([mix_real, mix_imag], 1), jnp.concatenate([-mix_imag, mix_real], 1)], 0
    )
    z = member // 2

    fourier = forward_transform(x, norm_gain[None, :], weights, rounded(ahead_np), BANDS, STEP, 1 << 37)
    moved = lax.all_to_all(fourier, "band", split_axis=0, concat_axis=0, tiled=True)

    control_parts = across(
        scattered(x, jnp.pad(in_three(degree_gain), ((0, 16 - 3), (0, E - L))))
    )
    control_x = control_parts[: 2 * W].reshape(2, W, E)
    control_gain = jnp.sum(control_parts[2 * W : 2 * W + 3, :L].astype(jnp.float32), axis=0)
    control_weights = lax.dynamic_slice(jnp.pad(weights, (0, 1)), (2 * z,), (2,))
    control_fourier = forward_transform(
        control_x, norm_gain[None, :], control_weights, rounded(shared_ahead_np), DEPTH, 2, 1 << 29
    )
    moved, control_fourier = lax.optimization_barrier((moved, control_fourier))
    control_fourier = exchanged_along_z(control_fourier).reshape(DEPTH, 2, BANDS, 4, E)
    control_fourier = control_fourier.transpose(2, 0, 1, 3, 4).reshape(BANDS, 16, 4, E)[:, :ROWS]
    returned = spectral_pass(
        band_index[None],
        moved.reshape(H, SLOTS, E),
        legendre,
        gain,
        mixing,
        rounded(exchange_matrix()),
    )
    returned, control_fourier = lax.optimization_barrier((returned, control_fourier))
    control_moved = lax.all_to_all(control_fourier, "band", split_axis=0, concat_axis=0, tiled=True)
    control_spatial = shared_spectral_pass(
        place,
        control_moved.reshape(H, 4, E).transpose(1, 0, 2),
        legendre,
        control_gain.reshape(L, 1),
        mixing,
    )
    control_spatial = lax.all_to_all(
        control_spatial.transpose(1, 0, 2).reshape(BANDS, ROWS, 4, E),
        "band",
        split_axis=0,
        concat_axis=0,
        tiled=True,
    )
    control_spatial, returned = lax.optimization_barrier((control_spatial, returned))
    spatial = lax.all_to_all(
        returned.reshape(BANDS, ROWS, SLOTS, E), "band", split_axis=0, concat_axis=0, tiled=True
    )
    control_spatial = jnp.pad(control_spatial, ((0, 0), (0, 1), (0, 0), (0, 0)))
    control_spatial = control_spatial.reshape(BANDS, DEPTH, 2, 4, E).transpose(1, 2, 0, 3, 4)
    control_spatial = permuted_along_z(control_spatial.reshape(DEPTH, 2, BANDS * 4, E))
    control = inverse_transform(control_spatial, control_x, rounded(shared_back_np), 2, 1 << 29)
    control = lax.all_gather(control, "member", tiled=True, axis_index_groups=RINGS)

    forecast = inverse_transform(spatial, x, rounded(back_np), STEP, 1 << 38)
    sums = lax.all_to_all(
        spread_sums(weights, forecast, control),
        "band",
        split_axis=0,
        concat_axis=0,
        tiled=True,
    )
    target = jnp.sum(
        jnp.where(
            jnp.arange(amplitudes.shape[0], dtype=jnp.int32) == desired_magnitude_slot[0],
            amplitudes,
            0.0,
        )
    )
    bred = rescaled(jnp.where(member > 0, target, 0.0)[None], sums, forecast, control)
    return jnp.transpose(bred, (0, 2, 1))[None]


def solution(mesh):
    in_specs = (P("member", "band", None, None), P(), P(), P(), P(), P("member"), P(), P("member"))
    out_specs = P("member", "band", None, None)
    return jax.shard_map(shards, mesh=mesh, in_specs=in_specs, out_specs=out_specs, check_vma=False)
```

```python
import functools
import math

import jax
import jax.numpy as jnp
import numpy as np
from jax import lax
from jax.experimental import pallas as pl
from jax.experimental.pallas import tpu as pltpu
from jax.sharding import PartitionSpec as P

H = 240
W = 480
M = 240
L = 240
E = 384
BANDS = 16
ROWS = H // BANDS
OWN = M // BANDS
SLOTS = 32
DEPTH = 8
SHIFT = 3
BOTH_WAYS = (1, 7, 2, 6, 3, 5, 4)
RINGS = [[2 * z + h for z in range(DEPTH)] for h in range(2)]
STEP = 3
TOTAL_WEIGHT = float(np.sum(np.sin((np.arange(H) + 0.5) * np.pi / H)) * np.pi / H * E * W)
MIB = 1 << 20


def legendre_table(degree_count, order_count, lat_count):
    colatitude = (np.arange(lat_count) + 0.5) * np.pi / lat_count
    cosines = np.cos(colatitude)
    sines = np.sin(colatitude)
    orders = np.arange(order_count)[:, None] * 1.0
    steps_up = np.arange(1, order_count) * 1.0
    log_factor = np.concatenate(
        [[0.0], np.cumsum(np.log((2.0 * steps_up - 1.0) / (2.0 * steps_up)))]
    )
    diagonal_start = np.exp(
        0.5 * np.log((2.0 * orders + 1.0) / 2.0)
        + 0.5 * log_factor[:, None]
        + orders * np.log(sines)[None, :]
    )
    result = np.zeros((order_count, degree_count, lat_count))
    previous = np.zeros(diagonal_start.shape)
    before_previous = np.zeros(diagonal_start.shape)
    for degree in range(degree_count):
        lower = degree - 1.0
        rising = np.sqrt(
            np.maximum(4.0 * degree * degree - 1.0, 1.0)
            / np.maximum(degree * degree - orders * orders, 1.0)
        )
        falling = np.sqrt(
            np.maximum(lower * lower - orders * orders, 0.0) / max(4.0 * lower * lower - 1.0, 1.0)
        )
        current = np.where(
            orders == degree,
            diagonal_start,
            np.where(
                degree > orders,
                rising * (cosines[None, :] * previous - falling * before_previous),
                0.0,
            ),
        )
        result[:, degree] = current
        before_previous = previous
        previous = current
    return result


def fourier_tables(lon_count, mode_order):
    longitude = 2.0 * np.pi * np.arange(lon_count)[:, None] / lon_count
    angles = longitude * (mode_order[None, :] * 1.0)
    forward_factor = math.sqrt(2.0 * math.pi) / lon_count
    forward_table = np.stack(
        [forward_factor * np.cos(angles), -forward_factor * np.sin(angles)], axis=1
    )
    inverse_factor = np.where(mode_order == 0, 1.0, 2.0) / math.sqrt(2.0 * math.pi)
    inverse_table = np.stack(
        [
            (inverse_factor[None, :] * np.cos(angles)).T,
            (-inverse_factor[None, :] * np.sin(angles)).T,
        ],
        axis=0,
    )
    return (forward_table, inverse_table)


def slot_tables():
    forward, inverse = fourier_tables(W, np.arange(M))
    ahead = np.zeros((W, 2, 16, BANDS))
    back = np.zeros((2, 16, BANDS, W))
    ahead[:, :, :OWN] = forward.reshape(W, 2, OWN, BANDS)
    back[:, :OWN] = inverse.reshape(2, OWN, BANDS, W)
    ahead = ahead.reshape(W, 2, DEPTH, 2, BANDS)
    back = back.reshape(2, DEPTH, 2, BANDS, W)
    rows = BANDS * SLOTS
    return (
        ahead.transpose(4, 2, 1, 3, 0).reshape(rows, W),
        back.transpose(3, 1, 0, 2, 4).reshape(rows, W).T,
        ahead.transpose(2, 4, 1, 3, 0).reshape(rows, W),
        back.transpose(1, 3, 0, 2, 4).reshape(rows, W).T,
    )


def rounded(table):
    return jnp.asarray(table, jnp.float32).astype(jnp.bfloat16)


def exchange_matrix():
    matrix = np.zeros((256, 256))
    for a in range(16):
        for b in range(16):
            matrix[b * 16 + a, a * 16 + b] = 1.0
    return matrix


def forward_kernel(weights_ref, x_ref, gain_ref, table_ref, out_ref):
    rows = x_ref.shape[0]
    for j in range(rows):
        x = x_ref[j].astype(jnp.float32)
        centred = x - jnp.mean(x, axis=1, keepdims=True)
        variance = jnp.mean(jnp.square(centred), axis=1, keepdims=True)
        normed = (centred * lax.rsqrt(variance + 1e-05) * gain_ref[...]).astype(jnp.bfloat16)
        sums = jnp.dot(table_ref[...], normed, preferred_element_type=jnp.float32)
        sums = (sums * weights_ref[pl.program_id(0) * rows + j]).astype(jnp.bfloat16)
        out_ref[:, j] = sums.reshape(out_ref.shape[0], out_ref.shape[2], E)


def forward_transform(x, gain, weights, table, groups, step, flops):
    rows = x.shape[0]
    size = BANDS * SLOTS // groups
    return pl.pallas_call(
        forward_kernel,
        grid=(rows // step,),
        in_specs=[
            pl.BlockSpec(memory_space=pltpu.SMEM),
            pl.BlockSpec((step, W, E), lambda j: (j, 0, 0)),
            pl.BlockSpec((1, E), lambda j: (0, 0)),
            pl.BlockSpec((BANDS * SLOTS, W), lambda j: (0, 0)),
        ],
        out_specs=pl.BlockSpec((groups, step, size, E), lambda j: (0, j, 0, 0)),
        out_shape=jax.ShapeDtypeStruct((groups, rows, size, E), jnp.bfloat16),
        compiler_params=pltpu.CompilerParams(vmem_limit_bytes=58 * MIB),
        cost_estimate=pl.CostEstimate(flops=flops, bytes_accessed=rows << 20, transcendentals=0),
        name="forward_transform",
    )(weights, x, gain, table)


def mix_degrees(table, values, gain, mixing):
    coeffs = jnp.dot(table, values, preferred_element_type=jnp.float32).astype(jnp.bfloat16)
    return (jnp.dot(coeffs, mixing, preferred_element_type=jnp.float32) * gain).astype(jnp.bfloat16)


def to_latitudes(table, mixed):
    return lax.dot_general(
        table, mixed, (((0,), (0,)), ((), ())), preferred_element_type=jnp.float32
    ).astype(jnp.bfloat16)


def shared_spectral_kernel(
    place_ref, re_ref, im_ref, legendre_ref, gain_ref, mixing_ref, out_re_ref, out_im_ref
):
    table = legendre_ref[0, 0]
    values = jnp.concatenate([re_ref[0], im_ref[0]], axis=1)
    spatial = to_latitudes(table, mix_degrees(table, values, gain_ref[...], mixing_ref[...]))
    out_re_ref[0] = spatial[:, :E]
    out_im_ref[0] = spatial[:, E:]


def shared_spectral_pass(place, moved, legendre, gain, mixing):
    row = lambda first: pl.BlockSpec((1, H, E), lambda o, place: (first + o, 0, 0))
    whole = lambda *shape: pl.BlockSpec(shape, lambda o, place: (0,) * len(shape))
    pair = jax.ShapeDtypeStruct((2, H, E), jnp.bfloat16)
    out_re, out_im = pl.pallas_call(
        shared_spectral_kernel,
        grid_spec=pltpu.PrefetchScalarGridSpec(
            num_scalar_prefetch=1,
            grid=(2,),
            in_specs=[
                row(0),
                row(2),
                pl.BlockSpec(
                    (1, 1, L, H),
                    lambda o, place: (place[0], jnp.minimum(2 * place[1] + o, OWN - 1), 0, 0),
                ),
                whole(L, 1),
                whole(2 * E, 2 * E),
            ],
            out_specs=[row(0), row(0)],
        ),
        out_shape=[pair, pair],
        compiler_params=pltpu.CompilerParams(vmem_limit_bytes=58 * MIB),
        cost_estimate=pl.CostEstimate(flops=1 << 30, bytes_accessed=4 << 20, transcendentals=0),
        name="shared_spectral_pass",
    )(place, moved, moved, legendre, gain, mixing)
    return jnp.concatenate([out_re, out_im], axis=0)


def spectral_kernel(
    band_ref, moved_ref, legendre_ref, gain_ref, mixing_ref, swap_ref, out_ref, by_mode, mixed
):
    swap = swap_ref[...]
    halves = [(half, lanes) for half, lanes in ((0, slice(0, E)), (16, slice(E, 2 * E)))]
    unroll = 3

    def place_of(slot):
        z, part, o = slot // 4, (slot // 2) % 2, slot % 2
        return 2 * z + o, slice(part * E, part * E + E)

    def to_modes(step, carry):
        for piece in range(unroll):
            rows = pl.ds(pl.multiple_of((step * unroll + piece) * 16, 16), 16)
            block = jnp.concatenate(
                [moved_ref[rows, half : half + 16, :].reshape(256, E) for half, _ in halves], axis=1
            )
            turned = jnp.dot(swap, block, preferred_element_type=jnp.float32).astype(jnp.bfloat16)
            turned = turned.reshape(16, 16, 2 * E)
            for half, lanes in halves:
                for k in range(16):
                    i, part = place_of(half + k)
                    by_mode[i, rows, part] = turned[k, :, lanes]
        return carry

    lax.fori_loop(0, H // 16 // unroll, to_modes, 0)
    mixing = mixing_ref[...]
    for i in range(OWN):
        low = 16 * i
        table = legendre_ref[0, i]
        mixed[low:, :] = mix_degrees(table[low:], by_mode[i], gain_ref[low:], mixing)
        by_mode[i] = to_latitudes(table, mixed[...])

    def to_rows(step, carry):
        for piece in range(unroll):
            rows = pl.ds(pl.multiple_of((step * unroll + piece) * 16, 16), 16)
            blocks = []
            for half, _ in halves:
                slots = []
                for k in range(16):
                    i, part = place_of(half + k)
                    slots.append(by_mode[i, rows, part])
                blocks.append(jnp.concatenate(slots, axis=0))
            block = jnp.concatenate(blocks, axis=1)
            turned = jnp.dot(swap, block, preferred_element_type=jnp.float32).astype(jnp.bfloat16)
            turned = turned.reshape(16, 16, 2 * E)
            for half, lanes in halves:
                out_ref[rows, half : half + 16, :] = turned[:, :, lanes]
        return carry

    lax.fori_loop(0, H // 16 // unroll, to_rows, 0)


def spectral_pass(band, moved, legendre, gain, mixing, swap):
    whole = lambda *shape: pl.BlockSpec(shape, lambda step, band: (0,) * len(shape))
    return pl.pallas_call(
        spectral_kernel,
        grid_spec=pltpu.PrefetchScalarGridSpec(
            num_scalar_prefetch=1,
            grid=(1,),
            in_specs=[
                whole(H, SLOTS, E),
                pl.BlockSpec((1, OWN, L, H), lambda step, band: (band[0], 0, 0, 0)),
                whole(L, 1),
                whole(2 * E, 2 * E),
                whole(256, 256),
            ],
            out_specs=whole(H, SLOTS, E),
            scratch_shapes=[
                pltpu.VMEM((16, H, 2 * E), jnp.bfloat16),
                pltpu.VMEM((L, 2 * E), jnp.bfloat16),
            ],
        ),
        out_shape=jax.ShapeDtypeStruct((H, SLOTS, E), jnp.bfloat16),
        compiler_params=pltpu.CompilerParams(vmem_limit_bytes=58 * MIB),
        cost_estimate=pl.CostEstimate(flops=8 << 30, bytes_accessed=14 << 20, transcendentals=0),
        name="spectral_pass",
    )(band, moved, legendre, gain, mixing, swap)


def inverse_kernel(spatial_ref, x_ref, table_ref, out_ref):
    for j in range(x_ref.shape[0]):
        spatial = spatial_ref[:, j].reshape(BANDS * SLOTS, E)
        sums = jnp.dot(table_ref[...], spatial, preferred_element_type=jnp.float32)
        out_ref[j] = (x_ref[j].astype(jnp.float32) + jax.nn.gelu(sums)).astype(jnp.bfloat16)


def inverse_transform(spatial, x, table, step, flops):
    rows = x.shape[0]
    groups, _, size, _ = spatial.shape
    return pl.pallas_call(
        inverse_kernel,
        grid=(rows // step,),
        in_specs=[
            pl.BlockSpec((groups, step, size, E), lambda j: (0, j, 0, 0)),
            pl.BlockSpec((step, W, E), lambda j: (j, 0, 0)),
            pl.BlockSpec((W, BANDS * SLOTS), lambda j: (0, 0)),
        ],
        out_specs=pl.BlockSpec((step, W, E), lambda j: (j, 0, 0)),
        out_shape=jax.ShapeDtypeStruct((rows, W, E), jnp.bfloat16),
        compiler_params=pltpu.CompilerParams(vmem_limit_bytes=58 * MIB),
        cost_estimate=pl.CostEstimate(
            flops=flops, bytes_accessed=rows << 20, transcendentals=rows * W * E
        ),
        name="inverse_transform",
    )(spatial, x, table)


def control_rows(t):
    return pl.BlockSpec((1, W, E), lambda j: ((STEP * j + t + 16 - 2 * SHIFT) % 16, 0, 0))


def spread_kernel(weights_ref, own_ref, *refs):
    *control_refs, out_ref, total = refs
    step = pl.program_id(0)
    partial = 0.0
    for j in range(STEP):
        difference = own_ref[j].astype(jnp.float32) - control_refs[j][0].astype(jnp.float32)
        squares = jnp.sum((difference * difference).reshape(W // 8, 8, E), axis=0)
        partial = partial + squares * weights_ref[step * STEP + j]

    @pl.when(step == 0)
    def _():
        total[...] = partial

    @pl.when(step > 0)
    def _():
        total[...] += partial

    @pl.when(step == ROWS // STEP - 1)
    def _():
        lanes = total[:, :128] + total[:, 128:256] + total[:, 256:]
        out_ref[...] = jnp.broadcast_to(lanes[None], out_ref.shape)


def spread_sums(weights, own, control):
    row = pl.BlockSpec((STEP, W, E), lambda j: (j, 0, 0))
    scalars = pl.BlockSpec(memory_space=pltpu.SMEM)
    return pl.pallas_call(
        spread_kernel,
        grid=(ROWS // STEP,),
        in_specs=[scalars, row] + [control_rows(t) for t in range(STEP)],
        out_specs=pl.BlockSpec((BANDS, 8, 128), lambda j: (0, 0, 0)),
        out_shape=jax.ShapeDtypeStruct((BANDS, 8, 128), jnp.float32),
        scratch_shapes=[pltpu.VMEM((8, E), jnp.float32)],
        compiler_params=pltpu.CompilerParams(vmem_limit_bytes=58 * MIB),
        cost_estimate=pl.CostEstimate(flops=9 << 20, bytes_accessed=11 << 20, transcendentals=0),
        name="spread_sums",
    )(weights, own, *[control] * STEP)


def rescale_kernel(target_ref, sums_ref, own_ref, *refs):
    *control_refs, out_ref = refs
    total = jnp.sum(jnp.sum(sums_ref[...], axis=0), axis=(0, 1), keepdims=True)
    scale = target_ref[0] / jnp.sqrt(total * (1.0 / TOTAL_WEIGHT) + 1e-06)
    for j in range(STEP):
        control = control_refs[j][0].astype(jnp.float32)
        difference = own_ref[j].astype(jnp.float32) - control
        out_ref[j] = (control + scale * difference).astype(jnp.bfloat16)


def rescaled(target, sums, own, control):
    row = pl.BlockSpec((STEP, W, E), lambda j: (j, 0, 0))
    scalars = pl.BlockSpec(memory_space=pltpu.SMEM)
    return pl.pallas_call(
        rescale_kernel,
        grid=(ROWS // STEP,),
        in_specs=[
            scalars,
            pl.BlockSpec((BANDS, 8, 128), lambda j: (0, 0, 0)),
            row,
        ]
        + [control_rows(t) for t in range(STEP)],
        out_specs=row,
        out_shape=jax.ShapeDtypeStruct((ROWS, W, E), jnp.bfloat16),
        compiler_params=pltpu.CompilerParams(vmem_limit_bytes=58 * MIB),
        cost_estimate=pl.CostEstimate(flops=9 << 20, bytes_accessed=17 << 20, transcendentals=0),
        name="rescaled",
    )(target, sums, own, *[control] * STEP)


def in_three(value):
    parts = []
    for _ in range(3):
        parts.append(lax.reduce_precision(value, exponent_bits=8, mantissa_bits=7))
        value = value - parts[-1]
    return jnp.stack(parts).astype(jnp.bfloat16)


def scattered(field, extra):
    member = lax.axis_index("member")

    def piece(z):
        first = 2 * ((z + SHIFT) % DEPTH)
        rows = field[first : min(first + 2, ROWS)].reshape(-1, E)
        return jnp.concatenate([rows, extra])

    kept = piece(0)
    for z in BOTH_WAYS:
        arrived = lax.ppermute(piece(z), "member", [(0, 2 * z)])
        if arrived.shape != kept.shape:
            arrived = jnp.concatenate([arrived[:W], arrived])
        kept = jnp.where(member == 2 * z, arrived, kept)
    return kept


def exchanged_along_z(pieces):
    return lax.all_to_all(
        pieces, "member", split_axis=0, concat_axis=0, axis_index_groups=RINGS, tiled=True
    )


def permuted_along_z(pieces):
    z = lax.axis_index("member") // 2
    result = pieces
    for shift in BOTH_WAYS:
        block = lax.dynamic_index_in_dim(pieces, (z + shift) % DEPTH, 0, keepdims=False)
        pairs = [(ring[a], ring[(a + shift) % DEPTH]) for ring in RINGS for a in range(DEPTH)]
        arrived = lax.ppermute(block, "member", pairs)
        result = lax.dynamic_update_index_in_dim(result, arrived, (z - shift) % DEPTH, 0)
    return result


def across(value):
    half = BANDS // 2
    pairs = [
        (2 * z * BANDS + b, (2 * z + 1) * BANDS + (b + half) % BANDS)
        for z in range(DEPTH)
        for b in range(BANDS)
    ]
    arrived = lax.ppermute(value, ("member", "band"), pairs)
    return jnp.where(lax.axis_index("member") % 2 == 1, arrived, value)


def home_again(value):
    half = BANDS // 2
    pairs = [
        ((2 * z + 1) * BANDS + b, (2 * z + 1) * BANDS + (b + half) % BANDS)
        for z in range(DEPTH)
        for b in range(BANDS)
    ]
    arrived = lax.ppermute(value, ("member", "band"), pairs)
    return jnp.where(lax.axis_index("member") % 2 == 1, arrived, value)


def turned(value, first):
    return jnp.concatenate([value[first:], value[:first]])


def latitude_weights(rows):
    return jnp.sin((rows.astype(jnp.float32) + 0.5) * (math.pi / H)) * (math.pi / H)


def shards(
    copy_fields,
    norm_gain,
    mix_real,
    mix_imag,
    filter_bank,
    perturbation_draw_numbers,
    amplitudes,
    desired_magnitude_slot,
):
    band_index = lax.axis_index("band")
    ahead_np, back_np, shared_ahead_np, shared_back_np = slot_tables()
    legendre_np = legendre_table(L, M, H).reshape(OWN, BANDS, L, H).transpose(1, 0, 2, 3)
    x = jnp.transpose(copy_fields[0], (0, 2, 1))

    weights = latitude_weights(band_index * ROWS + jnp.arange(ROWS, dtype=jnp.int32))
    bank_rows = filter_bank.shape[0]
    draw_onehot = (jnp.arange(bank_rows, dtype=jnp.int32) == perturbation_draw_numbers[0]).astype(
        jnp.float32
    )
    degree_gain = jnp.sum(draw_onehot[:, None] * filter_bank, axis=0)

    legendre = rounded(legendre_np)
    gain = degree_gain[:, None]
    member = lax.axis_index("member")
    place = jnp.stack([band_index, member // 2])

    mixing = jnp.concatenate(
        [jnp.concatenate([mix_real, mix_imag], 1), jnp.concatenate([-mix_imag, mix_real], 1)], 0
    )
    z = member // 2
    crossed = member % 2 == 1
    control_band = jnp.where(crossed, (band_index + BANDS // 2) % BANDS, band_index)

    fourier = forward_transform(x, norm_gain[None, :], weights, rounded(ahead_np), BANDS, STEP, 1 << 37)
    moved = lax.all_to_all(fourier, "band", split_axis=0, concat_axis=0, tiled=True)

    control_parts = across(
        scattered(x, jnp.pad(in_three(degree_gain), ((0, 16 - 3), (0, E - L))))
    )
    control_x = control_parts[: 2 * W].reshape(2, W, E)
    control_gain = jnp.sum(control_parts[2 * W : 2 * W + 3, :L].astype(jnp.float32), axis=0)
    control_first = control_band * ROWS + 2 * ((z + SHIFT) % DEPTH)
    control_weights = latitude_weights(control_first + jnp.arange(2, dtype=jnp.int32))
    control_fourier = forward_transform(
        control_x, norm_gain[None, :], control_weights, rounded(shared_ahead_np), DEPTH, 2, 1 << 29
    )
    moved, control_fourier = lax.optimization_barrier((moved, control_fourier))
    control_fourier = exchanged_along_z(control_fourier).reshape(DEPTH, 2, BANDS, 4, E)
    control_fourier = turned(control_fourier, DEPTH - SHIFT)
    control_fourier = control_fourier.transpose(2, 0, 1, 3, 4).reshape(BANDS, 16, 4, E)[:, :ROWS]
    returned = spectral_pass(
        band_index[None],
        moved.reshape(H, SLOTS, E),
        legendre,
        gain,
        mixing,
        rounded(exchange_matrix()),
    )
    returned, control_fourier = lax.optimization_barrier((returned, control_fourier))
    control_moved = lax.all_to_all(control_fourier, "band", split_axis=0, concat_axis=0, tiled=True)
    control_moved = jnp.where(crossed, turned(control_moved, BANDS // 2), control_moved)
    control_x, control_moved = lax.optimization_barrier((home_again(control_x), control_moved))
    control_spatial = shared_spectral_pass(
        place,
        control_moved.reshape(H, 4, E).transpose(1, 0, 2),
        legendre,
        control_gain.reshape(L, 1),
        mixing,
    )
    control_spatial = lax.all_to_all(
        control_spatial.transpose(1, 0, 2).reshape(BANDS, ROWS, 4, E),
        "band",
        split_axis=0,
        concat_axis=0,
        tiled=True,
    )
    control_spatial, returned = lax.optimization_barrier((control_spatial, returned))
    spatial = lax.all_to_all(
        returned.reshape(BANDS, ROWS, SLOTS, E), "band", split_axis=0, concat_axis=0, tiled=True
    )
    control_spatial = jnp.pad(control_spatial, ((0, 0), (0, 1), (0, 0), (0, 0)))
    control_spatial = control_spatial.reshape(BANDS, DEPTH, 2, 4, E).transpose(1, 2, 0, 3, 4)
    control_spatial = turned(control_spatial.reshape(DEPTH, 2, BANDS * 4, E), SHIFT)
    control_spatial = permuted_along_z(control_spatial)
    control = inverse_transform(control_spatial, control_x, rounded(shared_back_np), 2, 1 << 29)
    control = lax.all_gather(control, "member", tiled=True, axis_index_groups=RINGS)

    forecast = inverse_transform(spatial, x, rounded(back_np), STEP, 1 << 38)
    sums = lax.all_to_all(
        spread_sums(weights, forecast, control),
        "band",
        split_axis=0,
        concat_axis=0,
        tiled=True,
    )
    target = jnp.sum(
        jnp.where(
            jnp.arange(amplitudes.shape[0], dtype=jnp.int32) == desired_magnitude_slot[0],
            amplitudes,
            0.0,
        )
    )
    bred = rescaled(jnp.where(member > 0, target, 0.0)[None], sums, forecast, control)
    return jnp.transpose(bred, (0, 2, 1))[None]


def solution(mesh):
    in_specs = (P("member", "band", None, None), P(), P(), P(), P(), P("member"), P(), P("member"))
    out_specs = P("member", "band", None, None)
    return jax.shard_map(shards, mesh=mesh, in_specs=in_specs, out_specs=out_specs, check_vma=False)
```

```python
import functools
import math

import jax
import jax.numpy as jnp
import numpy as np
from jax import lax
from jax.experimental import pallas as pl
from jax.experimental.pallas import tpu as pltpu
from jax.sharding import PartitionSpec as P

H = 240
W = 480
M = 240
L = 240
E = 384
BANDS = 16
ROWS = H // BANDS
OWN = M // BANDS
SLOTS = 32
DEPTH = 8
SHIFT = 3
BOTH_WAYS = (1, 7, 2, 6, 3, 5, 4)
RINGS = [[2 * z + h for z in range(DEPTH)] for h in range(2)]
STEP = 3
TOTAL_WEIGHT = float(np.sum(np.sin((np.arange(H) + 0.5) * np.pi / H)) * np.pi / H * E * W)
HALF = W // 2
MIB = 1 << 20


def legendre_table(degree_count, order_count, lat_count):
    colatitude = (np.arange(lat_count) + 0.5) * np.pi / lat_count
    cosines = np.cos(colatitude)
    sines = np.sin(colatitude)
    orders = np.arange(order_count)[:, None] * 1.0
    steps_up = np.arange(1, order_count) * 1.0
    log_factor = np.concatenate(
        [[0.0], np.cumsum(np.log((2.0 * steps_up - 1.0) / (2.0 * steps_up)))]
    )
    diagonal_start = np.exp(
        0.5 * np.log((2.0 * orders + 1.0) / 2.0)
        + 0.5 * log_factor[:, None]
        + orders * np.log(sines)[None, :]
    )
    result = np.zeros((order_count, degree_count, lat_count))
    previous = np.zeros(diagonal_start.shape)
    before_previous = np.zeros(diagonal_start.shape)
    for degree in range(degree_count):
        lower = degree - 1.0
        rising = np.sqrt(
            np.maximum(4.0 * degree * degree - 1.0, 1.0)
            / np.maximum(degree * degree - orders * orders, 1.0)
        )
        falling = np.sqrt(
            np.maximum(lower * lower - orders * orders, 0.0) / max(4.0 * lower * lower - 1.0, 1.0)
        )
        current = np.where(
            orders == degree,
            diagonal_start,
            np.where(
                degree > orders,
                rising * (cosines[None, :] * previous - falling * before_previous),
                0.0,
            ),
        )
        result[:, degree] = current
        before_previous = previous
        previous = current
    return result


def fourier_tables(lon_count, mode_order):
    longitude = 2.0 * np.pi * np.arange(lon_count)[:, None] / lon_count
    angles = longitude * (mode_order[None, :] * 1.0)
    forward_factor = math.sqrt(2.0 * math.pi) / lon_count
    forward_table = np.stack(
        [forward_factor * np.cos(angles), -forward_factor * np.sin(angles)], axis=1
    )
    inverse_factor = np.where(mode_order == 0, 1.0, 2.0) / math.sqrt(2.0 * math.pi)
    inverse_table = np.stack(
        [
            (inverse_factor[None, :] * np.cos(angles)).T,
            (-inverse_factor[None, :] * np.sin(angles)).T,
        ],
        axis=0,
    )
    return (forward_table, inverse_table)


def slot_tables():
    forward, inverse = fourier_tables(W, np.arange(M))
    ahead = np.zeros((W, 2, 16, BANDS))
    back = np.zeros((2, 16, BANDS, W))
    ahead[:, :, :OWN] = forward.reshape(W, 2, OWN, BANDS)
    back[:, :OWN] = inverse.reshape(2, OWN, BANDS, W)
    ahead = ahead.reshape(W, 2, DEPTH, 2, BANDS)
    back = back.reshape(2, DEPTH, 2, BANDS, W)
    rows = BANDS * SLOTS
    return (
        ahead.transpose(4, 2, 1, 3, 0).reshape(rows, W),
        back.transpose(3, 1, 0, 2, 4).reshape(rows, W).T,
        ahead.transpose(2, 4, 1, 3, 0).reshape(rows, W),
        back.transpose(1, 3, 0, 2, 4).reshape(rows, W).T,
    )


def rounded(table):
    return jnp.asarray(table, jnp.float32).astype(jnp.bfloat16)


def exchange_matrix():
    matrix = np.zeros((256, 256))
    for a in range(16):
        for b in range(16):
            matrix[b * 16 + a, a * 16 + b] = 1.0
    return matrix


def forward_kernel(weights_ref, x_ref, gain_ref, table_ref, out_ref):
    rows = x_ref.shape[0]
    for j in range(rows):
        x = x_ref[j].astype(jnp.float32)
        centred = x - jnp.mean(x, axis=1, keepdims=True)
        variance = jnp.mean(jnp.square(centred), axis=1, keepdims=True)
        normed = (centred * lax.rsqrt(variance + 1e-05) * gain_ref[...]).astype(jnp.bfloat16)
        sums = jnp.dot(table_ref[...], normed, preferred_element_type=jnp.float32)
        sums = (sums * weights_ref[pl.program_id(0) * rows + j]).astype(jnp.bfloat16)
        out_ref[:, j] = sums.reshape(out_ref.shape[0], out_ref.shape[2], E)


def forward_transform(x, gain, weights, table, groups, step, flops):
    rows = x.shape[0]
    size = BANDS * SLOTS // groups
    return pl.pallas_call(
        forward_kernel,
        grid=(rows // step,),
        in_specs=[
            pl.BlockSpec(memory_space=pltpu.SMEM),
            pl.BlockSpec((step, W, E), lambda j: (j, 0, 0)),
            pl.BlockSpec((1, E), lambda j: (0, 0)),
            pl.BlockSpec((BANDS * SLOTS, W), lambda j: (0, 0)),
        ],
        out_specs=pl.BlockSpec((groups, step, size, E), lambda j: (0, j, 0, 0)),
        out_shape=jax.ShapeDtypeStruct((groups, rows, size, E), jnp.bfloat16),
        compiler_params=pltpu.CompilerParams(vmem_limit_bytes=58 * MIB),
        cost_estimate=pl.CostEstimate(flops=flops, bytes_accessed=rows << 20, transcendentals=0),
        name="forward_transform",
    )(weights, x, gain, table)


def mix_degrees(table, values, gain, mixing):
    coeffs = jnp.dot(table, values, preferred_element_type=jnp.float32).astype(jnp.bfloat16)
    return (jnp.dot(coeffs, mixing, preferred_element_type=jnp.float32) * gain).astype(jnp.bfloat16)


def to_latitudes(table, mixed):
    return lax.dot_general(
        table, mixed, (((0,), (0,)), ((), ())), preferred_element_type=jnp.float32
    ).astype(jnp.bfloat16)


def shared_spectral_kernel(
    place_ref, re_ref, im_ref, legendre_ref, gain_ref, mixing_ref, out_re_ref, out_im_ref
):
    table = legendre_ref[0, 0]
    values = jnp.concatenate([re_ref[0], im_ref[0]], axis=1)
    spatial = to_latitudes(table, mix_degrees(table, values, gain_ref[...], mixing_ref[...]))
    out_re_ref[0] = spatial[:, :E]
    out_im_ref[0] = spatial[:, E:]


def shared_spectral_pass(place, moved, legendre, gain, mixing):
    row = lambda first: pl.BlockSpec((1, H, E), lambda o, place: (first + o, 0, 0))
    whole = lambda *shape: pl.BlockSpec(shape, lambda o, place: (0,) * len(shape))
    pair = jax.ShapeDtypeStruct((2, H, E), jnp.bfloat16)
    out_re, out_im = pl.pallas_call(
        shared_spectral_kernel,
        grid_spec=pltpu.PrefetchScalarGridSpec(
            num_scalar_prefetch=1,
            grid=(2,),
            in_specs=[
                row(0),
                row(2),
                pl.BlockSpec(
                    (1, 1, L, H),
                    lambda o, place: (place[0], jnp.minimum(2 * place[1] + o, OWN - 1), 0, 0),
                ),
                whole(L, 1),
                whole(2 * E, 2 * E),
            ],
            out_specs=[row(0), row(0)],
        ),
        out_shape=[pair, pair],
        compiler_params=pltpu.CompilerParams(vmem_limit_bytes=58 * MIB),
        cost_estimate=pl.CostEstimate(flops=1 << 30, bytes_accessed=4 << 20, transcendentals=0),
        name="shared_spectral_pass",
    )(place, moved, moved, legendre, gain, mixing)
    return jnp.concatenate([out_re, out_im], axis=0)


def spectral_kernel(
    band_ref, moved_ref, legendre_ref, gain_ref, mixing_ref, swap_ref, out_ref, by_mode, mixed
):
    swap = swap_ref[...]
    halves = [(half, lanes) for half, lanes in ((0, slice(0, E)), (16, slice(E, 2 * E)))]
    unroll = 3

    def place_of(slot):
        z, part, o = slot // 4, (slot // 2) % 2, slot % 2
        return 2 * z + o, slice(part * E, part * E + E)

    def to_modes(step, carry):
        for piece in range(unroll):
            rows = pl.ds(pl.multiple_of((step * unroll + piece) * 16, 16), 16)
            block = jnp.concatenate(
                [moved_ref[rows, half : half + 16, :].reshape(256, E) for half, _ in halves], axis=1
            )
            turned = jnp.dot(swap, block, preferred_element_type=jnp.float32).astype(jnp.bfloat16)
            turned = turned.reshape(16, 16, 2 * E)
            for half, lanes in halves:
                for k in range(16):
                    i, part = place_of(half + k)
                    by_mode[i, rows, part] = turned[k, :, lanes]
        return carry

    lax.fori_loop(0, H // 16 // unroll, to_modes, 0)
    mixing = mixing_ref[...]
    for i in range(OWN):
        low = 16 * i
        table = legendre_ref[0, i]
        mixed[low:, :] = mix_degrees(table[low:], by_mode[i], gain_ref[low:], mixing)
        by_mode[i] = to_latitudes(table, mixed[...])

    def to_rows(step, carry):
        for piece in range(unroll):
            rows = pl.ds(pl.multiple_of((step * unroll + piece) * 16, 16), 16)
            blocks = []
            for half, _ in halves:
                slots = []
                for k in range(16):
                    i, part = place_of(half + k)
                    slots.append(by_mode[i, rows, part])
                blocks.append(jnp.concatenate(slots, axis=0))
            block = jnp.concatenate(blocks, axis=1)
            turned = jnp.dot(swap, block, preferred_element_type=jnp.float32).astype(jnp.bfloat16)
            turned = turned.reshape(16, 16, 2 * E)
            for half, lanes in halves:
                out_ref[rows, half : half + 16, :] = turned[:, :, lanes]
        return carry

    lax.fori_loop(0, H // 16 // unroll, to_rows, 0)


def spectral_pass(band, moved, legendre, gain, mixing, swap):
    whole = lambda *shape: pl.BlockSpec(shape, lambda step, band: (0,) * len(shape))
    return pl.pallas_call(
        spectral_kernel,
        grid_spec=pltpu.PrefetchScalarGridSpec(
            num_scalar_prefetch=1,
            grid=(1,),
            in_specs=[
                whole(H, SLOTS, E),
                pl.BlockSpec((1, OWN, L, H), lambda step, band: (band[0], 0, 0, 0)),
                whole(L, 1),
                whole(2 * E, 2 * E),
                whole(256, 256),
            ],
            out_specs=whole(H, SLOTS, E),
            scratch_shapes=[
                pltpu.VMEM((16, H, 2 * E), jnp.bfloat16),
                pltpu.VMEM((L, 2 * E), jnp.bfloat16),
            ],
        ),
        out_shape=jax.ShapeDtypeStruct((H, SLOTS, E), jnp.bfloat16),
        compiler_params=pltpu.CompilerParams(vmem_limit_bytes=58 * MIB),
        cost_estimate=pl.CostEstimate(flops=8 << 30, bytes_accessed=14 << 20, transcendentals=0),
        name="spectral_pass",
    )(band, moved, legendre, gain, mixing, swap)


def inverse_kernel(spatial_ref, x_ref, table_ref, out_ref):
    for j in range(x_ref.shape[0]):
        spatial = spatial_ref[:, j].reshape(BANDS * SLOTS, E)
        sums = jnp.dot(table_ref[...], spatial, preferred_element_type=jnp.float32)
        out_ref[j] = (x_ref[j].astype(jnp.float32) + jax.nn.gelu(sums)).astype(jnp.bfloat16)


def inverse_transform(spatial, x, table, step, flops):
    rows = x.shape[0]
    groups, _, size, _ = spatial.shape
    return pl.pallas_call(
        inverse_kernel,
        grid=(rows // step,),
        in_specs=[
            pl.BlockSpec((groups, step, size, E), lambda j: (0, j, 0, 0)),
            pl.BlockSpec((step, W, E), lambda j: (j, 0, 0)),
            pl.BlockSpec((W, BANDS * SLOTS), lambda j: (0, 0)),
        ],
        out_specs=pl.BlockSpec((step, W, E), lambda j: (j, 0, 0)),
        out_shape=jax.ShapeDtypeStruct((rows, W, E), jnp.bfloat16),
        compiler_params=pltpu.CompilerParams(vmem_limit_bytes=58 * MIB),
        cost_estimate=pl.CostEstimate(
            flops=flops, bytes_accessed=rows << 20, transcendentals=rows * W * E
        ),
        name="inverse_transform",
    )(spatial, x, table)


def control_rows():
    half = lambda t: pl.BlockSpec((1, HALF, E), lambda j: ((STEP * j + t + 16 - 2 * SHIFT) % 16, 0, 0))
    return [half(t) for t in range(STEP)] * 2


def halves(control_refs):
    for part in range(2):
        for j in range(STEP):
            where = slice(part * HALF, part * HALF + HALF)
            yield j, where, control_refs[part * STEP + j][0].astype(jnp.float32)


def spread_kernel(weights_ref, own_ref, *refs):
    *control_refs, out_ref, total = refs
    step = pl.program_id(0)
    partial = 0.0
    for j, where, control in halves(control_refs):
        difference = own_ref[j, where].astype(jnp.float32) - control
        squares = jnp.sum((difference * difference).reshape(HALF // 8, 8, E), axis=0)
        partial = partial + squares * weights_ref[step * STEP + j]

    @pl.when(step == 0)
    def _():
        total[...] = partial

    @pl.when(step > 0)
    def _():
        total[...] += partial

    @pl.when(step == ROWS // STEP - 1)
    def _():
        lanes = total[:, :128] + total[:, 128:256] + total[:, 256:]
        out_ref[...] = jnp.broadcast_to(lanes[None], out_ref.shape)


def spread_sums(weights, own, near, far):
    row = pl.BlockSpec((STEP, W, E), lambda j: (j, 0, 0))
    scalars = pl.BlockSpec(memory_space=pltpu.SMEM)
    return pl.pallas_call(
        spread_kernel,
        grid=(ROWS // STEP,),
        in_specs=[scalars, row] + control_rows(),
        out_specs=pl.BlockSpec((BANDS, 8, 128), lambda j: (0, 0, 0)),
        out_shape=jax.ShapeDtypeStruct((BANDS, 8, 128), jnp.float32),
        scratch_shapes=[pltpu.VMEM((8, E), jnp.float32)],
        compiler_params=pltpu.CompilerParams(vmem_limit_bytes=58 * MIB),
        cost_estimate=pl.CostEstimate(flops=9 << 20, bytes_accessed=11 << 20, transcendentals=0),
        name="spread_sums",
    )(weights, own, *[near] * STEP, *[far] * STEP)


def rescale_kernel(target_ref, sums_ref, own_ref, *refs):
    *control_refs, out_ref = refs
    total = jnp.sum(jnp.sum(sums_ref[...], axis=0), axis=(0, 1), keepdims=True)
    scale = target_ref[0] / jnp.sqrt(total * (1.0 / TOTAL_WEIGHT) + 1e-06)
    for j, where, control in halves(control_refs):
        difference = own_ref[j, where].astype(jnp.float32) - control
        out_ref[j, where] = (control + scale * difference).astype(jnp.bfloat16)


def rescaled(target, sums, own, near, far):
    row = pl.BlockSpec((STEP, W, E), lambda j: (j, 0, 0))
    scalars = pl.BlockSpec(memory_space=pltpu.SMEM)
    return pl.pallas_call(
        rescale_kernel,
        grid=(ROWS // STEP,),
        in_specs=[
            scalars,
            pl.BlockSpec((BANDS, 8, 128), lambda j: (0, 0, 0)),
            row,
        ]
        + control_rows(),
        out_specs=row,
        out_shape=jax.ShapeDtypeStruct((ROWS, W, E), jnp.bfloat16),
        compiler_params=pltpu.CompilerParams(vmem_limit_bytes=58 * MIB),
        cost_estimate=pl.CostEstimate(flops=9 << 20, bytes_accessed=17 << 20, transcendentals=0),
        name="rescaled",
    )(target, sums, own, *[near] * STEP, *[far] * STEP)


def in_three(value):
    parts = []
    for _ in range(3):
        parts.append(lax.reduce_precision(value, exponent_bits=8, mantissa_bits=7))
        value = value - parts[-1]
    return jnp.stack(parts).astype(jnp.bfloat16)


def scattered(field, extra):
    member = lax.axis_index("member")

    def piece(z):
        first = 2 * ((z + SHIFT) % DEPTH)
        rows = field[first : min(first + 2, ROWS)].reshape(-1, E)
        return jnp.concatenate([rows, extra])

    kept = piece(0)
    for z in BOTH_WAYS:
        arrived = lax.ppermute(piece(z), "member", [(0, 2 * z)])
        if arrived.shape != kept.shape:
            arrived = jnp.concatenate([arrived[:W], arrived])
        kept = jnp.where(member == 2 * z, arrived, kept)
    return kept


def exchanged_along_z(pieces):
    return lax.all_to_all(
        pieces, "member", split_axis=0, concat_axis=0, axis_index_groups=RINGS, tiled=True
    )


def permuted_along_z(pieces):
    z = lax.axis_index("member") // 2
    result = pieces
    for shift in BOTH_WAYS:
        block = lax.dynamic_index_in_dim(pieces, (z + shift) % DEPTH, 0, keepdims=False)
        pairs = [(ring[a], ring[(a + shift) % DEPTH]) for ring in RINGS for a in range(DEPTH)]
        arrived = lax.ppermute(block, "member", pairs)
        result = lax.dynamic_update_index_in_dim(result, arrived, (z - shift) % DEPTH, 0)
    return result


def around_the_ring(piece):
    z = lax.axis_index("member") // 2
    up = [(ring[a], ring[(a + 1) % DEPTH]) for ring in RINGS for a in range(DEPTH)]
    down = [(b, a) for a, b in up]
    result = jnp.zeros((2 * DEPTH,) + piece.shape[1:], piece.dtype)
    result = lax.dynamic_update_slice_in_dim(result, piece, 2 * z, 0)
    first, second = piece[:1], piece[1:]
    for step in range(1, DEPTH):
        first = lax.ppermute(first, "member", up)
        second = lax.ppermute(second, "member", down)
        result = lax.dynamic_update_slice_in_dim(result, first, 2 * ((z - step) % DEPTH), 0)
        result = lax.dynamic_update_slice_in_dim(result, second, 2 * ((z + step) % DEPTH) + 1, 0)
    return result


def across(value):
    half = BANDS // 2
    pairs = [
        (2 * z * BANDS + b, (2 * z + 1) * BANDS + (b + half) % BANDS)
        for z in range(DEPTH)
        for b in range(BANDS)
    ]
    arrived = lax.ppermute(value, ("member", "band"), pairs)
    return jnp.where(lax.axis_index("member") % 2 == 1, arrived, value)


def home_again(value):
    half = BANDS // 2
    pairs = [
        ((2 * z + 1) * BANDS + b, (2 * z + 1) * BANDS + (b + half) % BANDS)
        for z in range(DEPTH)
        for b in range(BANDS)
    ]
    arrived = lax.ppermute(value, ("member", "band"), pairs)
    return jnp.where(lax.axis_index("member") % 2 == 1, arrived, value)


def turned(value, first):
    return jnp.concatenate([value[first:], value[:first]])


def latitude_weights(rows):
    return jnp.sin((rows.astype(jnp.float32) + 0.5) * (math.pi / H)) * (math.pi / H)


def shards(
    copy_fields,
    norm_gain,
    mix_real,
    mix_imag,
    filter_bank,
    perturbation_draw_numbers,
    amplitudes,
    desired_magnitude_slot,
):
    band_index = lax.axis_index("band")
    ahead_np, back_np, shared_ahead_np, shared_back_np = slot_tables()
    legendre_np = legendre_table(L, M, H).reshape(OWN, BANDS, L, H).transpose(1, 0, 2, 3)
    x = jnp.transpose(copy_fields[0], (0, 2, 1))

    weights = latitude_weights(band_index * ROWS + jnp.arange(ROWS, dtype=jnp.int32))
    bank_rows = filter_bank.shape[0]
    draw_onehot = (jnp.arange(bank_rows, dtype=jnp.int32) == perturbation_draw_numbers[0]).astype(
        jnp.float32
    )
    degree_gain = jnp.sum(draw_onehot[:, None] * filter_bank, axis=0)

    legendre = rounded(legendre_np)
    gain = degree_gain[:, None]
    member = lax.axis_index("member")
    place = jnp.stack([band_index, member // 2])

    mixing = jnp.concatenate(
        [jnp.concatenate([mix_real, mix_imag], 1), jnp.concatenate([-mix_imag, mix_real], 1)], 0
    )
    z = member // 2
    crossed = member % 2 == 1
    control_band = jnp.where(crossed, (band_index + BANDS // 2) % BANDS, band_index)

    fourier = forward_transform(x, norm_gain[None, :], weights, rounded(ahead_np), BANDS, STEP, 1 << 37)
    moved = lax.all_to_all(fourier, "band", split_axis=0, concat_axis=0, tiled=True)

    control_parts = across(
        scattered(x, jnp.pad(in_three(degree_gain), ((0, 16 - 3), (0, E - L))))
    )
    control_x = control_parts[: 2 * W].reshape(2, W, E)
    control_gain = jnp.sum(control_parts[2 * W : 2 * W + 3, :L].astype(jnp.float32), axis=0)
    control_first = control_band * ROWS + 2 * ((z + SHIFT) % DEPTH)
    control_weights = latitude_weights(control_first + jnp.arange(2, dtype=jnp.int32))
    control_fourier = forward_transform(
        control_x, norm_gain[None, :], control_weights, rounded(shared_ahead_np), DEPTH, 2, 1 << 29
    )
    moved, control_fourier = lax.optimization_barrier((moved, control_fourier))
    control_fourier = exchanged_along_z(control_fourier).reshape(DEPTH, 2, BANDS, 4, E)
    control_fourier = turned(control_fourier, DEPTH - SHIFT)
    control_fourier = control_fourier.transpose(2, 0, 1, 3, 4).reshape(BANDS, 16, 4, E)[:, :ROWS]
    returned = spectral_pass(
        band_index[None],
        moved.reshape(H, SLOTS, E),
        legendre,
        gain,
        mixing,
        rounded(exchange_matrix()),
    )
    returned, control_fourier = lax.optimization_barrier((returned, control_fourier))
    control_moved = lax.all_to_all(control_fourier, "band", split_axis=0, concat_axis=0, tiled=True)
    control_moved = jnp.where(crossed, turned(control_moved, BANDS // 2), control_moved)
    control_x, control_moved = lax.optimization_barrier((home_again(control_x), control_moved))
    control_spatial = shared_spectral_pass(
        place,
        control_moved.reshape(H, 4, E).transpose(1, 0, 2),
        legendre,
        control_gain.reshape(L, 1),
        mixing,
    )
    control_spatial = lax.all_to_all(
        control_spatial.transpose(1, 0, 2).reshape(BANDS, ROWS, 4, E),
        "band",
        split_axis=0,
        concat_axis=0,
        tiled=True,
    )
    control_spatial, returned = lax.optimization_barrier((control_spatial, returned))
    spatial = lax.all_to_all(
        returned.reshape(BANDS, ROWS, SLOTS, E), "band", split_axis=0, concat_axis=0, tiled=True
    )
    control_spatial = jnp.pad(control_spatial, ((0, 0), (0, 1), (0, 0), (0, 0)))
    control_spatial = control_spatial.reshape(BANDS, DEPTH, 2, 4, E).transpose(1, 2, 0, 3, 4)
    control_spatial = turned(control_spatial.reshape(DEPTH, 2, BANDS * 4, E), SHIFT)
    control_spatial = permuted_along_z(control_spatial)
    control = inverse_transform(control_spatial, control_x, rounded(shared_back_np), 2, 1 << 29)
    near = lax.all_gather(control[:, :HALF], "member", tiled=True, axis_index_groups=RINGS)
    far = around_the_ring(control[:, HALF:])
    spatial, far = lax.optimization_barrier((spatial, far))

    forecast = inverse_transform(spatial, x, rounded(back_np), STEP, 1 << 38)
    sums = lax.all_to_all(
        spread_sums(weights, forecast, near, far),
        "band",
        split_axis=0,
        concat_axis=0,
        tiled=True,
    )
    target = jnp.sum(
        jnp.where(
            jnp.arange(amplitudes.shape[0], dtype=jnp.int32) == desired_magnitude_slot[0],
            amplitudes,
            0.0,
        )
    )
    bred = rescaled(jnp.where(member > 0, target, 0.0)[None], sums, forecast, near, far)
    return jnp.transpose(bred, (0, 2, 1))[None]


def solution(mesh):
    in_specs = (P("member", "band", None, None), P(), P(), P(), P(), P("member"), P(), P("member"))
    out_specs = P("member", "band", None, None)
    return jax.shard_map(shards, mesh=mesh, in_specs=in_specs, out_specs=out_specs, check_vma=False)
```

```python
import functools
import math

import jax
import jax.numpy as jnp
import numpy as np
from jax import lax
from jax.experimental import pallas as pl
from jax.experimental.pallas import tpu as pltpu
from jax.sharding import PartitionSpec as P

H = 240
W = 480
M = 240
L = 240
E = 384
BANDS = 16
ROWS = H // BANDS
OWN = M // BANDS
SLOTS = 32
DEPTH = 8
SHIFT = 3
BOTH_WAYS = (1, 7, 2, 6, 3, 5, 4)
RINGS = [[2 * z + h for z in range(DEPTH)] for h in range(2)]
STEP = 5
TOTAL_WEIGHT = float(np.sum(np.sin((np.arange(H) + 0.5) * np.pi / H)) * np.pi / H * E * W)
MIB = 1 << 20


def legendre_table(degree_count, order_count, lat_count):
    colatitude = (np.arange(lat_count) + 0.5) * np.pi / lat_count
    cosines = np.cos(colatitude)
    sines = np.sin(colatitude)
    orders = np.arange(order_count)[:, None] * 1.0
    steps_up = np.arange(1, order_count) * 1.0
    log_factor = np.concatenate(
        [[0.0], np.cumsum(np.log((2.0 * steps_up - 1.0) / (2.0 * steps_up)))]
    )
    diagonal_start = np.exp(
        0.5 * np.log((2.0 * orders + 1.0) / 2.0)
        + 0.5 * log_factor[:, None]
        + orders * np.log(sines)[None, :]
    )
    result = np.zeros((order_count, degree_count, lat_count))
    previous = np.zeros(diagonal_start.shape)
    before_previous = np.zeros(diagonal_start.shape)
    for degree in range(degree_count):
        lower = degree - 1.0
        rising = np.sqrt(
            np.maximum(4.0 * degree * degree - 1.0, 1.0)
            / np.maximum(degree * degree - orders * orders, 1.0)
        )
        falling = np.sqrt(
            np.maximum(lower * lower - orders * orders, 0.0) / max(4.0 * lower * lower - 1.0, 1.0)
        )
        current = np.where(
            orders == degree,
            diagonal_start,
            np.where(
                degree > orders,
                rising * (cosines[None, :] * previous - falling * before_previous),
                0.0,
            ),
        )
        result[:, degree] = current
        before_previous = previous
        previous = current
    return result


def fourier_tables(lon_count, mode_order):
    longitude = 2.0 * np.pi * np.arange(lon_count)[:, None] / lon_count
    angles = longitude * (mode_order[None, :] * 1.0)
    forward_factor = math.sqrt(2.0 * math.pi) / lon_count
    forward_table = np.stack(
        [forward_factor * np.cos(angles), -forward_factor * np.sin(angles)], axis=1
    )
    inverse_factor = np.where(mode_order == 0, 1.0, 2.0) / math.sqrt(2.0 * math.pi)
    inverse_table = np.stack(
        [
            (inverse_factor[None, :] * np.cos(angles)).T,
            (-inverse_factor[None, :] * np.sin(angles)).T,
        ],
        axis=0,
    )
    return (forward_table, inverse_table)


def slot_tables():
    forward, inverse = fourier_tables(W, np.arange(M))
    ahead = np.zeros((W, 2, 16, BANDS))
    back = np.zeros((2, 16, BANDS, W))
    ahead[:, :, :OWN] = forward.reshape(W, 2, OWN, BANDS)
    back[:, :OWN] = inverse.reshape(2, OWN, BANDS, W)
    ahead = ahead.reshape(W, 2, DEPTH, 2, BANDS)
    back = back.reshape(2, DEPTH, 2, BANDS, W)
    rows = BANDS * SLOTS
    return (
        ahead.transpose(4, 2, 1, 3, 0).reshape(rows, W),
        back.transpose(3, 1, 0, 2, 4).reshape(rows, W).T,
        ahead.transpose(2, 4, 1, 3, 0).reshape(rows, W),
        back.transpose(1, 3, 0, 2, 4).reshape(rows, W).T,
    )


def rounded(table):
    return jnp.asarray(table, jnp.float32).astype(jnp.bfloat16)


def exchange_matrix():
    matrix = np.zeros((256, 256))
    for a in range(16):
        for b in range(16):
            matrix[b * 16 + a, a * 16 + b] = 1.0
    return matrix


def forward_kernel(weights_ref, x_ref, gain_ref, table_ref, out_ref):
    rows = x_ref.shape[0]
    for j in range(rows):
        x = x_ref[j].astype(jnp.float32)
        centred = x - jnp.mean(x, axis=1, keepdims=True)
        variance = jnp.mean(jnp.square(centred), axis=1, keepdims=True)
        normed = (centred * lax.rsqrt(variance + 1e-05) * gain_ref[...][None, :]).astype(jnp.bfloat16)
        sums = jnp.dot(table_ref[...], normed, preferred_element_type=jnp.float32)
        sums = (sums * weights_ref[pl.program_id(0) * rows + j]).astype(jnp.bfloat16)
        out_ref[:, j] = sums.reshape(out_ref.shape[0], out_ref.shape[2], E)


def forward_transform(x, gain, weights, table, groups, step, flops):
    rows = x.shape[0]
    size = BANDS * SLOTS // groups
    return pl.pallas_call(
        forward_kernel,
        grid=(rows // step,),
        in_specs=[
            pl.BlockSpec(memory_space=pltpu.SMEM),
            pl.BlockSpec((step, W, E), lambda j: (j, 0, 0)),
            pl.BlockSpec((E,), lambda j: (0,)),
            pl.BlockSpec((BANDS * SLOTS, W), lambda j: (0, 0)),
        ],
        out_specs=pl.BlockSpec((groups, step, size, E), lambda j: (0, j, 0, 0)),
        out_shape=jax.ShapeDtypeStruct((groups, rows, size, E), jnp.bfloat16),
        compiler_params=pltpu.CompilerParams(vmem_limit_bytes=58 * MIB),
        cost_estimate=pl.CostEstimate(flops=flops, bytes_accessed=rows << 20, transcendentals=0),
        name="forward_transform",
    )(weights, x, gain, table)


def mix_degrees(table, values, gain, mixing):
    coeffs = jnp.dot(table, values, preferred_element_type=jnp.float32).astype(jnp.bfloat16)
    return (jnp.dot(coeffs, mixing, preferred_element_type=jnp.float32) * gain).astype(jnp.bfloat16)


def to_latitudes(table, mixed):
    return lax.dot_general(
        table, mixed, (((0,), (0,)), ((), ())), preferred_element_type=jnp.float32
    ).astype(jnp.bfloat16)


def shared_spectral_kernel(
    place_ref, re_ref, im_ref, legendre_ref, gain_ref, mixing_ref, out_re_ref, out_im_ref
):
    table = legendre_ref[0, 0]
    values = jnp.concatenate([re_ref[0], im_ref[0]], axis=1)
    spatial = to_latitudes(table, mix_degrees(table, values, gain_ref[...], mixing_ref[...]))
    out_re_ref[0] = spatial[:, :E]
    out_im_ref[0] = spatial[:, E:]


def shared_spectral_pass(place, moved, legendre, gain, mixing):
    row = lambda first: pl.BlockSpec((1, H, E), lambda o, place: (first + o, 0, 0))
    whole = lambda *shape: pl.BlockSpec(shape, lambda o, place: (0,) * len(shape))
    pair = jax.ShapeDtypeStruct((2, H, E), jnp.bfloat16)
    out_re, out_im = pl.pallas_call(
        shared_spectral_kernel,
        grid_spec=pltpu.PrefetchScalarGridSpec(
            num_scalar_prefetch=1,
            grid=(2,),
            in_specs=[
                row(0),
                row(2),
                pl.BlockSpec(
                    (1, 1, L, H),
                    lambda o, place: (place[0], jnp.minimum(2 * place[1] + o, OWN - 1), 0, 0),
                ),
                whole(L, 1),
                whole(2 * E, 2 * E),
            ],
            out_specs=[row(0), row(0)],
        ),
        out_shape=[pair, pair],
        compiler_params=pltpu.CompilerParams(vmem_limit_bytes=58 * MIB),
        cost_estimate=pl.CostEstimate(flops=1 << 30, bytes_accessed=4 << 20, transcendentals=0),
        name="shared_spectral_pass",
    )(place, moved, moved, legendre, gain, mixing)
    return jnp.concatenate([out_re, out_im], axis=0)


def spectral_kernel(
    band_ref, moved_ref, legendre_ref, gain_ref, mixing_ref, swap_ref, out_ref, by_mode, mixed
):
    swap = swap_ref[...]
    halves = [(half, lanes) for half, lanes in ((0, slice(0, E)), (16, slice(E, 2 * E)))]
    unroll = 3

    def place_of(slot):
        z, part, o = slot // 4, (slot // 2) % 2, slot % 2
        return 2 * z + o, slice(part * E, part * E + E)

    def to_modes(step, carry):
        for piece in range(unroll):
            rows = pl.ds(pl.multiple_of((step * unroll + piece) * 16, 16), 16)
            block = jnp.concatenate(
                [moved_ref[rows, half : half + 16, :].reshape(256, E) for half, _ in halves], axis=1
            )
            turned = jnp.dot(swap, block, preferred_element_type=jnp.float32).astype(jnp.bfloat16)
            turned = turned.reshape(16, 16, 2 * E)
            for half, lanes in halves:
                for k in range(16):
                    i, part = place_of(half + k)
                    by_mode[i, rows, part] = turned[k, :, lanes]
        return carry

    lax.fori_loop(0, H // 16 // unroll, to_modes, 0)
    mixing = mixing_ref[...]
    for i in range(OWN):
        low = 16 * i
        table = legendre_ref[0, i]
        mixed[low:, :] = mix_degrees(table[low:], by_mode[i], gain_ref[low:], mixing)
        by_mode[i] = to_latitudes(table, mixed[...])

    def to_rows(step, carry):
        for piece in range(unroll):
            rows = pl.ds(pl.multiple_of((step * unroll + piece) * 16, 16), 16)
            blocks = []
            for half, _ in halves:
                slots = []
                for k in range(16):
                    i, part = place_of(half + k)
                    slots.append(by_mode[i, rows, part])
                blocks.append(jnp.concatenate(slots, axis=0))
            block = jnp.concatenate(blocks, axis=1)
            turned = jnp.dot(swap, block, preferred_element_type=jnp.float32).astype(jnp.bfloat16)
            turned = turned.reshape(16, 16, 2 * E)
            for half, lanes in halves:
                out_ref[rows, half : half + 16, :] = turned[:, :, lanes]
        return carry

    lax.fori_loop(0, H // 16 // unroll, to_rows, 0)


def spectral_pass(band, moved, legendre, gain, mixing, swap):
    whole = lambda *shape: pl.BlockSpec(shape, lambda step, band: (0,) * len(shape))
    return pl.pallas_call(
        spectral_kernel,
        grid_spec=pltpu.PrefetchScalarGridSpec(
            num_scalar_prefetch=1,
            grid=(1,),
            in_specs=[
                whole(H, SLOTS, E),
                pl.BlockSpec((1, OWN, L, H), lambda step, band: (band[0], 0, 0, 0)),
                whole(L, 1),
                whole(2 * E, 2 * E),
                whole(256, 256),
            ],
            out_specs=whole(H, SLOTS, E),
            scratch_shapes=[
                pltpu.VMEM((16, H, 2 * E), jnp.bfloat16),
                pltpu.VMEM((L, 2 * E), jnp.bfloat16),
            ],
        ),
        out_shape=jax.ShapeDtypeStruct((H, SLOTS, E), jnp.bfloat16),
        compiler_params=pltpu.CompilerParams(vmem_limit_bytes=58 * MIB),
        cost_estimate=pl.CostEstimate(flops=8 << 30, bytes_accessed=14 << 20, transcendentals=0),
        name="spectral_pass",
    )(band, moved, legendre, gain, mixing, swap)


def inverse_kernel(spatial_ref, x_ref, table_ref, out_ref):
    for j in range(x_ref.shape[0]):
        spatial = spatial_ref[:, j].reshape(BANDS * SLOTS, E)
        sums = jnp.dot(table_ref[...], spatial, preferred_element_type=jnp.float32)
        out_ref[j] = (x_ref[j].astype(jnp.float32) + jax.nn.gelu(sums)).astype(jnp.bfloat16)


def inverse_transform(spatial, x, table, step, flops):
    rows = x.shape[0]
    groups, _, size, _ = spatial.shape
    return pl.pallas_call(
        inverse_kernel,
        grid=(rows // step,),
        in_specs=[
            pl.BlockSpec((groups, step, size, E), lambda j: (0, j, 0, 0)),
            pl.BlockSpec((step, W, E), lambda j: (j, 0, 0)),
            pl.BlockSpec((W, BANDS * SLOTS), lambda j: (0, 0)),
        ],
        out_specs=pl.BlockSpec((step, W, E), lambda j: (j, 0, 0)),
        out_shape=jax.ShapeDtypeStruct((rows, W, E), jnp.bfloat16),
        compiler_params=pltpu.CompilerParams(vmem_limit_bytes=58 * MIB),
        cost_estimate=pl.CostEstimate(
            flops=flops, bytes_accessed=rows << 20, transcendentals=rows * W * E
        ),
        name="inverse_transform",
    )(spatial, x, table)


def control_rows(t):
    return pl.BlockSpec((1, W, E), lambda j: ((STEP * j + t + 16 - 2 * SHIFT) % 16, 0, 0))


def spread_kernel(weights_ref, own_ref, *refs):
    *control_refs, out_ref, total = refs
    step = pl.program_id(0)
    partial = 0.0
    for j in range(STEP):
        difference = own_ref[j].astype(jnp.float32) - control_refs[j][0].astype(jnp.float32)
        squares = jnp.sum((difference * difference).reshape(W // 8, 8, E), axis=0)
        partial = partial + squares * weights_ref[step * STEP + j]

    @pl.when(step == 0)
    def _():
        total[...] = partial

    @pl.when(step > 0)
    def _():
        total[...] += partial

    @pl.when(step == ROWS // STEP - 1)
    def _():
        lanes = total[:, :128] + total[:, 128:256] + total[:, 256:]
        out_ref[...] = jnp.broadcast_to(lanes[None], out_ref.shape)


def spread_sums(weights, own, control):
    row = pl.BlockSpec((STEP, W, E), lambda j: (j, 0, 0))
    scalars = pl.BlockSpec(memory_space=pltpu.SMEM)
    return pl.pallas_call(
        spread_kernel,
        grid=(ROWS // STEP,),
        in_specs=[scalars, row] + [control_rows(t) for t in range(STEP)],
        out_specs=pl.BlockSpec((BANDS, 8, 128), lambda j: (0, 0, 0)),
        out_shape=jax.ShapeDtypeStruct((BANDS, 8, 128), jnp.float32),
        scratch_shapes=[pltpu.VMEM((8, E), jnp.float32)],
        compiler_params=pltpu.CompilerParams(vmem_limit_bytes=58 * MIB),
        cost_estimate=pl.CostEstimate(flops=9 << 20, bytes_accessed=11 << 20, transcendentals=0),
        name="spread_sums",
    )(weights, own, *[control] * STEP)


def rescale_kernel(target_ref, sums_ref, own_ref, *refs):
    *control_refs, out_ref = refs
    total = jnp.sum(jnp.sum(sums_ref[...], axis=0), axis=(0, 1), keepdims=True)
    scale = target_ref[0] / jnp.sqrt(total * (1.0 / TOTAL_WEIGHT) + 1e-06)
    for j in range(STEP):
        control = control_refs[j][0].astype(jnp.float32)
        difference = own_ref[j].astype(jnp.float32) - control
        out_ref[j] = (control + scale * difference).astype(jnp.bfloat16)


def rescaled(target, sums, own, control):
    row = pl.BlockSpec((STEP, W, E), lambda j: (j, 0, 0))
    scalars = pl.BlockSpec(memory_space=pltpu.SMEM)
    return pl.pallas_call(
        rescale_kernel,
        grid=(ROWS // STEP,),
        in_specs=[
            scalars,
            pl.BlockSpec((BANDS, 8, 128), lambda j: (0, 0, 0)),
            row,
        ]
        + [control_rows(t) for t in range(STEP)],
        out_specs=row,
        out_shape=jax.ShapeDtypeStruct((ROWS, W, E), jnp.bfloat16),
        compiler_params=pltpu.CompilerParams(vmem_limit_bytes=58 * MIB),
        cost_estimate=pl.CostEstimate(flops=9 << 20, bytes_accessed=17 << 20, transcendentals=0),
        name="rescaled",
    )(target, sums, own, *[control] * STEP)


def in_three(value):
    parts = []
    for _ in range(3):
        parts.append(lax.reduce_precision(value, exponent_bits=8, mantissa_bits=7))
        value = value - parts[-1]
    return jnp.stack(parts).astype(jnp.bfloat16)


def scattered(field, extra):
    member = lax.axis_index("member")

    def piece(z):
        first = 2 * ((z + SHIFT) % DEPTH)
        rows = field[first : min(first + 2, ROWS)].reshape(-1, E)
        return jnp.concatenate([rows, extra])

    kept = piece(0)
    for z in BOTH_WAYS:
        arrived = lax.ppermute(piece(z), "member", [(0, 2 * z)])
        if arrived.shape != kept.shape:
            arrived = jnp.concatenate([arrived[:W], arrived])
        kept = jnp.where(member == 2 * z, arrived, kept)
    return kept


def exchanged_along_z(pieces):
    return lax.all_to_all(
        pieces, "member", split_axis=0, concat_axis=0, axis_index_groups=RINGS, tiled=True
    )


def permuted_along_z(pieces):
    z = lax.axis_index("member") // 2
    result = pieces
    for shift in BOTH_WAYS:
        block = lax.dynamic_index_in_dim(pieces, (z + shift) % DEPTH, 0, keepdims=False)
        pairs = [(ring[a], ring[(a + shift) % DEPTH]) for ring in RINGS for a in range(DEPTH)]
        arrived = lax.ppermute(block, "member", pairs)
        result = lax.dynamic_update_index_in_dim(result, arrived, (z - shift) % DEPTH, 0)
    return result


def across(value):
    half = BANDS // 2
    pairs = [
        (2 * z * BANDS + b, (2 * z + 1) * BANDS + (b + half) % BANDS)
        for z in range(DEPTH)
        for b in range(BANDS)
    ]
    arrived = lax.ppermute(value, ("member", "band"), pairs)
    return jnp.where(lax.axis_index("member") % 2 == 1, arrived, value)


def home_again(value):
    half = BANDS // 2
    pairs = [
        ((2 * z + 1) * BANDS + b, (2 * z + 1) * BANDS + (b + half) % BANDS)
        for z in range(DEPTH)
        for b in range(BANDS)
    ]
    arrived = lax.ppermute(value, ("member", "band"), pairs)
    return jnp.where(lax.axis_index("member") % 2 == 1, arrived, value)


def turned(value, first):
    return jnp.concatenate([value[first:], value[:first]])


def latitude_weights(rows):
    return jnp.sin((rows.astype(jnp.float32) + 0.5) * (math.pi / H)) * (math.pi / H)


def shards(
    copy_fields,
    norm_gain,
    mix_real,
    mix_imag,
    filter_bank,
    perturbation_draw_numbers,
    amplitudes,
    desired_magnitude_slot,
):
    band_index = lax.axis_index("band")
    ahead_np, back_np, shared_ahead_np, shared_back_np = slot_tables()
    legendre_np = legendre_table(L, M, H).reshape(OWN, BANDS, L, H).transpose(1, 0, 2, 3)
    x = jnp.transpose(copy_fields[0], (0, 2, 1))

    weights = latitude_weights(band_index * ROWS + jnp.arange(ROWS, dtype=jnp.int32))
    bank_rows = filter_bank.shape[0]
    draw_onehot = (jnp.arange(bank_rows, dtype=jnp.int32) == perturbation_draw_numbers[0]).astype(
        jnp.float32
    )
    degree_gain = jnp.sum(draw_onehot[:, None] * filter_bank, axis=0)

    legendre = rounded(legendre_np)
    gain = degree_gain[:, None]
    member = lax.axis_index("member")
    place = jnp.stack([band_index, member // 2])

    mixing = jnp.concatenate(
        [jnp.concatenate([mix_real, mix_imag], 1), jnp.concatenate([-mix_imag, mix_real], 1)], 0
    )
    z = member // 2
    crossed = member % 2 == 1
    control_band = jnp.where(crossed, (band_index + BANDS // 2) % BANDS, band_index)

    fourier = forward_transform(x, norm_gain, weights, rounded(ahead_np), BANDS, STEP, 1 << 37)
    moved = lax.all_to_all(fourier, "band", split_axis=0, concat_axis=0, tiled=True)

    control_parts = across(
        scattered(x, jnp.pad(in_three(degree_gain), ((0, 16 - 3), (0, E - L))))
    )
    control_x = control_parts[: 2 * W].reshape(2, W, E)
    control_gain = jnp.sum(control_parts[2 * W : 2 * W + 3, :L].astype(jnp.float32), axis=0)
    control_first = control_band * ROWS + 2 * ((z + SHIFT) % DEPTH)
    control_weights = latitude_weights(control_first + jnp.arange(2, dtype=jnp.int32))
    control_fourier = forward_transform(
        control_x, norm_gain, control_weights, rounded(shared_ahead_np), DEPTH, 2, 1 << 29
    )
    moved, control_fourier = lax.optimization_barrier((moved, control_fourier))
    control_fourier = exchanged_along_z(control_fourier).reshape(DEPTH, 2, BANDS, 4, E)
    control_fourier = turned(control_fourier, DEPTH - SHIFT)
    control_fourier = control_fourier.transpose(2, 0, 1, 3, 4).reshape(BANDS, 16, 4, E)[:, :ROWS]
    returned = spectral_pass(
        band_index[None],
        moved.reshape(H, SLOTS, E),
        legendre,
        gain,
        mixing,
        rounded(exchange_matrix()),
    )
    returned, control_fourier = lax.optimization_barrier((returned, control_fourier))
    control_moved = lax.all_to_all(control_fourier, "band", split_axis=0, concat_axis=0, tiled=True)
    control_moved = jnp.where(crossed, turned(control_moved, BANDS // 2), control_moved)
    control_x, control_moved = lax.optimization_barrier((home_again(control_x), control_moved))
    control_spatial = shared_spectral_pass(
        place,
        control_moved.reshape(H, 4, E).transpose(1, 0, 2),
        legendre,
        control_gain.reshape(L, 1),
        mixing,
    )
    control_spatial = lax.all_to_all(
        control_spatial.transpose(1, 0, 2).reshape(BANDS, ROWS, 4, E),
        "band",
        split_axis=0,
        concat_axis=0,
        tiled=True,
    )
    control_spatial, returned = lax.optimization_barrier((control_spatial, returned))
    spatial = lax.all_to_all(
        returned.reshape(BANDS, ROWS, SLOTS, E), "band", split_axis=0, concat_axis=0, tiled=True
    )
    control_spatial = jnp.pad(control_spatial, ((0, 0), (0, 1), (0, 0), (0, 0)))
    control_spatial = control_spatial.reshape(BANDS, DEPTH, 2, 4, E).transpose(1, 2, 0, 3, 4)
    control_spatial = turned(control_spatial.reshape(DEPTH, 2, BANDS * 4, E), SHIFT)
    control_spatial = permuted_along_z(control_spatial)
    control = inverse_transform(control_spatial, control_x, rounded(shared_back_np), 2, 1 << 29)
    control = lax.all_gather(control, "member", tiled=True, axis_index_groups=RINGS)

    forecast = inverse_transform(spatial, x, rounded(back_np), STEP, 1 << 38)
    sums = lax.all_to_all(
        spread_sums(weights, forecast, control),
        "band",
        split_axis=0,
        concat_axis=0,
        tiled=True,
    )
    target = jnp.sum(
        jnp.where(
            jnp.arange(amplitudes.shape[0], dtype=jnp.int32) == desired_magnitude_slot[0],
            amplitudes,
            0.0,
        )
    )
    bred = rescaled(jnp.where(member > 0, target, 0.0)[None], sums, forecast, control)
    return jnp.transpose(bred, (0, 2, 1))[None]


def solution(mesh):
    in_specs = (P("member", "band", None, None), P(), P(), P(), P(), P("member"), P(), P("member"))
    out_specs = P("member", "band", None, None)
    return jax.shard_map(shards, mesh=mesh, in_specs=in_specs, out_specs=out_specs, check_vma=False)
```
